32 devices in a mesh: section: 2 (over y), dp: 16 (over z, x, core).
Axes of the slice: x: 2, y: 2, z: 4, core: 2. Of those that a mesh axis runs over, the one named last changes fastest.
Arguments:
- frames: bfloat16 [2, 32, 42, 64, 192], P('section', 'dp'), may hold values from -4 to 4
- action_ids: int32 [2, 32, 42], P('section', 'dp'), may hold values from 0 to 16
- delta_ids: int32 [2, 32, 42, 4], P('section', 'dp'), may hold values from 0 to 1023
- seq_len: int32 [2, 32], P(None, 'dp'), may hold values from 8 to 21, as said below
- enc_w1: bfloat16 [48, 128], replicated, may hold values from -0.875 to 0.875
- enc_w2: bfloat16 [512, 512], replicated, may hold values from -0.25 to 0.25
- codebook: bfloat16 [1024, 512], replicated, may hold values from -6 to 6
- action_table: bfloat16 [17, 512], replicated, may hold values from -6 to 6
- ln_gain: float32 [2, 512, 2], replicated, may hold values from 0.25 to 1.75
- ln_bias: float32 [2, 512, 2], replicated, may hold values from -2 to 2
- w_qkv: bfloat16 [2, 512, 1536], replicated, may hold values from -0.25 to 0.25
- w_out: bfloat16 [2, 512, 512], replicated, may hold values from -1 to 1
- w_up: bfloat16 [2, 512, 2048], replicated, may hold values from -0.25 to 0.25
- w_down: bfloat16 [2, 2048, 512], replicated, may hold values from -0.125 to 0.125
- cotangent: bfloat16 [2, 32, 252, 512], P('section', 'dp'), may hold values from -6 to 6
Outputs:
- activations: bfloat16 [2, 32, 252, 512], P('section', 'dp')
- embed_grad: bfloat16 [2, 32, 252, 512], P('section', 'dp')
- grad_qkv: float32 [2, 2, 512, 1536], P('section', None, 'dp')
- grad_out: float32 [2, 2, 512, 512], P('section', None, 'dp')
- grad_up: float32 [2, 2, 512, 2048], P('section', None, 'dp')
- grad_down: float32 [2, 2, 2048, 512], P('section', None, 'dp')
- grad_gain: float32 [2, 2, 512, 2], P('section', None, 'dp')
- grad_bias: float32 [2, 2, 512], P('section', None, 'dp')
- grad_bias_two: float32 [2, 2, 512], P('section', None, 'dp')
- grad_enc1: float32 [2, 48, 128], P('section', None, 'dp')
- grad_enc2: float32 [2, 512, 512], P('section', None, 'dp')
- grad_codebook: float32 [2, 1024, 512], P('section', None, 'dp')
- grad_actions: float32 [2, 17, 512], P('section', None, 'dp')
The draws below stay inside these ranges and needn't reach their ends.
Inputs may be any that keep to these rules, and one draw needn't show every extreme that they name: `seq_len`: each entry is 8 or 21; the 42 steps of a micro-batch form sequences of that many steps one after the other, the last one shorter where it does not divide 42; both values occur in every draw.
All inputs are finite; a program needn't handle non-finite values.
Results may differ from the reference program's by a relative error of at most 0.019.
Values may be sent and summed in bfloat16 or wider, within the bound.
A program may use at most 256 MiB of HBM per device.

```python
import jax
import jax.numpy as jnp
from jax import lax

D = 512
HEADS = 8
HEAD_DIM = 64
FF = 2048
CODES = 1024
ACTIONS = 17
ENC_CH = 128
FRAME = 64
TPS = 6
LAYERS = 2
MB = 2
STEPS_MB = 42
ROWS_MB = 252
SLOTS = 32
N_DP = 16


def draw_seq_len(key, part):
    key = jax.random.fold_in(key, 11)
    total = 2 * SLOTS
    picks = jax.random.randint(key, (total,), 0, 2, dtype=jnp.int32)
    order = jax.random.permutation(jax.random.fold_in(key, 1), total)
    picks = picks.at[order[0]].set(1).at[order[1]].set(0)
    return (8 + 13 * picks).reshape(2, SLOTS).astype(jnp.int32)


def plant(entries, key, smallest, high):
    extent = entries.shape
    index_at = [jax.random.randint(jax.random.fold_in(key, axis), (), 0, extent[axis]) for axis in range(len(extent))]
    entries = entries.at[tuple(index_at)].set(smallest)
    longest = extent.index(max(extent))
    index_at[longest] = (index_at[longest] + 1) % extent[longest]
    return entries.at[tuple(index_at)].set(high)


def block_scale(own_key, extent, split, low, high):
    level = 1.0
    for axis_at, shards_of in split:
        draws = jax.random.uniform(jax.random.fold_in(jax.random.fold_in(own_key, 6), axis_at), (shards_of,), jnp.float32, low / len(split), high / len(split))
        level = level * jnp.repeat(jnp.exp(draws), extent[axis_at] // shards_of).reshape((-1,) + (1,) * (len(extent) - 1 - axis_at))
    return level


def bell_draw(own_key, extent, deviation, bound, shards=(), kind=jnp.bfloat16):
    loudness = block_scale(own_key, extent, shards, -0.22, 0.18) if shards else 1.0
    values = jax.random.normal(own_key, extent, jnp.float32) * deviation * loudness
    return jnp.minimum(jnp.maximum(values, -bound), bound).astype(kind)


def setup_inputs(seed: int = 0) -> dict:
    arg_keys = jax.random.split(jax.random.key(seed), 16)
    return {
        "frames": bell_draw(arg_keys[0], (2, SLOTS, STEPS_MB, FRAME, 3 * FRAME), 1.0, 4.0, ((0, 2), (1, 16))),
        "action_ids": plant(jax.random.randint(arg_keys[1], (2, SLOTS, STEPS_MB), 0, ACTIONS), jax.random.fold_in(arg_keys[1], 1), 0, ACTIONS - 1).astype(jnp.int32),
        "delta_ids": plant(jax.random.randint(arg_keys[2], (2, SLOTS, STEPS_MB, TPS - 2), 0, CODES), jax.random.fold_in(arg_keys[2], 1), 0, CODES - 1).astype(jnp.int32),
        "seq_len": draw_seq_len(jax.random.fold_in(arg_keys[15], 71), 0),
        "enc_w1": bell_draw(arg_keys[4], (48, ENC_CH), 48 ** -0.5, 0.875),
        "enc_w2": bell_draw(arg_keys[5], (4 * ENC_CH, D), (4 * ENC_CH) ** -0.5, 0.25),
        "codebook": bell_draw(arg_keys[6], (CODES, D), 1.0, 6.0),
        "action_table": bell_draw(arg_keys[7], (ACTIONS, D), 1.0, 6.0),
        "ln_gain": jnp.clip(1.0 + 0.15 * jax.random.normal(arg_keys[8], (LAYERS, D, 2), jnp.float32), 0.25, 1.75),
        "ln_bias": bell_draw(arg_keys[9], (LAYERS, D, 2), 0.3, 2.0, (), jnp.float32),
        "w_qkv": bell_draw(arg_keys[10], (LAYERS, D, 3 * D), D ** -0.5, 0.25),
        "w_out": bell_draw(arg_keys[11], (LAYERS, D, D), (D // 16) ** -0.5, 1.0),
        "w_up": bell_draw(arg_keys[12], (LAYERS, D, FF), D ** -0.5, 0.25),
        "w_down": bell_draw(arg_keys[13], (LAYERS, FF, D), FF ** -0.5, 0.125),
        "cotangent": bell_draw(arg_keys[14], (2, SLOTS, ROWS_MB, D), 1.0, 6.0, ((0, 2), (1, 16))),
    }


HIGHEST = lax.Precision.HIGHEST
EPS = 1e-05

@jax.custom_vjp
def low(v):
    return lax.optimization_barrier(v.astype(jnp.bfloat16)).astype(jnp.float32)

@jax.custom_vjp
def low_back(v):
    return v

def low_keep(v):
    return (low(v), None)

def low_pass(kept, grad):
    return (grad,)

def back_keep(v):
    return (v, None)

def back_low(kept, grad):
    return (low(grad),)
low.defvjp(low_keep, low_pass)
low_back.defvjp(back_keep, back_low)

def dot_high(operand, partner):
    return jnp.dot(operand, partner, precision=HIGHEST, preferred_element_type=jnp.float32)

def layer_norm(stream, gain, shift):
    row_mean = lax.optimization_barrier(jnp.mean(stream, axis=-1, keepdims=True))
    center = stream - row_mean
    spread = lax.optimization_barrier(jnp.mean(center * center, axis=-1, keepdims=True))
    return center * lax.rsqrt(spread + EPS) * gain + shift

def encode(frame_rows, actions, deltas, encoder):
    first_w, second_w, code_table, act_table = encoder
    micro_count, step_count = (frame_rows.shape[0], frame_rows.shape[1])
    frame_count = micro_count * step_count
    patch_grid = FRAME // 4
    pool_grid = FRAME // 8
    patches = frame_rows.reshape(frame_count, patch_grid, 4, patch_grid, 12).transpose(0, 1, 3, 2, 4).reshape(-1, 48)
    first_conv = low_back(dot_high(patches, first_w))
    hidden = low(jax.nn.gelu(first_conv, approximate=False))
    blocks = hidden.reshape(frame_count, pool_grid, 2, pool_grid, 2, ENC_CH).transpose(0, 1, 3, 2, 4, 5).reshape(-1, 4 * ENC_CH)
    second = low_back(dot_high(blocks, second_w))
    pooled = lax.optimization_barrier(jnp.mean(jax.nn.gelu(second, approximate=False).reshape(frame_count, pool_grid * pool_grid, D), axis=1))
    action_rows = act_table[actions.reshape(-1)]
    code_rows = code_table[deltas.reshape(-1)].reshape(frame_count, TPS - 2, D)
    tokens = jnp.concatenate([pooled[:, None], action_rows[:, None], code_rows], axis=1)
    return low(low_back(tokens)).reshape(micro_count, step_count * TPS, D)

def transform(tokens, lengths, weights):
    gains, shifts, qkv_w, out_w, up_w, down_w = weights
    micro_count, row_count, model_width = tokens.shape
    step_of_row = jnp.arange(row_count, dtype=jnp.int32) // TPS
    sequence = step_of_row[None, :] // lengths[:, None]
    allowed = (step_of_row[None, None, :] <= step_of_row[None, :, None]) & (sequence[:, :, None] == sequence[:, None, :])
    stream = tokens.reshape(micro_count * row_count, model_width)
    for depth in range(qkv_w.shape[0]):
        normed = low(layer_norm(stream, gains[depth, :, 0], shifts[depth, :, 0]))
        packed = low(low_back(dot_high(normed, qkv_w[depth]))).reshape(micro_count, row_count, 3, HEADS, HEAD_DIM)
        scores = low_back(jnp.einsum('bqhd,bkhd->bhqk', packed[:, :, 0], packed[:, :, 1], precision=HIGHEST) * HEAD_DIM ** (-0.5))
        soft_weights = low(jax.nn.softmax(jnp.where(allowed[:, None], scores, -jnp.inf), axis=-1))
        attended = low(low_back(jnp.einsum('bhqk,bkhd->bqhd', soft_weights, packed[:, :, 2], precision=HIGHEST)))
        stream = stream + low_back(dot_high(attended.reshape(-1, model_width), out_w[depth]))
        normed_two = low(layer_norm(stream, gains[depth, :, 1], shifts[depth, :, 1]))
        gated_rows = low(jax.nn.gelu(low_back(dot_high(normed_two, up_w[depth])), approximate=False))
        stream = stream + low_back(dot_high(gated_rows, down_w[depth]))
    return stream.reshape(micro_count, row_count, model_width)

def one_group(encoder, layers, items):
    frame_rows, actions, deltas, lengths, zeros = items
    embedded = []
    for owner in range(2):
        owned = tuple((weight[owner] for weight in encoder))
        embedded.append(encode(frame_rows[owner].astype(jnp.float32), actions[owner], deltas[owner], owned) + zeros[owner])
    results = []
    for owner in range(2):
        owned = tuple((weight[owner] for weight in layers))
        results.append(transform(embedded[1 - owner], lengths[1 - owner], owned))
    return jnp.stack(results)

def regroup(array):
    shaped = array.reshape((2, N_DP, MB) + array.shape[2:])
    return jnp.swapaxes(shaped, 0, 1)

def ungroup(array):
    shaped = jnp.swapaxes(array, 0, 1)
    return shaped.reshape((2, N_DP * MB) + shaped.shape[3:])

def reference(frames, action_ids, delta_ids, seq_len, enc_w1, enc_w2, codebook, action_table, ln_gain, ln_bias, w_qkv, w_out, w_up, w_down, cotangent):

    def twice(array):
        wide = array.astype(jnp.float32)
        return jnp.stack([wide, wide])
    encoder = tuple((twice(weight) for weight in (enc_w1, enc_w2, codebook, action_table)))
    layers = tuple((twice(weight) for weight in (ln_gain, ln_bias, w_qkv, w_out, w_up, w_down)))
    inputs = (regroup(frames), regroup(action_ids), regroup(delta_ids), regroup(seq_len))
    zeros = jnp.zeros((N_DP, 2, MB, STEPS_MB * TPS, D), jnp.float32)

    def forward(encoder, layers, zeros):

        def group(items):
            return jax.checkpoint(one_group)(encoder, layers, items)
        return lax.map(group, inputs + (zeros,))
    outputs, backward = jax.vjp(forward, encoder, layers, zeros)
    grad_encoder, grad_layers, grad_zeros = backward(regroup(cotangent.astype(jnp.float32)))
    activations = ungroup(outputs).astype(jnp.bfloat16)
    embed_grad = ungroup(grad_zeros).astype(jnp.bfloat16)
    shift_grads = grad_layers[1]
    return (activations, embed_grad, grad_layers[2], grad_layers[3], grad_layers[4], grad_layers[5], grad_layers[0], shift_grads[..., 0], shift_grads[..., 1], grad_encoder[0], grad_encoder[1], grad_encoder[2], grad_encoder[3])
```

```python
import functools

import jax
import jax.numpy as jnp
from jax import lax
from jax.experimental import pallas as pl
from jax.experimental.pallas import tpu as pltpu
from jax.sharding import PartitionSpec as P

HEADS = 8
HEAD_DIM = 64
TPS = 6
EPS = 1e-05
BF = jnp.bfloat16
F32 = jnp.float32
I32 = jnp.int32

WIDTH = 512
CODES = 1024
FRAMES_BLOCK = 28
BLOCK_ROWS = FRAMES_BLOCK * 8
TABLE = 1152
POOL_AT = 1056
ACT_AT = 1024
LAYER_COLS = 6144
ENC_COLS = 1664
VMEM_LIMIT = 60 << 20


def dot(a, b):
    return jnp.dot(a, b, preferred_element_type=F32)


def dot_rows(a, b):
    return lax.dot_general(a, b, (((0,), (0,)), ((), ())), preferred_element_type=F32)


def dot_lanes(a, b):
    return lax.dot_general(a, b, (((1,), (1,)), ((), ())), preferred_element_type=F32)


def iota(shape, axis):
    return lax.broadcasted_iota(I32, shape, axis)


def gelu_pair(v):
    e = jnp.exp2(v * v * (-0.5 * 1.4426950408889634))
    t = 1.0 / (1.0 + 0.23164190 * jnp.abs(v))
    poly = 0.5 * 1.061405429
    poly = poly * t + 0.5 * -1.453152027
    poly = poly * t + 0.5 * 1.421413741
    poly = poly * t + 0.5 * -0.284496736
    poly = poly * t + 0.5 * 0.254829592
    tail = poly * t * e
    cdf = jnp.where(v >= 0, 1.0 - tail, tail)
    return v * cdf, cdf + v * e * 0.3989422804014327


def patch_index(rows):
    k = iota((rows, 48), 0)
    dy = (k * 2731) >> 16
    rest = k - dy * 24
    j = jnp.where(rest >= 12, rest - 12, rest)
    return jnp.where((iota((rows, 48), 1) == dy * 12 + j) & (k < 96), 1.0, 0.0), rest


def encoder_weights(w1):
    hot, rest = patch_index(128)
    wide = dot(hot.astype(BF), w1)
    first = jnp.where(rest[:, :1] < 12, wide, 0.0)
    second = jnp.where(rest[:, :1] >= 12, wide, 0.0)
    block = jnp.concatenate([first, second], axis=1)
    zero = jnp.zeros_like(block)
    return jnp.concatenate(
        [jnp.concatenate([block, zero], axis=1), jnp.concatenate([zero, block], axis=1)], axis=0
    ).astype(BF)


def enc_fwd_kernel(
    frames, w1, w2, book, acts, ids, tok, xl, blocks, g1, g2, perm, lanes, big, xs, acc, table
):
    step = pl.program_id(0)

    @pl.when(step == 0)
    def _():
        a, b = iota((256, 256), 0), iota((256, 256), 1)
        perm[...] = jnp.where(b == 8 * (a & 31) + (a >> 5), 1.0, 0.0).astype(BF)
        src = iota((192, 1024), 0)
        px = (src * 5462) >> 16
        at = (px >> 1) * 128 + (px & 1) * 12 + (src - px * 12)
        out = iota((192, 1024), 1)
        for dy in range(4):
            lanes[dy] = jnp.where(out == at + dy * 24, 1.0, 0.0).astype(BF)
        big[...] = encoder_weights(w1[...])
        table[pl.ds(0, CODES), :] = book[...]
        named = acts[...].astype(F32)
        pad = jnp.zeros((TABLE - ACT_AT - named.shape[0], WIDTH), F32)
        table[pl.ds(ACT_AT, TABLE - ACT_AT), :] = jnp.concatenate([named, pad], axis=0).astype(BF)

    for group in range(FRAMES_BLOCK // 4):
        rows = frames[pl.ds(group * 4, 4)].reshape(256, 192)
        moved = dot(perm[...], rows).astype(BF).reshape(8, 32, 192)
        xs[:, pl.ds(group * 32, 32), :] = moved
    for dy2 in range(2):
        spread = dot(xs[dy2 * 4], lanes[0])
        for dy in range(1, 4):
            spread += dot(xs[dy2 * 4 + dy], lanes[dy])
        spread = spread.astype(BF)
        for bx in range(8):
            xl[0, pl.ds(bx * BLOCK_ROWS, BLOCK_ROWS), pl.ds(dy2 * 128, 128)] = spread[
                :, bx * 128 : (bx + 1) * 128
            ]
    acc[...] = jnp.zeros_like(acc)

    def part(bx, _):
        rows = pl.ds(pl.multiple_of(bx * BLOCK_ROWS, BLOCK_ROWS), BLOCK_ROWS)
        value, slope = gelu_pair(dot(xl[0, rows, :], big[...]))
        value = value.astype(BF)
        blocks[0, rows, :] = value
        g1[0, rows, :] = slope.astype(BF)
        value, slope = gelu_pair(dot(value, w2[...]))
        g2[0, rows, :] = slope.astype(BF)
        acc[...] += value
        return 0

    lax.fori_loop(0, 8, part, 0)
    pooled = jnp.sum(acc[...].reshape(FRAMES_BLOCK, 8, WIDTH), axis=1) * (1.0 / 64.0)
    pooled = jnp.concatenate([pooled, jnp.zeros((32 - FRAMES_BLOCK, WIDTH), F32)], axis=0)
    table[pl.ds(pl.multiple_of(POOL_AT + step * 32, 32), 32), :] = pooled.astype(BF)

    @pl.when(step == pl.num_programs(0) - 1)
    def _():
        for part_at in range(2):
            rows = pl.ds(part_at * 256, 256)
            hot = jnp.where(iota((256, TABLE), 1) == ids[rows, :], 1.0, 0.0).astype(BF)
            tok[rows, :] = dot(hot, table[...]).astype(BF)


def enc_forward(frames, w1, w2, book, acts, ids):
    count = frames.shape[0]
    grid = count // FRAMES_BLOCK
    rows = 8 * BLOCK_ROWS

    def whole(shape):
        return pl.BlockSpec(shape, lambda i: (0,) * len(shape))

    def saved(lanes):
        return pl.BlockSpec((1, rows, lanes), lambda i: (i, 0, 0))

    return pl.pallas_call(
        enc_fwd_kernel,
        grid=(grid,),
        in_specs=[
            pl.BlockSpec((FRAMES_BLOCK, 64, 192), lambda i: (i, 0, 0)),
            whole(w1.shape),
            whole(w2.shape),
            whole(book.shape),
            whole(acts.shape),
            whole(ids.shape),
        ],
        out_specs=[whole((512, WIDTH)), saved(256), saved(512), saved(512), saved(512)],
        out_shape=[
            jax.ShapeDtypeStruct((512, WIDTH), BF),
            jax.ShapeDtypeStruct((grid, rows, 256), BF),
            jax.ShapeDtypeStruct((grid, rows, 512), BF),
            jax.ShapeDtypeStruct((grid, rows, 512), BF),
            jax.ShapeDtypeStruct((grid, rows, 512), BF),
        ],
        scratch_shapes=[
            pltpu.VMEM((256, 256), BF),
            pltpu.VMEM((4, 192, 1024), BF),
            pltpu.VMEM((256, 512), BF),
            pltpu.VMEM((8, BLOCK_ROWS, 192), BF),
            pltpu.VMEM((BLOCK_ROWS, WIDTH), F32),
            pltpu.VMEM((TABLE, WIDTH), BF),
        ],
        compiler_params=pltpu.CompilerParams(vmem_limit_bytes=VMEM_LIMIT),
        name="enc_fwd",
    )(frames, w1, w2, book, acts, ids)


def ln_parts(x):
    mean = jnp.mean(x, axis=-1, keepdims=True)
    center = x - mean
    var = jnp.mean(center * center, axis=-1, keepdims=True)
    scale = lax.rsqrt(var + EPS)
    return center * scale, scale


def ln_back(x, d, gain):
    hat, scale = ln_parts(x)
    dh = d * gain
    one = jnp.mean(dh, axis=-1, keepdims=True)
    two = jnp.mean(dh * hat, axis=-1, keepdims=True)
    back = scale * (dh - one - hat * two)
    return back, jnp.sum(d * hat, axis=0, keepdims=True), jnp.sum(d, axis=0, keepdims=True)


def head_mask(h):
    lane = iota((1, 256), 1) >> 6
    return lane == h


def stacked(rows, scale):
    out = []
    for h in range(4):
        mask = jnp.where(head_mask(h), scale, 0.0).astype(BF)
        out.append(rows * mask)
    return jnp.concatenate(out, axis=0)


def unstacked(rows):
    out = rows[768:]
    for h in range(3):
        out = jnp.where(head_mask(h), rows[h * 256 : (h + 1) * 256], out)
    return out


def scatter_rows(g, d, cols, value, dests=16):
    shaped = value.astype(BF).reshape(dests // 2, 2, 32, value.shape[1])
    for core in range(2):
        g[d, core, :, :, cols] = shaped[:, core]


def layers_kernel(
    tok, cot, lens, lnp, wq_h, wo_h, wu_h, wd_h,
    act, eg, g, gl,
    wq, wo, wu, wd, stream, normed, packed, probs, att, normed2, gated, slope, bias,
    up, back_up, back_att, back_packed, lng, sems,
):
    layers = wq.shape[0]
    section = lax.axis_index("section")
    copies = []
    for d in range(layers):
        for k, (src, dst) in enumerate(((wq_h, wq), (wo_h, wo), (wu_h, wu), (wd_h, wd))):
            copy = pltpu.make_async_copy(src.at[d], dst.at[d], sems.at[d, k])
            copy.start()
            copies.append(copy)

    stream[0, 0] = tok[...].astype(F32)
    row = iota((256, 1), 0)
    col = iota((1, 256), 1)
    q_step = ((row * 10923) >> 16).astype(F32)
    k_step = ((col * 10923) >> 16).astype(F32)
    for s in range(2):
        inv = 1.0 / lens[section, s].astype(F32)
        q_seq = jnp.floor((q_step + 0.5) * inv)
        k_seq = jnp.floor((k_step + 0.5) * inv)
        bias[s] = jnp.where((k_step <= q_step) & (q_seq == k_seq), 0.0, -1e30)
    for copy in copies:
        copy.wait()

    def forward(d, _):
        x = stream[d, 0]
        hat, _ = ln_parts(x)
        normed[d] = (hat * lnp[d, 0:1] + lnp[d, 2:3]).astype(BF)
        for c in range(3):
            cols = pl.ds(c * 512, 512)
            packed[d, :, cols] = dot(normed[d], wq[d, :, cols]).astype(BF)
        for s in range(2):
            rows = pl.ds(s * 256, 256)
            for quad in range(2):
                q = stacked(packed[d, rows, pl.ds(quad * 256, 256)], HEAD_DIM**-0.5)
                k = packed[d, rows, pl.ds(512 + quad * 256, 256)]
                v = packed[d, rows, pl.ds(1024 + quad * 256, 256)]
                scores = dot_lanes(q, k).reshape(4, 256, 256) + bias[s][None]
                top = jnp.max(scores, axis=-1, keepdims=True)
                e = jnp.exp(scores - top)
                total = jnp.sum(e, axis=-1, keepdims=True)
                p = (e * (1.0 / total)).astype(BF).reshape(1024, 256)
                probs[d, s * 2 + quad] = p
                att[d, rows, pl.ds(quad * 256, 256)] = unstacked(dot(p, v)).astype(BF)
        middle = stream[d, 0] + dot(att[d], wo[d])
        stream[d, 1] = middle
        hat, _ = ln_parts(middle)
        normed2[d] = (hat * lnp[d, 1:2] + lnp[d, 3:4]).astype(BF)

        def chunk(c, _):
            cols = pl.ds(pl.multiple_of(c * 512, 512), 512)
            value, grad = gelu_pair(dot(normed2[d], wu[d, :, cols]))
            gated[d, :, cols] = value.astype(BF)
            slope[d, :, cols] = grad.astype(BF)
            return 0

        lax.fori_loop(0, 4, chunk, 0)
        stream[d + 1, 0] = stream[d, 1] + dot(gated[d], wd[d])
        return 0

    lax.fori_loop(0, layers, forward, 0)
    for s in range(2):
        act[s] = stream[layers, 0, pl.ds(s * 256, 252), :].astype(BF)
        up[pl.ds(s * 256, 252), :] = cot[s].astype(F32)
        up[pl.ds(s * 256 + 252, 4), :] = jnp.zeros((4, WIDTH), F32)
    lng[...] = jnp.zeros_like(lng)

    def backward(i, _):
        d = layers - 1 - i
        down = up[...].astype(BF)

        def chunk(c, _):
            cols = pl.ds(pl.multiple_of(c * 256, 256), 256)
            part = dot_rows(gated[d, :, cols], down).astype(BF).reshape(2, 4, 32, WIDTH)
            for core in range(2):
                for j in range(4):
                    g[d, core, c, :, pl.ds(4096 + 512 * j, 512)] = part[core, j]
            back = dot_lanes(down, wd[d, cols, :])
            back = (back * slope[d, :, cols].astype(F32)).astype(BF)
            back_up[:, cols] = back
            part = dot_rows(normed2[d], back).astype(BF).reshape(8, 2, 32, 256)
            out = pl.ds(pl.multiple_of(2048 + c * 256, 256), 256)
            for core in range(2):
                g[d, core, :, :, out] = part[:, core]
            return 0

        lax.fori_loop(0, 8, chunk, 0)
        back, gain, shift = ln_back(stream[d, 1], dot_lanes(back_up[...], wu[d]), lnp[d, 1:2])
        lng[pl.ds(d * 4 + 1, 1), :] = gain
        lng[pl.ds(d * 4 + 3, 1), :] = shift
        up[...] += back
        branch = up[...].astype(BF)
        scatter_rows(g, d, pl.ds(1536, 512), dot_rows(att[d], branch))
        back_att[...] = dot_lanes(branch, wo[d]).astype(BF)
        for s in range(2):
            rows = pl.ds(s * 256, 256)
            for quad in range(2):
                lanes = pl.ds(quad * 256, 256)
                qs = stacked(packed[d, rows, lanes], HEAD_DIM**-0.5)
                k = packed[d, rows, pl.ds(512 + quad * 256, 256)]
                v = packed[d, rows, pl.ds(1024 + quad * 256, 256)]
                outs = stacked(back_att[rows, lanes], 1.0)
                p = probs[d, s * 2 + quad]
                dp = dot_lanes(outs, v)
                pf = p.astype(F32)
                weighted = pf * dp
                total = jnp.sum(weighted, axis=-1, keepdims=True)
                ds = (weighted - pf * total).astype(BF)
                back_packed[rows, lanes] = (unstacked(dot(ds, k)) * HEAD_DIM**-0.5).astype(BF)
                back_packed[rows, pl.ds(512 + quad * 256, 256)] = dot_rows(ds, qs).astype(BF)
                back_packed[rows, pl.ds(1024 + quad * 256, 256)] = dot_rows(p, outs).astype(BF)
        for c in range(3):
            cols = pl.ds(c * 512, 512)
            scatter_rows(g, d, cols, dot_rows(normed[d], back_packed[:, cols]))
        back, gain, shift = ln_back(stream[d, 0], dot_lanes(back_packed[...], wq[d]), lnp[d, 0:1])
        lng[pl.ds(d * 4, 1), :] = gain
        lng[pl.ds(d * 4 + 2, 1), :] = shift
        up[...] += back
        return 0

    lax.fori_loop(0, layers, backward, 0)
    eg[...] = up[...].astype(BF)
    turned = jnp.transpose(lng[...]).astype(BF).reshape(8, 2, 32, 128)
    for core in range(2):
        gl[core] = turned[:, core]


def run_layers(tok, cot, lens, lnp, wq, wo, wu, wd):
    layers = wq.shape[0]
    vm = pl.BlockSpec(memory_space=pltpu.VMEM)
    sm = pl.BlockSpec(memory_space=pltpu.SMEM)
    hb = pl.BlockSpec(memory_space=pl.ANY)
    rows = 512
    return pl.pallas_call(
        layers_kernel,
        in_specs=[vm, vm, sm, vm, hb, hb, hb, hb],
        out_specs=[vm, vm, vm, vm],
        out_shape=[
            jax.ShapeDtypeStruct((2, 252, WIDTH), BF),
            jax.ShapeDtypeStruct((rows, WIDTH), BF),
            jax.ShapeDtypeStruct((layers, 2, 8, 32, LAYER_COLS), BF),
            jax.ShapeDtypeStruct((2, 8, 32, 128), BF),
        ],
        scratch_shapes=[
            pltpu.VMEM(wq.shape, BF),
            pltpu.VMEM(wo.shape, BF),
            pltpu.VMEM(wu.shape, BF),
            pltpu.VMEM(wd.shape, BF),
            pltpu.VMEM((layers + 1, 2, rows, WIDTH), F32),
            pltpu.VMEM((layers, rows, WIDTH), BF),
            pltpu.VMEM((layers, rows, 3 * WIDTH), BF),
            pltpu.VMEM((layers, 4, 1024, 256), BF),
            pltpu.VMEM((layers, rows, WIDTH), BF),
            pltpu.VMEM((layers, rows, WIDTH), BF),
            pltpu.VMEM((layers, rows, 4 * WIDTH), BF),
            pltpu.VMEM((layers, rows, 4 * WIDTH), BF),
            pltpu.VMEM((2, 256, 256), F32),
            pltpu.VMEM((rows, WIDTH), F32),
            pltpu.VMEM((rows, 4 * WIDTH), BF),
            pltpu.VMEM((rows, WIDTH), BF),
            pltpu.VMEM((rows, 3 * WIDTH), BF),
            pltpu.VMEM((128, WIDTH), F32),
            pltpu.SemaphoreType.DMA((layers, 4)),
        ],
        compiler_params=pltpu.CompilerParams(vmem_limit_bytes=VMEM_LIMIT),
        name="layers",
    )(tok, cot, lens, lnp, wq, wo, wu, wd)


def enc_bwd_kernel(eg, xl, blocks, g1, g2, w2, ids, e, dpool, bs, bf, acc2, acc1):
    step = pl.program_id(0)

    @pl.when(step == 0)
    def _():
        hot = jnp.where(iota((512, TABLE), 1) == ids[...], 1.0, 0.0).astype(BF)
        code = dot_rows(eg[...], hot[:, :POOL_AT + 96]).astype(BF)
        dpool[...] = dot_rows(hot[:, POOL_AT : POOL_AT + 96], eg[...])
        parts = code[:, :CODES].reshape(8, 2, 32, CODES)
        tail = code[:, CODES : CODES + 128].reshape(8, 2, 32, 128)
        for core in range(2):
            e[core, :, :, pl.ds(512, CODES)] = parts[:, core]
            e[core, :, :, pl.ds(1536, 128)] = tail[:, core]
        acc2[...] = jnp.zeros_like(acc2)
        acc1[...] = jnp.zeros_like(acc1)

    pooled = dpool[pl.ds(pl.multiple_of(step * 32, 32), 32), :][:FRAMES_BLOCK] * (1.0 / 64.0)
    wide = jnp.broadcast_to(pooled[:, None, :], (FRAMES_BLOCK, 8, WIDTH)).reshape(BLOCK_ROWS, WIDTH)

    def part(bx, _):
        rows = pl.ds(pl.multiple_of(bx * BLOCK_ROWS, BLOCK_ROWS), BLOCK_ROWS)
        back = (wide * g2[0, rows, :].astype(F32)).astype(BF)
        bs[rows, :] = back
        bf[rows, :] = (dot_lanes(back, w2[...]) * g1[0, rows, :].astype(F32)).astype(BF)
        return 0

    lax.fori_loop(0, 8, part, 0)
    acc2[...] += dot_rows(bs[...], blocks[0])
    for dy2 in range(2):
        acc1[:, pl.ds(dy2 * 256, 256)] += dot_rows(
            xl[0, :, pl.ds(dy2 * 128, 128)], bf[:, pl.ds(dy2 * 256, 256)]
        )

    @pl.when(step == pl.num_programs(0) - 1)
    def _():
        parts = acc2[...].astype(BF).reshape(8, 2, 32, WIDTH)
        both = acc1[:, pl.ds(0, 256)] + acc1[:, pl.ds(256, 256)]
        hot, rest = patch_index(128)
        first = jnp.where(rest[:, :1] < 12, both[:, :128], both[:, 128:])
        first = lax.dot_general(
            first, hot, (((0,), (0,)), ((), ())), preferred_element_type=F32,
            precision=lax.Precision.HIGHEST,
        )
        first = first.reshape(8, 2, 8, 48)
        first = jnp.concatenate([first, jnp.zeros((8, 2, 24, 48), F32)], axis=2).astype(BF)
        for core in range(2):
            e[core, :, :, pl.ds(0, WIDTH)] = parts[:, core]
            e[core, :, :, pl.ds(1536 + 64, 48)] = first[:, core]


def enc_backward(eg, xl, blocks, g1, g2, w2, ids):
    grid, rows, _ = xl.shape

    def whole(shape):
        return pl.BlockSpec(shape, lambda i: (0,) * len(shape))

    def saved(lanes):
        return pl.BlockSpec((1, rows, lanes), lambda i: (i, 0, 0))

    return pl.pallas_call(
        enc_bwd_kernel,
        grid=(grid,),
        in_specs=[
            whole(eg.shape), saved(256), saved(512), saved(512), saved(512),
            whole(w2.shape), whole(ids.shape),
        ],
        out_specs=whole((2, 8, 32, ENC_COLS)),
        out_shape=jax.ShapeDtypeStruct((2, 8, 32, ENC_COLS), BF),
        scratch_shapes=[
            pltpu.VMEM((96, WIDTH), F32),
            pltpu.VMEM((rows, WIDTH), BF),
            pltpu.VMEM((rows, WIDTH), BF),
            pltpu.VMEM((WIDTH, WIDTH), F32),
            pltpu.VMEM((128, WIDTH), F32),
        ],
        compiler_params=pltpu.CompilerParams(vmem_limit_bytes=VMEM_LIMIT),
        name="enc_bwd",
    )(eg, xl, blocks, g1, g2, w2, ids)


CHIPS = 8
HOPS = CHIPS - 1
MESH = pl.DeviceIdType.MESH


def ring_place(chip):
    z, x = chip // 2, chip % 2
    return z * (1 - x) + (7 - z) * x


def ring_chip(place):
    half = place // 4
    return (1 - half) * (2 * place) + half * (15 - 2 * place)


def where_am_i():
    section, me = lax.axis_index("section"), lax.axis_index("dp")
    core, chip = me % 2, me // 2
    place = ring_place(chip)
    ahead = ring_chip((place + 1) % CHIPS) * 2 + core
    behind = ring_chip((place + CHIPS - 1) % CHIPS) * 2 + core
    sibling = chip * 2 + (1 - core)
    return section, me, core, place, ahead, behind, sibling


def greet():
    section, me, _, _, ahead, behind, sibling = where_am_i()
    barrier = pltpu.get_barrier_semaphore()
    for target in ((section, sibling), (section, ahead), (section, behind), (1 - section, me)):
        pl.semaphore_signal(barrier, inc=1, device_id=target, device_id_type=MESH)
    pl.semaphore_wait(barrier, 4)


class Ring:
    def __init__(self, part, pair, hop, pair_sem, send_sem, recv_sem):
        self.part, self.pair, self.hop = part, pair, hop
        self.pair_sem, self.send_sem, self.recv_sem = pair_sem, send_sem, recv_sem

    def pair_copy(self):
        section, _, core, _, _, _, sibling = where_am_i()
        return pltpu.make_async_remote_copy(
            src_ref=self.part.at[1 - core], dst_ref=self.pair,
            send_sem=self.pair_sem.at[0], recv_sem=self.pair_sem.at[1],
            device_id=(section, sibling), device_id_type=MESH,
        )

    def target(self, way, step):
        place = where_am_i()[3]
        move = CHIPS - 1 - step if way == 0 else 1 + step
        return ring_chip((place + move) % CHIPS)

    def hop_copy(self, way, step):
        section, _, _, _, ahead, behind, _ = where_am_i()
        return pltpu.make_async_remote_copy(
            src_ref=self.pair.at[self.target(way, step), pl.ds(16 * way, 16)],
            dst_ref=self.hop.at[way, step],
            send_sem=self.send_sem.at[way, step], recv_sem=self.recv_sem.at[way, step],
            device_id=(section, ahead if way == 0 else behind), device_id_type=MESH,
        )

    def total(self, way, step, first):
        core = where_am_i()[2]
        at, rows = self.target(way, step), pl.ds(16 * way, 16)
        value = self.part[core, at, rows, :].astype(F32) + self.pair[at, rows, :].astype(F32)
        if not first:
            value += self.hop[way, step - 1].astype(F32)
        return value

    def start(self):
        self.pair_copy().start()

    def open(self):
        self.pair_copy().wait()
        for way in range(2):
            value = self.total(way, 0, True)
            self.pair[self.target(way, 0), pl.ds(16 * way, 16), :] = value.astype(BF)
            self.hop_copy(way, 0).start()

    def step(self, step):
        for way in range(2):
            self.hop_copy(way, step - 1).wait()
            value = self.total(way, step, False)
            self.pair[self.target(way, step), pl.ds(16 * way, 16), :] = value.astype(BF)
            self.hop_copy(way, step).start()

    def close(self, out):
        for way in range(2):
            self.hop_copy(way, HOPS - 1).wait()
            out[pl.ds(16 * way, 16), :] = self.total(way, HOPS, False).astype(out.dtype)


def cross_copy(src, dst, sem):
    section, me = lax.axis_index("section"), lax.axis_index("dp")
    return pltpu.make_async_remote_copy(
        src_ref=src, dst_ref=dst, send_sem=sem.at[0], recv_sem=sem.at[1],
        device_id=(1 - section, me), device_id_type=MESH,
    )


def sums_kernel(*refs):
    count = 4
    (g, gl, e), refs = refs[:3], refs[3:]
    parts = [g.at[1], g.at[0], gl, e]
    outs, refs = refs[:count], refs[count:]
    pairs, refs = refs[:count], refs[count:]
    hops, refs = refs[:count], refs[count:]
    mine, refs = refs[: count - 1], refs[count - 1 :]
    theirs, refs = refs[: count - 1], refs[count - 1 :]
    pair_sem, send_sem, recv_sem, cross_sem = refs
    greet()
    rings = [
        Ring(parts[k], pairs[k], hops[k], pair_sem.at[k], send_sem.at[k], recv_sem.at[k])
        for k in range(count)
    ]
    for ring in rings:
        ring.start()
    for ring in rings:
        ring.open()

    def hop(step, _):
        for ring in rings:
            ring.step(step)
        return 0

    lax.fori_loop(1, HOPS, hop, 0)
    crossings = []
    for k in range(count - 1):
        rings[k].close(mine[k])
        crossing = cross_copy(mine[k], theirs[k], cross_sem.at[k])
        crossing.start()
        crossings.append(crossing)
    rings[count - 1].close(outs[count - 1])
    for k in range(count - 1):
        crossings[k].wait()
        outs[k][...] = theirs[k][...]


def scatter_ring(g, gl, e):
    count = 4
    widths = [g.shape[-1], g.shape[-1], gl.shape[-1], e.shape[-1]]
    vm = pl.BlockSpec(memory_space=pltpu.VMEM)
    return pl.pallas_call(
        sums_kernel,
        in_specs=[vm] * 3,
        out_specs=[vm] * count,
        out_shape=[jax.ShapeDtypeStruct((32, n), BF) for n in widths],
        scratch_shapes=(
            [pltpu.VMEM((CHIPS, 32, n), BF) for n in widths]
            + [pltpu.VMEM((2, HOPS, 16, n), BF) for n in widths]
            + [pltpu.VMEM((32, n), BF) for n in widths[:-1]] * 2
            + [
                pltpu.SemaphoreType.DMA((count, 2)),
                pltpu.SemaphoreType.DMA((count, 2, HOPS)),
                pltpu.SemaphoreType.DMA((count, 2, HOPS)),
                pltpu.SemaphoreType.DMA((count - 1, 2)),
            ]
        ),
        compiler_params=pltpu.CompilerParams(
            collective_id=0, has_side_effects=True, vmem_limit_bytes=VMEM_LIMIT
        ),
        name="sums",
    )(g, gl, e)


def turn(rows):
    tall = jnp.concatenate([rows, jnp.zeros((96, rows.shape[1]), F32)], axis=0)
    return jnp.transpose(tall)[:, :32]


def outputs_kernel(late, early, norm, enc, qkv, out, up, down, gain, bias, bias2, enc1, enc2, book, acts):
    for d, rows in enumerate((early, late)):
        qkv[0, d] = rows[:, pl.ds(0, 1536)].astype(F32)
        out[0, d] = rows[:, pl.ds(1536, 512)].astype(F32)
        up[0, d] = rows[:, pl.ds(2048, 2048)].astype(F32)
        for j in range(4):
            down[0, d, pl.ds(32 * j, 32), :] = rows[:, pl.ds(4096 + 512 * j, 512)].astype(F32)
    turned = turn(norm[...].astype(F32))
    for d in range(2):
        gain[0, d] = norm[...].astype(F32)[:, 4 * d : 4 * d + 2]
        bias[0, pl.ds(d, 1)] = turned[4 * d + 2 : 4 * d + 3]
        bias2[0, pl.ds(d, 1)] = turned[4 * d + 3 : 4 * d + 4]
    enc2[0] = turn(enc[:, pl.ds(0, 512)].astype(F32))
    book[0] = turn(enc[:, pl.ds(512, 1024)].astype(F32))
    turned = turn(enc[:, pl.ds(1536, 128)].astype(F32))
    acts[0] = turned[:17]
    enc1[0] = turned[64:112, :8]


def spread_outputs(late, early, norm, enc):
    vm = pl.BlockSpec(memory_space=pltpu.VMEM)
    shapes = [
        (1, 2, 32, 1536), (1, 2, 32, 512), (1, 2, 32, 2048), (1, 2, 128, 512), (1, 2, 32, 2),
        (1, 2, 32), (1, 2, 32), (1, 48, 8), (1, 512, 32), (1, 1024, 32), (1, 17, 32),
    ]
    return pl.pallas_call(
        outputs_kernel,
        in_specs=[vm] * 4,
        out_specs=[vm] * len(shapes),
        out_shape=[jax.ShapeDtypeStruct(shape, F32) for shape in shapes],
        compiler_params=pltpu.CompilerParams(vmem_limit_bytes=VMEM_LIMIT),
        name="outputs",
    )(late, early, norm, enc)


def swap(array):
    return lax.ppermute(array, "section", [(0, 1), (1, 0)])


def whole_rows(g):
    return g.transpose(1, 0, 2, 3).reshape(512, g.shape[-1])


def scatter_plain(g, gl, e):
    def sums(array, axis):
        return lax.psum_scatter(array.astype(F32)[None], "dp", scatter_dimension=axis, tiled=True)

    layers = [whole_rows(g[d]) for d in range(g.shape[0])]
    qkv = jnp.stack([rows[:, :1536] for rows in layers])
    out = jnp.stack([rows[:, 1536:2048] for rows in layers])
    up = jnp.stack([rows[:, 2048:4096] for rows in layers])
    down = jnp.stack(
        [
            rows[:, 4096:].reshape(16, 32, 4, WIDTH).transpose(0, 2, 1, 3).reshape(2048, WIDTH)
            for rows in layers
        ]
    )
    norm = whole_rows(gl)[:, :8].reshape(512, 2, 4).transpose(1, 0, 2)
    enc = whole_rows(e)
    first = e.transpose(1, 0, 2, 3)[:, :, :8, 1600:1648].reshape(128, 48)
    layer_sums = [sums(x, 2) for x in (qkv, out, up, down, norm)]
    layer_sums = [swap(x) for x in layer_sums]
    norm = layer_sums.pop()
    return tuple(layer_sums) + (
        norm[..., 0:2],
        norm[..., 2],
        norm[..., 3],
        sums(first.T, 2),
        sums(enc[:, :512].T, 2),
        sums(enc[:, 512:1536].T, 2),
        sums(enc[:, 1536:1553].T, 2),
    )


def on_device(
    frames, action_ids, delta_ids, seq_len, enc_w1, enc_w2, codebook, action_table,
    ln_gain, ln_bias, w_qkv, w_out, w_up, w_down, cotangent,
):
    micro, steps = frames.shape[1], frames.shape[2]
    count = micro * steps
    frame = jnp.arange(count, dtype=I32).reshape(micro, steps, 1)
    pool_ids = POOL_AT + (frame // FRAMES_BLOCK) * 32 + frame % FRAMES_BLOCK
    ids = jnp.concatenate([pool_ids, action_ids[0][:, :, None] + ACT_AT, delta_ids[0]], axis=2)
    ids = ids.reshape(micro, steps * TPS)
    ids = jnp.pad(ids, ((0, 0), (0, 256 - steps * TPS)), constant_values=-1).reshape(512, 1)
    lnp = jnp.concatenate([ln_gain, ln_bias], axis=2).transpose(0, 2, 1)

    cot = swap(cotangent[0])
    tok, xl, blocks, g1, g2 = enc_forward(
        frames.reshape((count,) + frames.shape[3:]), enc_w1, enc_w2, codebook, action_table, ids
    )
    act, eg, g, gl = run_layers(tok, cot, seq_len, lnp, w_qkv, w_out, w_up, w_down)
    activations = swap(act)[None]
    embed_grad = eg.reshape(micro, 256, WIDTH)[None, :, : steps * TPS]
    e = enc_backward(eg, xl, blocks, g1, g2, enc_w2, ids)
    if lax.axis_size("dp") == 2 * CHIPS:
        late, early, norm, enc = scatter_ring(g, gl, e)
        return (activations, embed_grad) + tuple(spread_outputs(late, early, norm, enc))
    return (activations, embed_grad) + scatter_plain(g, gl, e)


def solution(mesh):
    return jax.shard_map(
        on_device,
        mesh=mesh,
        in_specs=(
            P("section", "dp", None, None, None),
            P("section", "dp", None),
            P("section", "dp", None, None),
            P(None, "dp"),
            P(), P(), P(), P(), P(), P(), P(), P(), P(), P(),
            P("section", "dp", None, None),
        ),
        out_specs=(
            P("section", "dp", None, None),
            P("section", "dp", None, None),
            P("section", None, "dp", None),
            P("section", None, "dp", None),
            P("section", None, "dp", None),
            P("section", None, "dp", None),
            P("section", None, "dp", None),
            P("section", None, "dp"),
            P("section", None, "dp"),
            P("section", None, "dp"),
            P("section", None, "dp"),
            P("section", None, "dp"),
            P("section", None, "dp"),
        ),
        check_vma=False,
    )
```

```python
import functools

import jax
import jax.numpy as jnp
from jax import lax
from jax.experimental import pallas as pl
from jax.experimental.pallas import tpu as pltpu
from jax.sharding import PartitionSpec as P

HEADS = 8
HEAD_DIM = 64
TPS = 6
EPS = 1e-05
BF = jnp.bfloat16
F32 = jnp.float32
I32 = jnp.int32

WIDTH = 512
CODES = 1024
FRAMES_BLOCK = 28
BLOCK_ROWS = FRAMES_BLOCK * 8
TABLE = 1152
POOL_AT = 1056
ACT_AT = 1024
LAYER_COLS = 6144
ENC_COLS = 1664
VMEM_LIMIT = 60 << 20


def dot(a, b):
    return jnp.dot(a, b, preferred_element_type=F32)


def dot_rows(a, b):
    return lax.dot_general(a, b, (((0,), (0,)), ((), ())), preferred_element_type=F32)


def dot_lanes(a, b):
    return lax.dot_general(a, b, (((1,), (1,)), ((), ())), preferred_element_type=F32)


def iota(shape, axis):
    return lax.broadcasted_iota(I32, shape, axis)


def gelu_pair(v):
    e = jnp.exp2(v * v * (-0.5 * 1.4426950408889634))
    t = 1.0 / (1.0 + 0.23164190 * jnp.abs(v))
    poly = 0.5 * 1.061405429
    poly = poly * t + 0.5 * -1.453152027
    poly = poly * t + 0.5 * 1.421413741
    poly = poly * t + 0.5 * -0.284496736
    poly = poly * t + 0.5 * 0.254829592
    tail = poly * t * e
    cdf = jnp.where(v >= 0, 1.0 - tail, tail)
    return v * cdf, cdf + v * e * 0.3989422804014327


def patch_index(rows):
    k = iota((rows, 48), 0)
    dy = (k * 2731) >> 16
    rest = k - dy * 24
    j = jnp.where(rest >= 12, rest - 12, rest)
    return jnp.where((iota((rows, 48), 1) == dy * 12 + j) & (k < 96), 1.0, 0.0), rest


def encoder_weights(w1):
    hot, rest = patch_index(128)
    wide = dot(hot.astype(BF), w1)
    first = jnp.where(rest[:, :1] < 12, wide, 0.0)
    second = jnp.where(rest[:, :1] >= 12, wide, 0.0)
    block = jnp.concatenate([first, second], axis=1)
    zero = jnp.zeros_like(block)
    return jnp.concatenate(
        [jnp.concatenate([block, zero], axis=1), jnp.concatenate([zero, block], axis=1)], axis=0
    ).astype(BF)


def enc_fwd_kernel(
    frames, w1, w2, book, acts, ids, tok, xl, blocks, g1, g2, perm, lanes, big, xs, acc, table
):
    step = pl.program_id(0)

    @pl.when(step == 0)
    def _():
        a, b = iota((256, 256), 0), iota((256, 256), 1)
        perm[...] = jnp.where(b == 8 * (a & 31) + (a >> 5), 1.0, 0.0).astype(BF)
        src = iota((192, 1024), 0)
        px = (src * 5462) >> 16
        at = (px >> 1) * 128 + (px & 1) * 12 + (src - px * 12)
        out = iota((192, 1024), 1)
        for dy in range(4):
            lanes[dy] = jnp.where(out == at + dy * 24, 1.0, 0.0).astype(BF)
        big[...] = encoder_weights(w1[...])
        table[pl.ds(0, CODES), :] = book[...]
        named = acts[...].astype(F32)
        pad = jnp.zeros((TABLE - ACT_AT - named.shape[0], WIDTH), F32)
        table[pl.ds(ACT_AT, TABLE - ACT_AT), :] = jnp.concatenate([named, pad], axis=0).astype(BF)

    for group in range(FRAMES_BLOCK // 4):
        rows = frames[pl.ds(group * 4, 4)].reshape(256, 192)
        moved = dot(perm[...], rows).astype(BF).reshape(8, 32, 192)
        xs[:, pl.ds(group * 32, 32), :] = moved
    for dy2 in range(2):
        spread = dot(xs[dy2 * 4], lanes[0])
        for dy in range(1, 4):
            spread += dot(xs[dy2 * 4 + dy], lanes[dy])
        spread = spread.astype(BF)
        for bx in range(8):
            xl[0, pl.ds(bx * BLOCK_ROWS, BLOCK_ROWS), pl.ds(dy2 * 128, 128)] = spread[
                :, bx * 128 : (bx + 1) * 128
            ]
    acc[...] = jnp.zeros_like(acc)

    def part(bx, _):
        rows = pl.ds(pl.multiple_of(bx * BLOCK_ROWS, BLOCK_ROWS), BLOCK_ROWS)
        value, slope = gelu_pair(dot(xl[0, rows, :], big[...]))
        value = value.astype(BF)
        blocks[0, rows, :] = value
        g1[0, rows, :] = slope.astype(BF)
        value, slope = gelu_pair(dot(value, w2[...]))
        g2[0, rows, :] = slope.astype(BF)
        acc[...] += value
        return 0

    lax.fori_loop(0, 8, part, 0)
    pooled = jnp.sum(acc[...].reshape(FRAMES_BLOCK, 8, WIDTH), axis=1) * (1.0 / 64.0)
    pooled = jnp.concatenate([pooled, jnp.zeros((32 - FRAMES_BLOCK, WIDTH), F32)], axis=0)
    table[pl.ds(pl.multiple_of(POOL_AT + step * 32, 32), 32), :] = pooled.astype(BF)

    @pl.when(step == pl.num_programs(0) - 1)
    def _():
        for part_at in range(2):
            rows = pl.ds(part_at * 256, 256)
            hot = jnp.where(iota((256, TABLE), 1) == ids[rows, :], 1.0, 0.0).astype(BF)
            tok[rows, :] = dot(hot, table[...]).astype(BF)


def enc_forward(frames, w1, w2, book, acts, ids):
    count = frames.shape[0]
    grid = count // FRAMES_BLOCK
    rows = 8 * BLOCK_ROWS

    def whole(shape):
        return pl.BlockSpec(shape, lambda i: (0,) * len(shape))

    def saved(lanes):
        return pl.BlockSpec((1, rows, lanes), lambda i: (i, 0, 0))

    return pl.pallas_call(
        enc_fwd_kernel,
        grid=(grid,),
        in_specs=[
            pl.BlockSpec((FRAMES_BLOCK, 64, 192), lambda i: (i, 0, 0)),
            whole(w1.shape),
            whole(w2.shape),
            whole(book.shape),
            whole(acts.shape),
            whole(ids.shape),
        ],
        out_specs=[whole((512, WIDTH)), saved(256), saved(512), saved(512), saved(512)],
        out_shape=[
            jax.ShapeDtypeStruct((512, WIDTH), BF),
            jax.ShapeDtypeStruct((grid, rows, 256), BF),
            jax.ShapeDtypeStruct((grid, rows, 512), BF),
            jax.ShapeDtypeStruct((grid, rows, 512), BF),
            jax.ShapeDtypeStruct((grid, rows, 512), BF),
        ],
        scratch_shapes=[
            pltpu.VMEM((256, 256), BF),
            pltpu.VMEM((4, 192, 1024), BF),
            pltpu.VMEM((256, 512), BF),
            pltpu.VMEM((8, BLOCK_ROWS, 192), BF),
            pltpu.VMEM((BLOCK_ROWS, WIDTH), F32),
            pltpu.VMEM((TABLE, WIDTH), BF),
        ],
        compiler_params=pltpu.CompilerParams(vmem_limit_bytes=VMEM_LIMIT),
        name="enc_fwd",
    )(frames, w1, w2, book, acts, ids)


def ln_parts(x):
    mean = jnp.mean(x, axis=-1, keepdims=True)
    center = x - mean
    var = jnp.mean(center * center, axis=-1, keepdims=True)
    scale = lax.rsqrt(var + EPS)
    return center * scale, scale


def ln_back(x, d, gain):
    hat, scale = ln_parts(x)
    dh = d * gain
    one = jnp.mean(dh, axis=-1, keepdims=True)
    two = jnp.mean(dh * hat, axis=-1, keepdims=True)
    back = scale * (dh - one - hat * two)
    return back, jnp.sum(d * hat, axis=0, keepdims=True), jnp.sum(d, axis=0, keepdims=True)


def head_mask(h):
    lane = iota((1, 256), 1) >> 6
    return lane == h


def stacked(rows, scale):
    out = []
    for h in range(4):
        mask = jnp.where(head_mask(h), scale, 0.0).astype(BF)
        out.append(rows * mask)
    return jnp.concatenate(out, axis=0)


def unstacked(rows):
    out = rows[768:]
    for h in range(3):
        out = jnp.where(head_mask(h), rows[h * 256 : (h + 1) * 256], out)
    return out


def scatter_rows(g, d, cols, value, dests=16):
    shaped = value.astype(BF).reshape(dests // 2, 2, 32, value.shape[1])
    for core in range(2):
        g[d, core, :, :, cols] = shaped[:, core]


def layers_kernel(
    tok, cot_h, lens, lnp, wq_h, wo_h, wu_h, wd_h,
    act, eg, g, gl,
    wq, wo, wu, wd, stream, normed, packed, probs, att, normed2, gated, slope, bias,
    up, back_up, back_att, back_packed, lng, cot, mine, theirs, sems, cross_sem,
):
    layers = wq.shape[0]
    section = lax.axis_index("section")
    barrier = pltpu.get_barrier_semaphore()
    pl.semaphore_signal(
        barrier, inc=1, device_id=(1 - section, lax.axis_index("dp")), device_id_type=MESH
    )
    pl.semaphore_wait(barrier, 1)
    cot_copy = cross_copy(cot_h, cot, cross_sem.at[0])
    cot_copy.start()
    act_copy = cross_copy(mine, theirs, cross_sem.at[1])
    copies = []
    for d in range(layers):
        for k, (src, dst) in enumerate(((wq_h, wq), (wo_h, wo), (wu_h, wu), (wd_h, wd))):
            copy = pltpu.make_async_copy(src.at[d], dst.at[d], sems.at[d, k])
            copy.start()
            copies.append(copy)

    stream[0, 0] = tok[...].astype(F32)
    row = iota((256, 1), 0)
    col = iota((1, 256), 1)
    q_step = ((row * 10923) >> 16).astype(F32)
    k_step = ((col * 10923) >> 16).astype(F32)
    for s in range(2):
        inv = 1.0 / lens[section, s].astype(F32)
        q_seq = jnp.floor((q_step + 0.5) * inv)
        k_seq = jnp.floor((k_step + 0.5) * inv)
        bias[s] = jnp.where((k_step <= q_step) & (q_seq == k_seq), 0.0, -1e30)
    for copy in copies:
        copy.wait()

    def forward(d, _):
        x = stream[d, 0]
        hat, _ = ln_parts(x)
        normed[d] = (hat * lnp[d, 0:1] + lnp[d, 2:3]).astype(BF)
        for c in range(3):
            cols = pl.ds(c * 512, 512)
            packed[d, :, cols] = dot(normed[d], wq[d, :, cols]).astype(BF)
        for s in range(2):
            rows = pl.ds(s * 256, 256)
            for quad in range(2):
                q = stacked(packed[d, rows, pl.ds(quad * 256, 256)], HEAD_DIM**-0.5)
                k = packed[d, rows, pl.ds(512 + quad * 256, 256)]
                v = packed[d, rows, pl.ds(1024 + quad * 256, 256)]
                scores = dot_lanes(q, k).reshape(4, 256, 256) + bias[s][None]
                top = jnp.max(scores, axis=-1, keepdims=True)
                e = jnp.exp(scores - top)
                total = jnp.sum(e, axis=-1, keepdims=True)
                p = (e * (1.0 / total)).astype(BF).reshape(1024, 256)
                probs[d, s * 2 + quad] = p
                att[d, rows, pl.ds(quad * 256, 256)] = unstacked(dot(p, v)).astype(BF)
        middle = stream[d, 0] + dot(att[d], wo[d])
        stream[d, 1] = middle
        hat, _ = ln_parts(middle)
        normed2[d] = (hat * lnp[d, 1:2] + lnp[d, 3:4]).astype(BF)

        def chunk(c, _):
            cols = pl.ds(pl.multiple_of(c * 512, 512), 512)
            value, grad = gelu_pair(dot(normed2[d], wu[d, :, cols]))
            gated[d, :, cols] = value.astype(BF)
            slope[d, :, cols] = grad.astype(BF)
            return 0

        lax.fori_loop(0, 4, chunk, 0)
        stream[d + 1, 0] = stream[d, 1] + dot(gated[d], wd[d])
        return 0

    lax.fori_loop(0, layers, forward, 0)
    cot_copy.wait()
    mine[...] = stream[layers, 0].astype(BF)
    act_copy.start()
    for s in range(2):
        up[pl.ds(s * 256, 252), :] = cot[s].astype(F32)
        up[pl.ds(s * 256 + 252, 4), :] = jnp.zeros((4, WIDTH), F32)
    lng[...] = jnp.zeros_like(lng)

    def backward(i, _):
        d = layers - 1 - i
        down = up[...].astype(BF)

        def chunk(c, _):
            cols = pl.ds(pl.multiple_of(c * 256, 256), 256)
            part = dot_rows(gated[d, :, cols], down).astype(BF).reshape(2, 4, 32, WIDTH)
            for core in range(2):
                for j in range(4):
                    g[d, core, c, :, pl.ds(4096 + 512 * j, 512)] = part[core, j]
            back = dot_lanes(down, wd[d, cols, :])
            back = (back * slope[d, :, cols].astype(F32)).astype(BF)
            back_up[:, cols] = back
            part = dot_rows(normed2[d], back).astype(BF).reshape(8, 2, 32, 256)
            out = pl.ds(pl.multiple_of(2048 + c * 256, 256), 256)
            for core in range(2):
                g[d, core, :, :, out] = part[:, core]
            return 0

        lax.fori_loop(0, 8, chunk, 0)
        back, gain, shift = ln_back(stream[d, 1], dot_lanes(back_up[...], wu[d]), lnp[d, 1:2])
        lng[pl.ds(d * 4 + 1, 1), :] = gain
        lng[pl.ds(d * 4 + 3, 1), :] = shift
        up[...] += back
        branch = up[...].astype(BF)
        scatter_rows(g, d, pl.ds(1536, 512), dot_rows(att[d], branch))
        back_att[...] = dot_lanes(branch, wo[d]).astype(BF)
        for s in range(2):
            rows = pl.ds(s * 256, 256)
            for quad in range(2):
                lanes = pl.ds(quad * 256, 256)
                qs = stacked(packed[d, rows, lanes], HEAD_DIM**-0.5)
                k = packed[d, rows, pl.ds(512 + quad * 256, 256)]
                v = packed[d, rows, pl.ds(1024 + quad * 256, 256)]
                outs = stacked(back_att[rows, lanes], 1.0)
                p = probs[d, s * 2 + quad]
                dp = dot_lanes(outs, v)
                pf = p.astype(F32)
                weighted = pf * dp
                total = jnp.sum(weighted, axis=-1, keepdims=True)
                ds = (weighted - pf * total).astype(BF)
                back_packed[rows, lanes] = (unstacked(dot(ds, k)) * HEAD_DIM**-0.5).astype(BF)
                back_packed[rows, pl.ds(512 + quad * 256, 256)] = dot_rows(ds, qs).astype(BF)
                back_packed[rows, pl.ds(1024 + quad * 256, 256)] = dot_rows(p, outs).astype(BF)
        for c in range(3):
            cols = pl.ds(c * 512, 512)
            scatter_rows(g, d, cols, dot_rows(normed[d], back_packed[:, cols]))
        back, gain, shift = ln_back(stream[d, 0], dot_lanes(back_packed[...], wq[d]), lnp[d, 0:1])
        lng[pl.ds(d * 4, 1), :] = gain
        lng[pl.ds(d * 4 + 2, 1), :] = shift
        up[...] += back
        return 0

    lax.fori_loop(0, layers, backward, 0)
    eg[...] = up[...].astype(BF)
    act_copy.wait()
    for s in range(2):
        act[s] = theirs[pl.ds(s * 256, 256), :].astype(F32)[:252].astype(BF)
    turned = jnp.transpose(lng[...]).astype(BF).reshape(8, 2, 32, 128)
    for core in range(2):
        gl[core] = turned[:, core]


def run_layers(tok, cot, lens, lnp, wq, wo, wu, wd):
    layers = wq.shape[0]
    vm = pl.BlockSpec(memory_space=pltpu.VMEM)
    sm = pl.BlockSpec(memory_space=pltpu.SMEM)
    hb = pl.BlockSpec(memory_space=pl.ANY)
    rows = 512
    return pl.pallas_call(
        layers_kernel,
        in_specs=[vm, hb, sm, vm, hb, hb, hb, hb],
        out_specs=[vm, vm, vm, vm],
        out_shape=[
            jax.ShapeDtypeStruct((2, 252, WIDTH), BF),
            jax.ShapeDtypeStruct((rows, WIDTH), BF),
            jax.ShapeDtypeStruct((layers, 2, 8, 32, LAYER_COLS), BF),
            jax.ShapeDtypeStruct((2, 8, 32, 128), BF),
        ],
        scratch_shapes=[
            pltpu.VMEM(wq.shape, BF),
            pltpu.VMEM(wo.shape, BF),
            pltpu.VMEM(wu.shape, BF),
            pltpu.VMEM(wd.shape, BF),
            pltpu.VMEM((layers + 1, 2, rows, WIDTH), F32),
            pltpu.VMEM((layers, rows, WIDTH), BF),
            pltpu.VMEM((layers, rows, 3 * WIDTH), BF),
            pltpu.VMEM((layers, 4, 1024, 256), BF),
            pltpu.VMEM((layers, rows, WIDTH), BF),
            pltpu.VMEM((layers, rows, WIDTH), BF),
            pltpu.VMEM((layers, rows, 4 * WIDTH), BF),
            pltpu.VMEM((layers, rows, 4 * WIDTH), BF),
            pltpu.VMEM((2, 256, 256), F32),
            pltpu.VMEM((rows, WIDTH), F32),
            pltpu.VMEM((rows, 4 * WIDTH), BF),
            pltpu.VMEM((rows, WIDTH), BF),
            pltpu.VMEM((rows, 3 * WIDTH), BF),
            pltpu.VMEM((128, WIDTH), F32),
            pltpu.VMEM(cot.shape, BF),
            pltpu.VMEM((rows, WIDTH), BF),
            pltpu.VMEM((rows, WIDTH), BF),
            pltpu.SemaphoreType.DMA((layers, 4)),
            pltpu.SemaphoreType.DMA((2, 2)),
        ],
        compiler_params=pltpu.CompilerParams(
            collective_id=1, has_side_effects=True, vmem_limit_bytes=VMEM_LIMIT
        ),
        name="layers",
    )(tok, cot, lens, lnp, wq, wo, wu, wd)


def enc_bwd_kernel(eg, xl, blocks, g1, g2, w2, ids, e, dpool, bs, bf, acc2, acc1):
    step = pl.program_id(0)

    @pl.when(step == 0)
    def _():
        hot = jnp.where(iota((512, TABLE), 1) == ids[...], 1.0, 0.0).astype(BF)
        code = dot_rows(eg[...], hot[:, :POOL_AT + 96]).astype(BF)
        dpool[...] = dot_rows(hot[:, POOL_AT : POOL_AT + 96], eg[...])
        parts = code[:, :CODES].reshape(8, 2, 32, CODES)
        tail = code[:, CODES : CODES + 128].reshape(8, 2, 32, 128)
        for core in range(2):
            e[core, :, :, pl.ds(512, CODES)] = parts[:, core]
            e[core, :, :, pl.ds(1536, 128)] = tail[:, core]
        acc2[...] = jnp.zeros_like(acc2)
        acc1[...] = jnp.zeros_like(acc1)

    pooled = dpool[pl.ds(pl.multiple_of(step * 32, 32), 32), :][:FRAMES_BLOCK] * (1.0 / 64.0)
    wide = jnp.broadcast_to(pooled[:, None, :], (FRAMES_BLOCK, 8, WIDTH)).reshape(BLOCK_ROWS, WIDTH)

    def part(bx, _):
        rows = pl.ds(pl.multiple_of(bx * BLOCK_ROWS, BLOCK_ROWS), BLOCK_ROWS)
        back = (wide * g2[0, rows, :].astype(F32)).astype(BF)
        bs[rows, :] = back
        bf[rows, :] = (dot_lanes(back, w2[...]) * g1[0, rows, :].astype(F32)).astype(BF)
        return 0

    lax.fori_loop(0, 8, part, 0)
    acc2[...] += dot_rows(bs[...], blocks[0])
    for dy2 in range(2):
        acc1[:, pl.ds(dy2 * 256, 256)] += dot_rows(
            xl[0, :, pl.ds(dy2 * 128, 128)], bf[:, pl.ds(dy2 * 256, 256)]
        )

    @pl.when(step == pl.num_programs(0) - 1)
    def _():
        parts = acc2[...].astype(BF).reshape(8, 2, 32, WIDTH)
        both = acc1[:, pl.ds(0, 256)] + acc1[:, pl.ds(256, 256)]
        hot, rest = patch_index(128)
        first = jnp.where(rest[:, :1] < 12, both[:, :128], both[:, 128:])
        first = lax.dot_general(
            first, hot, (((0,), (0,)), ((), ())), preferred_element_type=F32,
            precision=lax.Precision.HIGHEST,
        )
        first = first.reshape(8, 2, 8, 48)
        first = jnp.concatenate([first, jnp.zeros((8, 2, 24, 48), F32)], axis=2).astype(BF)
        for core in range(2):
            e[core, :, :, pl.ds(0, WIDTH)] = parts[:, core]
            e[core, :, :, pl.ds(1536 + 64, 48)] = first[:, core]


def enc_backward(eg, xl, blocks, g1, g2, w2, ids):
    grid, rows, _ = xl.shape

    def whole(shape):
        return pl.BlockSpec(shape, lambda i: (0,) * len(shape))

    def saved(lanes):
        return pl.BlockSpec((1, rows, lanes), lambda i: (i, 0, 0))

    return pl.pallas_call(
        enc_bwd_kernel,
        grid=(grid,),
        in_specs=[
            whole(eg.shape), saved(256), saved(512), saved(512), saved(512),
            whole(w2.shape), whole(ids.shape),
        ],
        out_specs=whole((2, 8, 32, ENC_COLS)),
        out_shape=jax.ShapeDtypeStruct((2, 8, 32, ENC_COLS), BF),
        scratch_shapes=[
            pltpu.VMEM((96, WIDTH), F32),
            pltpu.VMEM((rows, WIDTH), BF),
            pltpu.VMEM((rows, WIDTH), BF),
            pltpu.VMEM((WIDTH, WIDTH), F32),
            pltpu.VMEM((128, WIDTH), F32),
        ],
        compiler_params=pltpu.CompilerParams(vmem_limit_bytes=VMEM_LIMIT),
        name="enc_bwd",
    )(eg, xl, blocks, g1, g2, w2, ids)


CHIPS = 8
HOPS = CHIPS - 1
MESH = pl.DeviceIdType.MESH


def ring_place(chip):
    z, x = chip // 2, chip % 2
    return z * (1 - x) + (7 - z) * x


def ring_chip(place):
    half = place // 4
    return (1 - half) * (2 * place) + half * (15 - 2 * place)


def where_am_i():
    section, me = lax.axis_index("section"), lax.axis_index("dp")
    core, chip = me % 2, me // 2
    place = ring_place(chip)
    ahead = ring_chip((place + 1) % CHIPS) * 2 + core
    behind = ring_chip((place + CHIPS - 1) % CHIPS) * 2 + core
    sibling = chip * 2 + (1 - core)
    return section, me, core, place, ahead, behind, sibling


def greet():
    section, me, _, _, ahead, behind, sibling = where_am_i()
    barrier = pltpu.get_barrier_semaphore()
    for target in ((section, sibling), (section, ahead), (section, behind), (1 - section, me)):
        pl.semaphore_signal(barrier, inc=1, device_id=target, device_id_type=MESH)
    pl.semaphore_wait(barrier, 4)


class Ring:
    def __init__(self, part, pair, hop, pair_sem, send_sem, recv_sem):
        self.part, self.pair, self.hop = part, pair, hop
        self.pair_sem, self.send_sem, self.recv_sem = pair_sem, send_sem, recv_sem

    def pair_copy(self):
        section, _, core, _, _, _, sibling = where_am_i()
        return pltpu.make_async_remote_copy(
            src_ref=self.part.at[1 - core], dst_ref=self.pair,
            send_sem=self.pair_sem.at[0], recv_sem=self.pair_sem.at[1],
            device_id=(section, sibling), device_id_type=MESH,
        )

    def target(self, way, step):
        place = where_am_i()[3]
        move = CHIPS - 1 - step if way == 0 else 1 + step
        return ring_chip((place + move) % CHIPS)

    def hop_copy(self, way, step):
        section, _, _, _, ahead, behind, _ = where_am_i()
        return pltpu.make_async_remote_copy(
            src_ref=self.pair.at[self.target(way, step), pl.ds(16 * way, 16)],
            dst_ref=self.hop.at[way, step],
            send_sem=self.send_sem.at[way, step], recv_sem=self.recv_sem.at[way, step],
            device_id=(section, ahead if way == 0 else behind), device_id_type=MESH,
        )

    def total(self, way, step, first):
        core = where_am_i()[2]
        at, rows = self.target(way, step), pl.ds(16 * way, 16)
        value = self.part[core, at, rows, :].astype(F32) + self.pair[at, rows, :].astype(F32)
        if not first:
            value += self.hop[way, step - 1].astype(F32)
        return value

    def start(self):
        self.pair_copy().start()

    def open(self):
        self.pair_copy().wait()
        for way in range(2):
            value = self.total(way, 0, True)
            self.pair[self.target(way, 0), pl.ds(16 * way, 16), :] = value.astype(BF)
            self.hop_copy(way, 0).start()

    def step(self, step):
        for way in range(2):
            self.hop_copy(way, step - 1).wait()
            value = self.total(way, step, False)
            self.pair[self.target(way, step), pl.ds(16 * way, 16), :] = value.astype(BF)
            self.hop_copy(way, step).start()

    def close(self, out):
        for way in range(2):
            self.hop_copy(way, HOPS - 1).wait()
            out[pl.ds(16 * way, 16), :] = self.total(way, HOPS, False).astype(out.dtype)


def cross_copy(src, dst, sem):
    section, me = lax.axis_index("section"), lax.axis_index("dp")
    return pltpu.make_async_remote_copy(
        src_ref=src, dst_ref=dst, send_sem=sem.at[0], recv_sem=sem.at[1],
        device_id=(1 - section, me), device_id_type=MESH,
    )


def sums_kernel(*refs):
    count = 4
    (g, gl, e), refs = refs[:3], refs[3:]
    parts = [g.at[1], g.at[0], gl, e]
    outs, refs = refs[:count], refs[count:]
    pairs, refs = refs[:count], refs[count:]
    hops, refs = refs[:count], refs[count:]
    mine, refs = refs[: count - 1], refs[count - 1 :]
    theirs, refs = refs[: count - 1], refs[count - 1 :]
    pair_sem, send_sem, recv_sem, cross_sem = refs
    greet()
    rings = [
        Ring(parts[k], pairs[k], hops[k], pair_sem.at[k], send_sem.at[k], recv_sem.at[k])
        for k in range(count)
    ]
    for ring in rings:
        ring.start()
    for ring in rings:
        ring.open()

    def hop(step, _):
        for ring in rings:
            ring.step(step)
        return 0

    lax.fori_loop(1, HOPS, hop, 0)
    crossings = []
    for k in range(count - 1):
        rings[k].close(mine[k])
        crossing = cross_copy(mine[k], theirs[k], cross_sem.at[k])
        crossing.start()
        crossings.append(crossing)
    rings[count - 1].close(outs[count - 1])
    for k in range(count - 1):
        crossings[k].wait()
        outs[k][...] = theirs[k][...]


def scatter_ring(g, gl, e):
    count = 4
    widths = [g.shape[-1], g.shape[-1], gl.shape[-1], e.shape[-1]]
    vm = pl.BlockSpec(memory_space=pltpu.VMEM)
    return pl.pallas_call(
        sums_kernel,
        in_specs=[vm] * 3,
        out_specs=[vm] * count,
        out_shape=[jax.ShapeDtypeStruct((32, n), BF) for n in widths],
        scratch_shapes=(
            [pltpu.VMEM((CHIPS, 32, n), BF) for n in widths]
            + [pltpu.VMEM((2, HOPS, 16, n), BF) for n in widths]
            + [pltpu.VMEM((32, n), BF) for n in widths[:-1]] * 2
            + [
                pltpu.SemaphoreType.DMA((count, 2)),
                pltpu.SemaphoreType.DMA((count, 2, HOPS)),
                pltpu.SemaphoreType.DMA((count, 2, HOPS)),
                pltpu.SemaphoreType.DMA((count - 1, 2)),
            ]
        ),
        compiler_params=pltpu.CompilerParams(
            collective_id=0, has_side_effects=True, vmem_limit_bytes=VMEM_LIMIT
        ),
        name="sums",
    )(g, gl, e)


def turn(rows):
    tall = jnp.concatenate([rows, jnp.zeros((96, rows.shape[1]), F32)], axis=0)
    return jnp.transpose(tall)[:, :32]


def outputs_kernel(late, early, norm, enc, qkv, out, up, down, gain, bias, bias2, enc1, enc2, book, acts):
    for d, rows in enumerate((early, late)):
        qkv[0, d] = rows[:, pl.ds(0, 1536)].astype(F32)
        out[0, d] = rows[:, pl.ds(1536, 512)].astype(F32)
        up[0, d] = rows[:, pl.ds(2048, 2048)].astype(F32)
        for j in range(4):
            down[0, d, pl.ds(32 * j, 32), :] = rows[:, pl.ds(4096 + 512 * j, 512)].astype(F32)
    turned = turn(norm[...].astype(F32))
    for d in range(2):
        gain[0, d] = norm[...].astype(F32)[:, 4 * d : 4 * d + 2]
        bias[0, pl.ds(d, 1)] = turned[4 * d + 2 : 4 * d + 3]
        bias2[0, pl.ds(d, 1)] = turned[4 * d + 3 : 4 * d + 4]
    enc2[0] = turn(enc[:, pl.ds(0, 512)].astype(F32))
    book[0] = turn(enc[:, pl.ds(512, 1024)].astype(F32))
    turned = turn(enc[:, pl.ds(1536, 128)].astype(F32))
    acts[0] = turned[:17]
    enc1[0] = turned[64:112, :8]


def spread_outputs(late, early, norm, enc):
    vm = pl.BlockSpec(memory_space=pltpu.VMEM)
    shapes = [
        (1, 2, 32, 1536), (1, 2, 32, 512), (1, 2, 32, 2048), (1, 2, 128, 512), (1, 2, 32, 2),
        (1, 2, 32), (1, 2, 32), (1, 48, 8), (1, 512, 32), (1, 1024, 32), (1, 17, 32),
    ]
    return pl.pallas_call(
        outputs_kernel,
        in_specs=[vm] * 4,
        out_specs=[vm] * len(shapes),
        out_shape=[jax.ShapeDtypeStruct(shape, F32) for shape in shapes],
        compiler_params=pltpu.CompilerParams(vmem_limit_bytes=VMEM_LIMIT),
        name="outputs",
    )(late, early, norm, enc)


def swap(array):
    return lax.ppermute(array, "section", [(0, 1), (1, 0)])


def whole_rows(g):
    return g.transpose(1, 0, 2, 3).reshape(512, g.shape[-1])


def scatter_plain(g, gl, e):
    def sums(array, axis):
        return lax.psum_scatter(array.astype(F32)[None], "dp", scatter_dimension=axis, tiled=True)

    layers = [whole_rows(g[d]) for d in range(g.shape[0])]
    qkv = jnp.stack([rows[:, :1536] for rows in layers])
    out = jnp.stack([rows[:, 1536:2048] for rows in layers])
    up = jnp.stack([rows[:, 2048:4096] for rows in layers])
    down = jnp.stack(
        [
            rows[:, 4096:].reshape(16, 32, 4, WIDTH).transpose(0, 2, 1, 3).reshape(2048, WIDTH)
            for rows in layers
        ]
    )
    norm = whole_rows(gl)[:, :8].reshape(512, 2, 4).transpose(1, 0, 2)
    enc = whole_rows(e)
    first = e.transpose(1, 0, 2, 3)[:, :, :8, 1600:1648].reshape(128, 48)
    layer_sums = [sums(x, 2) for x in (qkv, out, up, down, norm)]
    layer_sums = [swap(x) for x in layer_sums]
    norm = layer_sums.pop()
    return tuple(layer_sums) + (
        norm[..., 0:2],
        norm[..., 2],
        norm[..., 3],
        sums(first.T, 2),
        sums(enc[:, :512].T, 2),
        sums(enc[:, 512:1536].T, 2),
        sums(enc[:, 1536:1553].T, 2),
    )


def on_device(
    frames, action_ids, delta_ids, seq_len, enc_w1, enc_w2, codebook, action_table,
    ln_gain, ln_bias, w_qkv, w_out, w_up, w_down, cotangent,
):
    micro, steps = frames.shape[1], frames.shape[2]
    count = micro * steps
    frame = jnp.arange(count, dtype=I32).reshape(micro, steps, 1)
    pool_ids = POOL_AT + (frame // FRAMES_BLOCK) * 32 + frame % FRAMES_BLOCK
    ids = jnp.concatenate([pool_ids, action_ids[0][:, :, None] + ACT_AT, delta_ids[0]], axis=2)
    ids = ids.reshape(micro, steps * TPS)
    ids = jnp.pad(ids, ((0, 0), (0, 256 - steps * TPS)), constant_values=-1).reshape(512, 1)
    lnp = jnp.concatenate([ln_gain, ln_bias], axis=2).transpose(0, 2, 1)

    tok, xl, blocks, g1, g2 = enc_forward(
        frames.reshape((count,) + frames.shape[3:]), enc_w1, enc_w2, codebook, action_table, ids
    )
    act, eg, g, gl = run_layers(tok, cotangent[0], seq_len, lnp, w_qkv, w_out, w_up, w_down)
    activations = act[None]
    embed_grad = eg.reshape(micro, 256, WIDTH)[None, :, : steps * TPS]
    e = enc_backward(eg, xl, blocks, g1, g2, enc_w2, ids)
    if lax.axis_size("dp") == 2 * CHIPS:
        late, early, norm, enc = scatter_ring(g, gl, e)
        return (activations, embed_grad) + tuple(spread_outputs(late, early, norm, enc))
    return (activations, embed_grad) + scatter_plain(g, gl, e)


def solution(mesh):
    return jax.shard_map(
        on_device,
        mesh=mesh,
        in_specs=(
            P("section", "dp", None, None, None),
            P("section", "dp", None),
            P("section", "dp", None, None),
            P(None, "dp"),
            P(), P(), P(), P(), P(), P(), P(), P(), P(), P(),
            P("section", "dp", None, None),
        ),
        out_specs=(
            P("section", "dp", None, None),
            P("section", "dp", None, None),
            P("section", None, "dp", None),
            P("section", None, "dp", None),
            P("section", None, "dp", None),
            P("section", None, "dp", None),
            P("section", None, "dp", None),
            P("section", None, "dp"),
            P("section", None, "dp"),
            P("section", None, "dp"),
            P("section", None, "dp"),
            P("section", None, "dp"),
            P("section", None, "dp"),
        ),
        check_vma=False,
    )
```

```python
import functools

import jax
import jax.numpy as jnp
from jax import lax
from jax.experimental import pallas as pl
from jax.experimental.pallas import tpu as pltpu
from jax.sharding import PartitionSpec as P

HEADS = 8
HEAD_DIM = 64
TPS = 6
EPS = 1e-05
BF = jnp.bfloat16
F32 = jnp.float32
I32 = jnp.int32

WIDTH = 512
CODES = 1024
FRAMES_BLOCK = 28
BLOCK_ROWS = FRAMES_BLOCK * 8
TABLE = 1152
POOL_AT = 1056
ACT_AT = 1024
LAYER_COLS = 6144
ENC_COLS = 1664
VMEM_LIMIT = 60 << 20
TRAIN_VMEM = 63 << 20


def dot(a, b):
    return jnp.dot(a, b, preferred_element_type=F32)


def dot_rows(a, b):
    return lax.dot_general(a, b, (((0,), (0,)), ((), ())), preferred_element_type=F32)


def dot_lanes(a, b):
    return lax.dot_general(a, b, (((1,), (1,)), ((), ())), preferred_element_type=F32)


def iota(shape, axis):
    return lax.broadcasted_iota(I32, shape, axis)


def gelu_pair(v):
    e = jnp.exp2(v * v * (-0.5 * 1.4426950408889634))
    t = 1.0 / (1.0 + 0.23164190 * jnp.abs(v))
    poly = 0.5 * 1.061405429
    poly = poly * t + 0.5 * -1.453152027
    poly = poly * t + 0.5 * 1.421413741
    poly = poly * t + 0.5 * -0.284496736
    poly = poly * t + 0.5 * 0.254829592
    tail = poly * t * e
    cdf = jnp.where(v >= 0, 1.0 - tail, tail)
    return v * cdf, cdf + v * e * 0.3989422804014327


def patch_index(rows):
    k = iota((rows, 48), 0)
    dy = (k * 2731) >> 16
    rest = k - dy * 24
    j = jnp.where(rest >= 12, rest - 12, rest)
    return jnp.where((iota((rows, 48), 1) == dy * 12 + j) & (k < 96), 1.0, 0.0), rest


def encoder_weights(w1):
    hot, rest = patch_index(128)
    wide = dot(hot.astype(BF), w1)
    first = jnp.where(rest[:, :1] < 12, wide, 0.0)
    second = jnp.where(rest[:, :1] >= 12, wide, 0.0)
    block = jnp.concatenate([first, second], axis=1)
    zero = jnp.zeros_like(block)
    return jnp.concatenate(
        [jnp.concatenate([block, zero], axis=1), jnp.concatenate([zero, block], axis=1)], axis=0
    ).astype(BF)


def enc_fwd_kernel(
    frames, w1, w2, book, acts, ids, tok, xl, blocks, g1, g2, perm, lanes, big, xs, acc, table
):
    step = pl.program_id(0)

    @pl.when(step == 0)
    def _():
        a, b = iota((256, 256), 0), iota((256, 256), 1)
        perm[...] = jnp.where(b == 8 * (a & 31) + (a >> 5), 1.0, 0.0).astype(BF)
        src = iota((192, 1024), 0)
        px = (src * 5462) >> 16
        at = (px >> 1) * 128 + (px & 1) * 12 + (src - px * 12)
        out = iota((192, 1024), 1)
        for dy in range(4):
            lanes[dy] = jnp.where(out == at + dy * 24, 1.0, 0.0).astype(BF)
        big[...] = encoder_weights(w1[...])
        table[pl.ds(0, CODES), :] = book[...]
        named = acts[...].astype(F32)
        pad = jnp.zeros((TABLE - ACT_AT - named.shape[0], WIDTH), F32)
        table[pl.ds(ACT_AT, TABLE - ACT_AT), :] = jnp.concatenate([named, pad], axis=0).astype(BF)

    for group in range(FRAMES_BLOCK // 4):
        rows = frames[pl.ds(group * 4, 4)].reshape(256, 192)
        moved = dot(perm[...], rows).astype(BF).reshape(8, 32, 192)
        xs[:, pl.ds(group * 32, 32), :] = moved
    for dy2 in range(2):
        spread = dot(xs[dy2 * 4], lanes[0])
        for dy in range(1, 4):
            spread += dot(xs[dy2 * 4 + dy], lanes[dy])
        spread = spread.astype(BF)
        for bx in range(8):
            xl[0, pl.ds(bx * BLOCK_ROWS, BLOCK_ROWS), pl.ds(dy2 * 128, 128)] = spread[
                :, bx * 128 : (bx + 1) * 128
            ]
    acc[...] = jnp.zeros_like(acc)

    def part(bx, _):
        rows = pl.ds(pl.multiple_of(bx * BLOCK_ROWS, BLOCK_ROWS), BLOCK_ROWS)
        value, slope = gelu_pair(dot(xl[0, rows, :], big[...]))
        value = value.astype(BF)
        blocks[0, rows, :] = value
        g1[0, rows, :] = slope.astype(BF)
        value, slope = gelu_pair(dot(value, w2[...]))
        g2[0, rows, :] = slope.astype(BF)
        acc[...] += value
        return 0

    lax.fori_loop(0, 8, part, 0)
    pooled = jnp.sum(acc[...].reshape(FRAMES_BLOCK, 8, WIDTH), axis=1) * (1.0 / 64.0)
    pooled = jnp.concatenate([pooled, jnp.zeros((32 - FRAMES_BLOCK, WIDTH), F32)], axis=0)
    table[pl.ds(pl.multiple_of(POOL_AT + step * 32, 32), 32), :] = pooled.astype(BF)

    @pl.when(step == pl.num_programs(0) - 1)
    def _():
        for part_at in range(2):
            rows = pl.ds(part_at * 256, 256)
            hot = jnp.where(iota((256, TABLE), 1) == ids[rows, :], 1.0, 0.0).astype(BF)
            tok[rows, :] = dot(hot, table[...]).astype(BF)


def enc_forward(frames, w1, w2, book, acts, ids):
    count = frames.shape[0]
    grid = count // FRAMES_BLOCK
    rows = 8 * BLOCK_ROWS

    def whole(shape):
        return pl.BlockSpec(shape, lambda i: (0,) * len(shape))

    def saved(lanes):
        return pl.BlockSpec((1, rows, lanes), lambda i: (i, 0, 0))

    return pl.pallas_call(
        enc_fwd_kernel,
        grid=(grid,),
        in_specs=[
            pl.BlockSpec((FRAMES_BLOCK, 64, 192), lambda i: (i, 0, 0)),
            whole(w1.shape),
            whole(w2.shape),
            whole(book.shape),
            whole(acts.shape),
            whole(ids.shape),
        ],
        out_specs=[whole((512, WIDTH)), saved(256), saved(512), saved(512), saved(512)],
        out_shape=[
            jax.ShapeDtypeStruct((512, WIDTH), BF),
            jax.ShapeDtypeStruct((grid, rows, 256), BF),
            jax.ShapeDtypeStruct((grid, rows, 512), BF),
            jax.ShapeDtypeStruct((grid, rows, 512), BF),
            jax.ShapeDtypeStruct((grid, rows, 512), BF),
        ],
        scratch_shapes=[
            pltpu.VMEM((256, 256), BF),
            pltpu.VMEM((4, 192, 1024), BF),
            pltpu.VMEM((256, 512), BF),
            pltpu.VMEM((8, BLOCK_ROWS, 192), BF),
            pltpu.VMEM((BLOCK_ROWS, WIDTH), F32),
            pltpu.VMEM((TABLE, WIDTH), BF),
        ],
        compiler_params=pltpu.CompilerParams(vmem_limit_bytes=VMEM_LIMIT),
        name="enc_fwd",
    )(frames, w1, w2, book, acts, ids)


def ln_parts(x):
    mean = jnp.mean(x, axis=-1, keepdims=True)
    center = x - mean
    var = jnp.mean(center * center, axis=-1, keepdims=True)
    scale = lax.rsqrt(var + EPS)
    return center * scale, scale


def ln_back(x, d, gain):
    hat, scale = ln_parts(x)
    dh = d * gain
    one = jnp.mean(dh, axis=-1, keepdims=True)
    two = jnp.mean(dh * hat, axis=-1, keepdims=True)
    back = scale * (dh - one - hat * two)
    return back, jnp.sum(d * hat, axis=0, keepdims=True), jnp.sum(d, axis=0, keepdims=True)


def head_mask(h):
    lane = iota((1, 256), 1) >> 6
    return lane == h


def stacked(rows, scale):
    out = []
    for h in range(4):
        mask = jnp.where(head_mask(h), scale, 0.0).astype(BF)
        out.append(rows * mask)
    return jnp.concatenate(out, axis=0)


def unstacked(rows):
    out = rows[768:]
    for h in range(3):
        out = jnp.where(head_mask(h), rows[h * 256 : (h + 1) * 256], out)
    return out


def scatter_rows(g, d, cols, value, dests=16):
    shaped = value.astype(BF).reshape(dests // 2, 2, 32, value.shape[1])
    for core in range(2):
        g[d, core, :, :, cols] = shaped[:, core]


def layers_kernel(
    tok, cot_h, lens, lnp, wq_h, wo_h, wu_h, wd_h,
    act, eg, g, gl,
    wq, wo, wu, wd, stream, normed, packed, probs, att, normed2, gated, slope, bias,
    up, back_up, back_att, back_packed, lng, cot, mine, theirs, sems, cross_sem,
):
    layers = wq.shape[0]
    section = lax.axis_index("section")
    barrier = pltpu.get_barrier_semaphore()
    pl.semaphore_signal(
        barrier, inc=1, device_id=(1 - section, lax.axis_index("dp")), device_id_type=MESH
    )
    pl.semaphore_wait(barrier, 1)
    cot_copy = cross_copy(cot_h, cot, cross_sem.at[0])
    cot_copy.start()
    act_copy = cross_copy(mine, theirs, cross_sem.at[1])
    copies = []
    for d in range(layers):
        for k, (src, dst) in enumerate(((wq_h, wq), (wo_h, wo), (wu_h, wu), (wd_h, wd))):
            copy = pltpu.make_async_copy(src.at[d], dst.at[d], sems.at[d, k])
            copy.start()
            copies.append(copy)

    stream[0, 0] = tok[...].astype(F32)
    row = iota((256, 1), 0)
    col = iota((1, 256), 1)
    q_step = ((row * 10923) >> 16).astype(F32)
    k_step = ((col * 10923) >> 16).astype(F32)
    for s in range(2):
        inv = 1.0 / lens[section, s].astype(F32)
        q_seq = jnp.floor((q_step + 0.5) * inv)
        k_seq = jnp.floor((k_step + 0.5) * inv)
        bias[s] = jnp.where((k_step <= q_step) & (q_seq == k_seq), 0.0, -1e30)
    for copy in copies:
        copy.wait()

    def forward(d, _):
        x = stream[d, 0]
        hat, _ = ln_parts(x)
        normed[d] = (hat * lnp[d, 0:1] + lnp[d, 2:3]).astype(BF)
        for c in range(3):
            cols = pl.ds(c * 512, 512)
            packed[d, :, cols] = dot(normed[d], wq[d, :, cols]).astype(BF)
        for s in range(2):
            rows = pl.ds(s * 256, 256)
            for quad in range(2):
                q = stacked(packed[d, rows, pl.ds(quad * 256, 256)], HEAD_DIM**-0.5)
                k = packed[d, rows, pl.ds(512 + quad * 256, 256)]
                v = packed[d, rows, pl.ds(1024 + quad * 256, 256)]
                scores = dot_lanes(q, k).reshape(4, 256, 256) + bias[s][None]
                top = jnp.max(scores, axis=-1, keepdims=True)
                e = jnp.exp(scores - top)
                total = jnp.sum(e, axis=-1, keepdims=True)
                p = (e * (1.0 / total)).astype(BF).reshape(1024, 256)
                probs[d, s * 2 + quad] = p
                att[d, rows, pl.ds(quad * 256, 256)] = unstacked(dot(p, v)).astype(BF)
        middle = stream[d, 0] + dot(att[d], wo[d])
        stream[d, 1] = middle
        hat, _ = ln_parts(middle)
        normed2[d] = (hat * lnp[d, 1:2] + lnp[d, 3:4]).astype(BF)

        def chunk(c, _):
            cols = pl.ds(pl.multiple_of(c * 512, 512), 512)
            value, grad = gelu_pair(dot(normed2[d], wu[d, :, cols]))
            gated[d, :, cols] = value.astype(BF)
            slope[d, :, cols] = grad.astype(BF)
            return 0

        lax.fori_loop(0, 4, chunk, 0)
        stream[d + 1, 0] = stream[d, 1] + dot(gated[d], wd[d])
        return 0

    lax.fori_loop(0, layers, forward, 0)
    cot_copy.wait()
    mine[...] = stream[layers, 0].astype(BF)
    act_copy.start()
    for s in range(2):
        up[pl.ds(s * 256, 252), :] = cot[s].astype(F32)
        up[pl.ds(s * 256 + 252, 4), :] = jnp.zeros((4, WIDTH), F32)
    lng[...] = jnp.zeros_like(lng)

    def backward(i, _):
        d = layers - 1 - i
        down = up[...].astype(BF)

        def chunk(c, _):
            cols = pl.ds(pl.multiple_of(c * 256, 256), 256)
            part = dot_rows(gated[d, :, cols], down).astype(BF).reshape(2, 4, 32, WIDTH)
            for core in range(2):
                for j in range(4):
                    g[d, core, c, :, pl.ds(4096 + 512 * j, 512)] = part[core, j]
            back = dot_lanes(down, wd[d, cols, :])
            back = (back * slope[d, :, cols].astype(F32)).astype(BF)
            back_up[:, cols] = back
            part = dot_rows(normed2[d], back).astype(BF).reshape(8, 2, 32, 256)
            out = pl.ds(pl.multiple_of(2048 + c * 256, 256), 256)
            for core in range(2):
                g[d, core, :, :, out] = part[:, core]
            return 0

        lax.fori_loop(0, 8, chunk, 0)
        back, gain, shift = ln_back(stream[d, 1], dot_lanes(back_up[...], wu[d]), lnp[d, 1:2])
        lng[pl.ds(d * 4 + 1, 1), :] = gain
        lng[pl.ds(d * 4 + 3, 1), :] = shift
        up[...] += back
        branch = up[...].astype(BF)
        scatter_rows(g, d, pl.ds(1536, 512), dot_rows(att[d], branch))
        back_att[...] = dot_lanes(branch, wo[d]).astype(BF)
        for s in range(2):
            rows = pl.ds(s * 256, 256)
            for quad in range(2):
                lanes = pl.ds(quad * 256, 256)
                qs = stacked(packed[d, rows, lanes], HEAD_DIM**-0.5)
                k = packed[d, rows, pl.ds(512 + quad * 256, 256)]
                v = packed[d, rows, pl.ds(1024 + quad * 256, 256)]
                outs = stacked(back_att[rows, lanes], 1.0)
                p = probs[d, s * 2 + quad]
                dp = dot_lanes(outs, v)
                pf = p.astype(F32)
                weighted = pf * dp
                total = jnp.sum(weighted, axis=-1, keepdims=True)
                ds = (weighted - pf * total).astype(BF)
                back_packed[rows, lanes] = (unstacked(dot(ds, k)) * HEAD_DIM**-0.5).astype(BF)
                back_packed[rows, pl.ds(512 + quad * 256, 256)] = dot_rows(ds, qs).astype(BF)
                back_packed[rows, pl.ds(1024 + quad * 256, 256)] = dot_rows(p, outs).astype(BF)
        for c in range(3):
            cols = pl.ds(c * 512, 512)
            scatter_rows(g, d, cols, dot_rows(normed[d], back_packed[:, cols]))
        back, gain, shift = ln_back(stream[d, 0], dot_lanes(back_packed[...], wq[d]), lnp[d, 0:1])
        lng[pl.ds(d * 4, 1), :] = gain
        lng[pl.ds(d * 4 + 2, 1), :] = shift
        up[...] += back
        return 0

    lax.fori_loop(0, layers, backward, 0)
    eg[...] = up[...].astype(BF)
    act_copy.wait()
    for s in range(2):
        act[s] = theirs[pl.ds(s * 256, 256), :].astype(F32)[:252].astype(BF)
    turned = jnp.transpose(lng[...]).astype(BF).reshape(8, 2, 32, 128)
    for core in range(2):
        gl[core] = turned[:, core]


def run_layers(tok, cot, lens, lnp, wq, wo, wu, wd):
    layers = wq.shape[0]
    vm = pl.BlockSpec(memory_space=pltpu.VMEM)
    sm = pl.BlockSpec(memory_space=pltpu.SMEM)
    hb = pl.BlockSpec(memory_space=pl.ANY)
    rows = 512
    return pl.pallas_call(
        layers_kernel,
        in_specs=[vm, hb, sm, vm, hb, hb, hb, hb],
        out_specs=[vm, vm, vm, vm],
        out_shape=[
            jax.ShapeDtypeStruct((2, 252, WIDTH), BF),
            jax.ShapeDtypeStruct((rows, WIDTH), BF),
            jax.ShapeDtypeStruct((layers, 2, 8, 32, LAYER_COLS), BF),
            jax.ShapeDtypeStruct((2, 8, 32, 128), BF),
        ],
        scratch_shapes=[
            pltpu.VMEM(wq.shape, BF),
            pltpu.VMEM(wo.shape, BF),
            pltpu.VMEM(wu.shape, BF),
            pltpu.VMEM(wd.shape, BF),
            pltpu.VMEM((layers + 1, 2, rows, WIDTH), F32),
            pltpu.VMEM((layers, rows, WIDTH), BF),
            pltpu.VMEM((layers, rows, 3 * WIDTH), BF),
            pltpu.VMEM((layers, 4, 1024, 256), BF),
            pltpu.VMEM((layers, rows, WIDTH), BF),
            pltpu.VMEM((layers, rows, WIDTH), BF),
            pltpu.VMEM((layers, rows, 4 * WIDTH), BF),
            pltpu.VMEM((layers, rows, 4 * WIDTH), BF),
            pltpu.VMEM((2, 256, 256), F32),
            pltpu.VMEM((rows, WIDTH), F32),
            pltpu.VMEM((rows, 4 * WIDTH), BF),
            pltpu.VMEM((rows, WIDTH), BF),
            pltpu.VMEM((rows, 3 * WIDTH), BF),
            pltpu.VMEM((128, WIDTH), F32),
            pltpu.VMEM(cot.shape, BF),
            pltpu.VMEM((rows, WIDTH), BF),
            pltpu.VMEM((rows, WIDTH), BF),
            pltpu.SemaphoreType.DMA((layers, 4)),
            pltpu.SemaphoreType.DMA((2, 2)),
        ],
        compiler_params=pltpu.CompilerParams(
            collective_id=1, has_side_effects=True, vmem_limit_bytes=VMEM_LIMIT
        ),
        name="layers",
    )(tok, cot, lens, lnp, wq, wo, wu, wd)


def enc_bwd_kernel(eg, xl, blocks, g1, g2, w2, ids, e, dpool, bs, bf, acc2, acc1):
    step = pl.program_id(0)

    @pl.when(step == 0)
    def _():
        hot = jnp.where(iota((512, TABLE), 1) == ids[...], 1.0, 0.0).astype(BF)
        code = dot_rows(eg[...], hot[:, :POOL_AT + 96]).astype(BF)
        dpool[...] = dot_rows(hot[:, POOL_AT : POOL_AT + 96], eg[...])
        parts = code[:, :CODES].reshape(8, 2, 32, CODES)
        tail = code[:, CODES : CODES + 128].reshape(8, 2, 32, 128)
        for core in range(2):
            e[core, :, :, pl.ds(512, CODES)] = parts[:, core]
            e[core, :, :, pl.ds(1536, 128)] = tail[:, core]
        acc2[...] = jnp.zeros_like(acc2)
        acc1[...] = jnp.zeros_like(acc1)

    pooled = dpool[pl.ds(pl.multiple_of(step * 32, 32), 32), :][:FRAMES_BLOCK] * (1.0 / 64.0)
    wide = jnp.broadcast_to(pooled[:, None, :], (FRAMES_BLOCK, 8, WIDTH)).reshape(BLOCK_ROWS, WIDTH)

    def part(bx, _):
        rows = pl.ds(pl.multiple_of(bx * BLOCK_ROWS, BLOCK_ROWS), BLOCK_ROWS)
        back = (wide * g2[0, rows, :].astype(F32)).astype(BF)
        bs[rows, :] = back
        bf[rows, :] = (dot_lanes(back, w2[...]) * g1[0, rows, :].astype(F32)).astype(BF)
        return 0

    lax.fori_loop(0, 8, part, 0)
    acc2[...] += dot_rows(bs[...], blocks[0])
    for dy2 in range(2):
        acc1[:, pl.ds(dy2 * 256, 256)] += dot_rows(
            xl[0, :, pl.ds(dy2 * 128, 128)], bf[:, pl.ds(dy2 * 256, 256)]
        )

    @pl.when(step == pl.num_programs(0) - 1)
    def _():
        parts = acc2[...].astype(BF).reshape(8, 2, 32, WIDTH)
        both = acc1[:, pl.ds(0, 256)] + acc1[:, pl.ds(256, 256)]
        hot, rest = patch_index(128)
        first = jnp.where(rest[:, :1] < 12, both[:, :128], both[:, 128:])
        first = lax.dot_general(
            first, hot, (((0,), (0,)), ((), ())), preferred_element_type=F32,
            precision=lax.Precision.HIGHEST,
        )
        first = first.reshape(8, 2, 8, 48)
        first = jnp.concatenate([first, jnp.zeros((8, 2, 24, 48), F32)], axis=2).astype(BF)
        for core in range(2):
            e[core, :, :, pl.ds(0, WIDTH)] = parts[:, core]
            e[core, :, :, pl.ds(1536 + 64, 48)] = first[:, core]


def enc_backward(eg, xl, blocks, g1, g2, w2, ids):
    grid, rows, _ = xl.shape

    def whole(shape):
        return pl.BlockSpec(shape, lambda i: (0,) * len(shape))

    def saved(lanes):
        return pl.BlockSpec((1, rows, lanes), lambda i: (i, 0, 0))

    return pl.pallas_call(
        enc_bwd_kernel,
        grid=(grid,),
        in_specs=[
            whole(eg.shape), saved(256), saved(512), saved(512), saved(512),
            whole(w2.shape), whole(ids.shape),
        ],
        out_specs=whole((2, 8, 32, ENC_COLS)),
        out_shape=jax.ShapeDtypeStruct((2, 8, 32, ENC_COLS), BF),
        scratch_shapes=[
            pltpu.VMEM((96, WIDTH), F32),
            pltpu.VMEM((rows, WIDTH), BF),
            pltpu.VMEM((rows, WIDTH), BF),
            pltpu.VMEM((WIDTH, WIDTH), F32),
            pltpu.VMEM((128, WIDTH), F32),
        ],
        compiler_params=pltpu.CompilerParams(vmem_limit_bytes=VMEM_LIMIT),
        name="enc_bwd",
    )(eg, xl, blocks, g1, g2, w2, ids)


CHIPS = 8
HOPS = CHIPS - 1
MESH = pl.DeviceIdType.MESH


def ring_place(chip):
    z, x = chip // 2, chip % 2
    return z * (1 - x) + (7 - z) * x


def ring_chip(place):
    half = place // 4
    return (1 - half) * (2 * place) + half * (15 - 2 * place)


def where_am_i():
    section, me = lax.axis_index("section"), lax.axis_index("dp")
    core, chip = me % 2, me // 2
    place = ring_place(chip)
    ahead = ring_chip((place + 1) % CHIPS) * 2 + core
    behind = ring_chip((place + CHIPS - 1) % CHIPS) * 2 + core
    sibling = chip * 2 + (1 - core)
    return section, me, core, place, ahead, behind, sibling


def greet():
    section, me, _, _, ahead, behind, sibling = where_am_i()
    barrier = pltpu.get_barrier_semaphore()
    for target in ((section, sibling), (section, ahead), (section, behind), (1 - section, me)):
        pl.semaphore_signal(barrier, inc=1, device_id=target, device_id_type=MESH)
    pl.semaphore_wait(barrier, 4)


def cross_copy(src, dst, sem):
    section, me = lax.axis_index("section"), lax.axis_index("dp")
    return pltpu.make_async_remote_copy(
        src_ref=src, dst_ref=dst, send_sem=sem.at[0], recv_sem=sem.at[1],
        device_id=(1 - section, me), device_id_type=MESH,
    )


def turn(rows):
    tall = jnp.concatenate([rows, jnp.zeros((96, rows.shape[1]), F32)], axis=0)
    return jnp.transpose(tall)[:, :32]


ACT_NORMED, ACT_Q, ACT_PROBS, ACT_ATT, ACT_NORMED2, ACT_GATED, ACT_SLOPE = 0, 1, 4, 8, 9, 10, 14
ACT_PANELS = 18
W_QKV, W_OUT, W_UP, W_DOWN = 0, 3, 4, 8
W_PANELS = 12


def panel(ref, d, p):
    return ref[d, pl.ds(2 * p, 2)].reshape(512, WIDTH)


def put_panel(ref, d, p, value):
    ref[d, pl.ds(2 * p, 2)] = value.astype(BF).reshape(2, 8, 32, WIDTH)


def quarter(ref, d, p, s, quad):
    return ref[d, 2 * p + s, :, :, pl.ds(256 * quad, 256)].reshape(256, 256)


def put_quarter(ref, d, p, s, quad, value):
    ref[d, 2 * p + s, :, :, pl.ds(256 * quad, 256)] = value.astype(BF).reshape(8, 32, 256)


def side_by_side(ref, d, p, count):
    return jnp.concatenate([panel(ref, d, p + c) for c in range(count)], axis=1)


class Piece:
    def __init__(self, own, pair, hop, mine, sems):
        self.own, self.pair, self.hop, self.mine = own, pair, hop, mine
        self.pair_sem, self.send_sem, self.recv_sem = sems

    def pair_copy(self):
        section, _, core, _, _, _, sibling = where_am_i()
        return pltpu.make_async_remote_copy(
            src_ref=self.own(1 - core), dst_ref=self.pair,
            send_sem=self.pair_sem.at[0], recv_sem=self.pair_sem.at[1],
            device_id=(section, sibling), device_id_type=MESH,
        )

    def target(self, way, step):
        place = where_am_i()[3]
        move = CHIPS - 1 - step if way == 0 else 1 + step
        return ring_chip((place + move) % CHIPS)

    def hop_copy(self, way, step):
        section, _, _, _, ahead, behind, _ = where_am_i()
        return pltpu.make_async_remote_copy(
            src_ref=self.pair.at[:, self.target(way, step), pl.ds(16 * way, 16), :],
            dst_ref=self.hop(way, step),
            send_sem=self.send_sem.at[way, step], recv_sem=self.recv_sem.at[way, step],
            device_id=(section, ahead if way == 0 else behind), device_id_type=MESH,
        )

    def total(self, way, step):
        core = where_am_i()[2]
        at, rows = self.target(way, step), pl.ds(16 * way, 16)
        value = self.own(core)[:, at, rows, :].astype(F32) + self.pair[:, at, rows, :].astype(F32)
        if step:
            value += self.hop(way, step - 1)[...].astype(F32)
        return value

    def send(self, step):
        for way in range(2):
            if step:
                self.hop_copy(way, step - 1).wait()
            at = self.target(way, step)
            self.pair[:, at, pl.ds(16 * way, 16), :] = self.total(way, step).astype(BF)
            self.hop_copy(way, step).start()

    def close(self):
        for way in range(2):
            self.hop_copy(way, HOPS - 1).wait()
            value = self.total(way, HOPS)
            self.mine[:, pl.ds(16 * way, 16), :] = value.astype(self.mine.dtype)


class Stream:
    def __init__(self, pieces, crossings):
        self.pieces, self.crossings = pieces, crossings

    def pair(self):
        for piece in self.pieces:
            piece.pair_copy().start()

    def open(self):
        for piece in self.pieces:
            piece.pair_copy().wait()
            piece.send(0)

    def send(self, step):
        for piece in self.pieces:
            piece.send(step)

    def close(self):
        for piece in self.pieces:
            piece.close()
        for crossing in self.crossings:
            cross_copy(*crossing).start()


class Traffic:
    def __init__(self):
        self.queue = []

    def open(self, stream):
        stream.open()
        self.queue.append((stream, 1))

    def tick(self, count=1):
        for _ in range(count):
            if not self.queue:
                return
            stream, step = self.queue.pop(0)
            if step < HOPS:
                stream.send(step)
                self.queue.append((stream, step + 1))
            else:
                stream.close()

    def finish(self):
        while self.queue:
            self.tick()


def train_kernel(
    tok, cot_h, lens, lnp, wq_h, wo_h, wu_h, wd_h, xl_h, bl_h, g1_h, g2_h, w2, ids,
    act, eg, late, early, norm, enc, misc,
    wts, acts, g1st, pair1, hop1, xin, mid, bias, back_att, lng, cot, act_mine, act_theirs,
    mine1, theirs1, mine0, theirs0, lnown, lnpair, lnhop, lnmine, lntheirs,
    genc, enc_mine, miscown, miscpair, mischop, miscmine, acc2, acc1, dpool,
    load_sem, stream_sem, cross_sem, pair_sem, send_sem, recv_sem, free_sem,
):
    section, me, core, _, ahead, behind, sibling = where_am_i()
    greet()
    cot_copy = cross_copy(cot_h, cot, cross_sem.at[0])
    cot_copy.start()
    act_copy = cross_copy(act_mine, act_theirs, cross_sem.at[1])
    loads = []
    for d in range(2):
        for c in range(W_PANELS):
            if c < 3:
                src = wq_h.at[d, :, :, :, pl.ds(512 * c, 512)]
            elif c == 3:
                src = wo_h.at[d]
            elif c < 8:
                src = wu_h.at[d, :, :, :, pl.ds(512 * (c - 4), 512)]
            else:
                src = wd_h.at[d, pl.ds(2 * (c - 8), 2)]
            loads.append(pltpu.make_async_copy(src, wts.at[d, pl.ds(2 * c, 2)], load_sem.at[d, c]))
            loads[-1].start()

    xin[0] = tok[...].astype(F32)
    row, col = iota((256, 1), 0), iota((1, 256), 1)
    q_step = ((row * 10923) >> 16).astype(F32)
    k_step = ((col * 10923) >> 16).astype(F32)
    for s in range(2):
        inv = 1.0 / lens[section, s].astype(F32)
        q_seq = jnp.floor((q_step + 0.5) * inv)
        k_seq = jnp.floor((k_step + 0.5) * inv)
        bias[s] = jnp.where((k_step <= q_step) & (q_seq == k_seq), 0.0, -1e30)
    for load in loads:
        load.wait()

    def forward(d, _):
        hat, _ = ln_parts(xin[d])
        normed = (hat * lnp[d, 0:1] + lnp[d, 2:3]).astype(BF)
        put_panel(acts, d, ACT_NORMED, normed)
        for c in range(3):
            put_panel(acts, d, ACT_Q + c, dot(normed, panel(wts, d, W_QKV + c)))
        for s in range(2):
            for quad in range(2):
                q = stacked(quarter(acts, d, ACT_Q, s, quad), HEAD_DIM**-0.5)
                k = quarter(acts, d, ACT_Q + 1, s, quad)
                v = quarter(acts, d, ACT_Q + 2, s, quad)
                scores = dot_lanes(q, k).reshape(4, 256, 256) + bias[s][None]
                top = jnp.max(scores, axis=-1, keepdims=True)
                e = jnp.exp(scores - top)
                total = jnp.sum(e, axis=-1, keepdims=True)
                p = (e * (1.0 / total)).astype(BF)
                for h in range(4):
                    put_quarter(acts, d, ACT_PROBS + s * 2 + quad, h // 2, h % 2, p[h])
                out = unstacked(dot(p.reshape(1024, 256), v))
                put_quarter(acts, d, ACT_ATT, s, quad, out)
        middle = xin[d] + dot(panel(acts, d, ACT_ATT), panel(wts, d, W_OUT))
        mid[d] = middle
        hat, _ = ln_parts(middle)
        put_panel(acts, d, ACT_NORMED2, hat * lnp[d, 1:2] + lnp[d, 3:4])

        def chunk(c, _):
            value, grad = gelu_pair(dot(panel(acts, d, ACT_NORMED2), panel(wts, d, W_UP + c)))
            put_panel(acts, d, ACT_GATED + c, value)
            put_panel(acts, d, ACT_SLOPE + c, grad)
            return 0

        lax.fori_loop(0, 4, chunk, 0)
        down = wts[d, pl.ds(2 * W_DOWN, 8)].reshape(4 * WIDTH, WIDTH)
        xin[d + 1] = mid[d] + dot(side_by_side(acts, d, ACT_GATED, 4), down)
        return 0

    lax.fori_loop(0, 2, forward, 0)
    act_mine[...] = xin[2].astype(BF)
    cot_copy.wait()
    act_copy.start()
    up = xin.at[2]
    for s in range(2):
        up[pl.ds(s * 256, 252), :] = cot[s].astype(F32)
        up[pl.ds(s * 256 + 252, 4), :] = jnp.zeros((4, WIDTH), F32)
    lng[...] = jnp.zeros_like(lng)

    def sems(k):
        return pair_sem.at[k], send_sem.at[k], recv_sem.at[k]

    def piece1(k, first, hop_at):
        return Piece(
            lambda c: g1st.at[pl.ds(c * 12 + first, 4)],
            pair1.at[pl.ds(first, 4)],
            lambda way, step: hop1.at[
                hop_at(step)[0], pl.ds(hop_at(step)[1], 4), pl.ds(16 * way, 16), :
            ],
            mine1.at[pl.ds(first, 4)], sems(k),
        )

    def piece0(k, first, hop_at):
        return Piece(
            lambda c: acts.at[1, pl.ds(c * 12 + first, 4)],
            acts.at[1, pl.ds(24 + first, 4)],
            lambda way, step: wts.at[
                1, hop_at(step)[0], pl.ds(hop_at(step)[1], 4), pl.ds(16 * way, 16), :
            ],
            mine0.at[pl.ds(first, 4)], sems(k),
        )

    def crossing(mine, theirs, first, k):
        return mine.at[pl.ds(first, 4)], theirs.at[pl.ds(first, 4)], cross_sem.at[k]

    def down_at(step):
        return step, 0

    def up_at(step):
        return step, 4

    def att_at(step):
        return HOPS + step // 2, 4 * (step % 2)

    down1 = Stream([piece1(0, W_DOWN, down_at)], [crossing(mine1, theirs1, W_DOWN, 2)])
    up1 = Stream([piece1(1, W_UP, up_at)], [crossing(mine1, theirs1, W_UP, 3)])
    att1 = Stream([piece1(2, 0, att_at)], [crossing(mine1, theirs1, 0, 4)])
    down0 = Stream([piece0(3, W_DOWN, down_at)], [crossing(mine0, theirs0, W_DOWN, 5)])
    up0 = Stream([piece0(4, W_UP, up_at)], [crossing(mine0, theirs0, W_UP, 6)])
    norms = Piece(
        lambda c: lnown.at[c], lnpair, lambda way, step: lnhop.at[way, step], lnmine, sems(5)
    )
    att0 = Stream(
        [piece0(6, 0, att_at), norms],
        [crossing(mine0, theirs0, 0, 7), (lnmine, lntheirs, cross_sem.at[8])],
    )
    encoder = Stream(
        [
            Piece(
                lambda c: genc.at[c], wts.at[1, pl.ds(21, 3)],
                lambda way, step: wts.at[1, 14 + step, pl.ds(0, 3), pl.ds(16 * way, 16), :],
                enc_mine, sems(7),
            ),
            Piece(
                lambda c: miscown.at[c], miscpair, lambda way, step: mischop.at[way, step],
                miscmine, sems(8),
            ),
        ],
        [],
    )
    traffic = Traffic()

    def backward(d, put, put_down, streams, before, ticks):
        down = up[...].astype(BF)
        for c in range(4):
            part = dot_rows(panel(acts, d, ACT_GATED + c), down).astype(BF).reshape(4, 4, 32, WIDTH)
            put_down(c, part)
            traffic.tick(ticks[0])
        before()
        streams[0].pair()
        for c in range(4):
            back = dot_lanes(down, panel(wts, d, W_DOWN + c))
            back = (back * panel(acts, d, ACT_SLOPE + c).astype(F32)).astype(BF)
            put_panel(acts, d, ACT_SLOPE + c, back)
            put(W_UP + c, dot_rows(panel(acts, d, ACT_NORMED2), back))
            traffic.tick(ticks[1])
        streams[1].pair()
        traffic.open(streams[0])
        back = dot_lanes(side_by_side(acts, d, ACT_SLOPE, 4), side_by_side(wts, d, W_UP, 4))
        back, gain, shift = ln_back(mid[d], back, lnp[d, 1:2])
        lng[pl.ds(d * 4 + 1, 1), :] = gain
        lng[pl.ds(d * 4 + 3, 1), :] = shift
        up[...] += back
        branch = up[...].astype(BF)
        put(W_OUT, dot_rows(panel(acts, d, ACT_ATT), branch))
        back_att[...] = dot_lanes(branch, panel(wts, d, W_OUT)).astype(BF)
        traffic.open(streams[1])
        for s in range(2):
            for quad in range(2):
                rows, lanes = pl.ds(s * 256, 256), pl.ds(quad * 256, 256)
                qs = stacked(quarter(acts, d, ACT_Q, s, quad), HEAD_DIM**-0.5)
                k = quarter(acts, d, ACT_Q + 1, s, quad)
                v = quarter(acts, d, ACT_Q + 2, s, quad)
                outs = stacked(back_att[rows, lanes], 1.0)
                at = ACT_PROBS + s * 2 + quad
                p = jnp.concatenate([quarter(acts, d, at, h // 2, h % 2) for h in range(4)], axis=0)
                dp = dot_lanes(outs, v)
                pf = p.astype(F32)
                weighted = pf * dp
                total = jnp.sum(weighted, axis=-1, keepdims=True)
                ds = (weighted - pf * total).astype(BF)
                put_quarter(acts, d, ACT_Q, s, quad, unstacked(dot(ds, k)) * HEAD_DIM**-0.5)
                put_quarter(acts, d, ACT_Q + 1, s, quad, dot_rows(ds, qs))
                put_quarter(acts, d, ACT_Q + 2, s, quad, dot_rows(p, outs))
                traffic.tick(ticks[2])
        for c in range(3):
            put(c, dot_rows(panel(acts, d, ACT_NORMED), panel(acts, d, ACT_Q + c)))
        streams[2].pieces[0].pair_copy().start()
        traffic.tick(ticks[3])
        back = dot_lanes(side_by_side(acts, d, ACT_Q, 3), side_by_side(wts, d, W_QKV, 3))
        back, gain, shift = ln_back(xin[d], back, lnp[d, 0:1])
        lng[pl.ds(d * 4, 1), :] = gain
        lng[pl.ds(d * 4 + 2, 1), :] = shift
        up[...] += back

    def split(value):
        return value.astype(BF).reshape(8, 2, 32, WIDTH)

    def put1(p, value):
        shaped = split(value)
        for c in range(2):
            g1st[c * 12 + p] = shaped[:, c]

    def put0(p, value):
        shaped = split(value)
        for c in range(2):
            acts[1, c * 12 + p] = shaped[:, c]

    def put_down1(c, part):
        for e in range(4):
            for j in range(4):
                g1st[(e % 2) * 12 + W_DOWN + j, 2 * c + e // 2] = part[e, j]

    def put_down0(c, part):
        for e in range(4):
            for j in range(4):
                acts[1, (e % 2) * 12 + W_DOWN + j, 2 * c + e // 2] = part[e, j]

    backward(1, put1, put_down1, (down1, up1, att1), lambda: None, (0, 0, 1, 1))
    for target in (sibling, ahead, behind):
        pl.semaphore_signal(free_sem, inc=1, device_id=(section, target), device_id_type=MESH)
    traffic.open(att1)
    traffic.tick()
    backward(
        0, put0, put_down0, (down0, up0, att0),
        lambda: pl.semaphore_wait(free_sem, 3), (1, 1, 1, 1),
    )
    eg[...] = up[...].astype(BF)
    turned = jnp.transpose(lng[...]).astype(BF).reshape(8, 2, 32, 128)
    for c in range(2):
        lnown[c, 0] = turned[:, c]
    norms.pair_copy().start()

    def fetch(k):
        i, half, base = k // 2, k % 2, 16 * (k % 2)
        copies = []
        for n, (src, lanes) in enumerate(((xl_h, 256), (bl_h, 512), (g1_h, 512), (g2_h, 512))):
            copies.append(
                pltpu.make_async_copy(
                    src.at[i, pl.ds(4 * half, 4)],
                    acts.at[0, pl.ds(base + 4 * n, 4), pl.ds(0, 7), :, pl.ds(0, lanes)],
                    stream_sem.at[k % 2, n],
                )
            )
        return copies

    for copy in fetch(0):
        copy.start()
    traffic.open(att0)
    hot = jnp.where(iota((512, TABLE), 1) == ids[...], 1.0, 0.0).astype(BF)
    code = dot_rows(eg[...], hot)
    for c in range(2):
        for half in range(2):
            genc[c, 1 + half] = split(code[:, 512 * half : 512 * (half + 1)])[:, c]
        miscown[c, 0] = code[:, CODES:].astype(BF).reshape(8, 2, 32, 128)[:, c]
    dpool[...] = dot_rows(hot[:, POOL_AT : POOL_AT + 96], eg[...])
    traffic.tick()
    rows = 4 * BLOCK_ROWS

    def held(ref, d, at, lanes=512):
        return ref[d, pl.ds(at, 4), pl.ds(0, 7), :, pl.ds(0, lanes)].reshape(rows, lanes)

    for k in range(6):
        base = 16 * (k % 2)
        for copy in fetch(k):
            copy.wait()
        if k < 5:
            for copy in fetch(k + 1):
                copy.start()
        pooled = dpool[pl.ds((k // 2) * 32, FRAMES_BLOCK), :] * (1.0 / 64.0)
        wide = jnp.broadcast_to(pooled[:, None, :], (FRAMES_BLOCK, 8, WIDTH))
        wide = wide.reshape(BLOCK_ROWS, WIDTH)

        def part(bx, _):
            slope = acts[0, base + 12 + bx, pl.ds(0, 7)].reshape(BLOCK_ROWS, WIDTH)
            back = (wide * slope.astype(F32)).astype(BF)
            wts[0, bx, pl.ds(0, 7)] = back.reshape(7, 32, WIDTH)
            slope = acts[0, base + 8 + bx, pl.ds(0, 7)].reshape(BLOCK_ROWS, WIDTH)
            back = (dot_lanes(back, w2[...]) * slope.astype(F32)).astype(BF)
            wts[0, 4 + bx, pl.ds(0, 7)] = back.reshape(7, 32, WIDTH)
            return 0

        lax.fori_loop(0, 4, part, 0)
        traffic.tick()
        second = dot_rows(held(wts, 0, 0), held(acts, 0, base + 4))
        back = held(wts, 0, 4)
        patch = held(acts, 0, base, 256)
        first = [
            dot_rows(patch[:, 128 * dy2 : 128 * (dy2 + 1)], back[:, 256 * dy2 : 256 * (dy2 + 1)])
            for dy2 in range(2)
        ]
        first = first[0] + first[1]
        if k == 0:
            acc2[...] = second
            acc1[...] = first
        else:
            acc2[...] += second
            acc1[...] += first
        traffic.tick()
    shaped = split(acc2[...])
    hot, rest = patch_index(128)
    first = jnp.where(rest[:, :1] < 12, acc1[:, pl.ds(0, 128)], acc1[:, pl.ds(128, 128)])
    first = lax.dot_general(
        first, hot, (((0,), (0,)), ((), ())), preferred_element_type=F32,
        precision=lax.Precision.HIGHEST,
    )
    first = first.reshape(8, 2, 8, 48)
    first = jnp.concatenate([first, jnp.zeros((8, 2, 24, 48), F32)], axis=2).astype(BF)
    for c in range(2):
        genc[c, 0] = shaped[:, c]
        miscown[c, 0, :, :, pl.ds(64, 48)] = first[:, c]
    encoder.pair()
    traffic.tick(2)
    traffic.open(encoder)
    traffic.finish()
    for stream in (down1, up1, att1, down0, up0, att0):
        for crossed in stream.crossings:
            cross_copy(*crossed).wait()
    act_copy.wait()
    act[...] = act_theirs[...]
    late[...] = theirs1[...]
    early[...] = theirs0[...]
    norm[...] = lntheirs[0]
    enc[...] = enc_mine[...]
    misc[...] = miscmine[0]


def train(tok, cot, lens, lnp, wq, wo, wu, wd, xl, bl, g1, g2, w2, ids):
    vm = pl.BlockSpec(memory_space=pltpu.VMEM)
    sm = pl.BlockSpec(memory_space=pltpu.SMEM)
    hb = pl.BlockSpec(memory_space=pl.ANY)

    def panels(w):
        return w.reshape(2, w.shape[1] // 256, 8, 32, w.shape[2])

    def parts(saved):
        return saved.reshape(saved.shape[0], 8, 7, 32, saved.shape[2])

    half = (8, 32, WIDTH)
    pieces = 9
    return pl.pallas_call(
        train_kernel,
        in_specs=[vm, hb, sm, vm] + [hb] * 8 + [vm, vm],
        out_specs=[vm] * 7,
        out_shape=[
            jax.ShapeDtypeStruct((512, WIDTH), BF),
            jax.ShapeDtypeStruct((512, WIDTH), BF),
            jax.ShapeDtypeStruct((12, 32, WIDTH), BF),
            jax.ShapeDtypeStruct((12, 32, WIDTH), BF),
            jax.ShapeDtypeStruct((32, 128), BF),
            jax.ShapeDtypeStruct((3, 32, WIDTH), BF),
            jax.ShapeDtypeStruct((32, 128), BF),
        ],
        scratch_shapes=[
            pltpu.VMEM((2, 2 * W_PANELS) + half, BF),
            pltpu.VMEM((2, 2 * ACT_PANELS) + half, BF),
            pltpu.VMEM((24,) + half, BF),
            pltpu.VMEM((12,) + half, BF),
            pltpu.VMEM((11,) + half, BF),
            pltpu.VMEM((3, 512, WIDTH), F32),
            pltpu.VMEM((2, 512, WIDTH), F32),
            pltpu.VMEM((2, 256, 256), F32),
            pltpu.VMEM((512, WIDTH), BF),
            pltpu.VMEM((128, WIDTH), F32),
            pltpu.VMEM(cot.shape, BF),
            pltpu.VMEM((512, WIDTH), BF),
            pltpu.VMEM((512, WIDTH), BF),
            pltpu.VMEM((12, 32, WIDTH), BF),
            pltpu.VMEM((12, 32, WIDTH), BF),
            pltpu.VMEM((12, 32, WIDTH), BF),
            pltpu.VMEM((12, 32, WIDTH), BF),
            pltpu.VMEM((2, 1, 8, 32, 128), BF),
            pltpu.VMEM((1, 8, 32, 128), BF),
            pltpu.VMEM((2, HOPS, 1, 16, 128), BF),
            pltpu.VMEM((1, 32, 128), BF),
            pltpu.VMEM((1, 32, 128), BF),
            pltpu.VMEM((2, 3) + half, BF),
            pltpu.VMEM((3, 32, WIDTH), BF),
            pltpu.VMEM((2, 1, 8, 32, 128), BF),
            pltpu.VMEM((1, 8, 32, 128), BF),
            pltpu.VMEM((2, HOPS, 1, 16, 128), BF),
            pltpu.VMEM((1, 32, 128), BF),
            pltpu.VMEM((512, WIDTH), F32),
            pltpu.VMEM((128, 256), F32),
            pltpu.VMEM((96, WIDTH), F32),
            pltpu.SemaphoreType.DMA((2, W_PANELS)),
            pltpu.SemaphoreType.DMA((2, 4)),
            pltpu.SemaphoreType.DMA((9, 2)),
            pltpu.SemaphoreType.DMA((pieces, 2)),
            pltpu.SemaphoreType.DMA((pieces, 2, HOPS)),
            pltpu.SemaphoreType.DMA((pieces, 2, HOPS)),
            pltpu.SemaphoreType.REGULAR,
        ],
        compiler_params=pltpu.CompilerParams(
            collective_id=2, has_side_effects=True, vmem_limit_bytes=TRAIN_VMEM
        ),
        name="train",
    )(
        tok, cot, lens, lnp, panels(wq), panels(wo), panels(wu), panels(wd),
        parts(xl), parts(bl), parts(g1), parts(g2), w2, ids,
    )


def outputs_kernel(act_in, eg_in, late, early, norm, enc, misc, *outs):
    act, eg, qkv, out, up, down, gain, bias, bias2, enc1, enc2, book, names = outs
    for s in range(2):
        act[0, s] = act_in[pl.ds(s * 256, 256), :].astype(F32)[:252].astype(BF)
        eg[0, s] = eg_in[pl.ds(s * 256, 256), :].astype(F32)[:252].astype(BF)
    for d, rows in enumerate((early, late)):
        for c in range(3):
            qkv[0, d, :, pl.ds(512 * c, 512)] = rows[W_QKV + c].astype(F32)
        out[0, d] = rows[W_OUT].astype(F32)
        for c in range(4):
            up[0, d, :, pl.ds(512 * c, 512)] = rows[W_UP + c].astype(F32)
            down[0, d, pl.ds(32 * c, 32), :] = rows[W_DOWN + c].astype(F32)
    turned = turn(norm[...].astype(F32))
    for d in range(2):
        gain[0, d] = turned[4 * d : 4 * d + 2]
        bias[0, pl.ds(d, 1)] = turned[4 * d + 2 : 4 * d + 3]
        bias2[0, pl.ds(d, 1)] = turned[4 * d + 3 : 4 * d + 4]
    enc2[0] = enc[0].astype(F32)
    for c in range(2):
        book[0, :, pl.ds(512 * c, 512)] = enc[1 + c].astype(F32)
    enc1[0] = misc[...].astype(F32)[:8, 64:112]
    turned = turn(misc[...].astype(F32))
    for a in range(17):
        names[a] = turned[a : a + 1]


def spread_outputs(*parts):
    vm = pl.BlockSpec(memory_space=pltpu.VMEM)
    shapes = [
        (1, 2, 32, 1536), (1, 2, 32, 512), (1, 2, 32, 2048), (1, 2, 128, 512), (1, 2, 2, 32),
        (1, 2, 32), (1, 2, 32), (1, 8, 48), (1, 32, 512), (1, 32, 1024), (17, 1, 32),
    ]
    acts = [jax.ShapeDtypeStruct((1, 2, 252, WIDTH), BF)] * 2
    outs = pl.pallas_call(
        outputs_kernel,
        in_specs=[vm] * len(parts),
        out_specs=[vm] * (len(shapes) + 2),
        out_shape=acts + [jax.ShapeDtypeStruct(shape, F32) for shape in shapes],
        compiler_params=pltpu.CompilerParams(vmem_limit_bytes=VMEM_LIMIT),
        name="outputs",
    )(*parts)
    outs = list(outs)
    outs[6] = outs[6].transpose(0, 1, 3, 2)
    for k in (9, 10, 11):
        outs[k] = outs[k].transpose(0, 2, 1)
    outs[12] = outs[12].transpose(1, 0, 2)
    return tuple(outs)


def swap(array):
    return lax.ppermute(array, "section", [(0, 1), (1, 0)])


def whole_rows(g):
    return g.transpose(1, 0, 2, 3).reshape(512, g.shape[-1])


def scatter_plain(g, gl, e):
    def sums(array, axis):
        return lax.psum_scatter(array.astype(F32)[None], "dp", scatter_dimension=axis, tiled=True)

    layers = [whole_rows(g[d]) for d in range(g.shape[0])]
    qkv = jnp.stack([rows[:, :1536] for rows in layers])
    out = jnp.stack([rows[:, 1536:2048] for rows in layers])
    up = jnp.stack([rows[:, 2048:4096] for rows in layers])
    down = jnp.stack(
        [
            rows[:, 4096:].reshape(16, 32, 4, WIDTH).transpose(0, 2, 1, 3).reshape(2048, WIDTH)
            for rows in layers
        ]
    )
    norm = whole_rows(gl)[:, :8].reshape(512, 2, 4).transpose(1, 0, 2)
    enc = whole_rows(e)
    first = e.transpose(1, 0, 2, 3)[:, :, :8, 1600:1648].reshape(128, 48)
    layer_sums = [sums(x, 2) for x in (qkv, out, up, down, norm)]
    layer_sums = [swap(x) for x in layer_sums]
    norm = layer_sums.pop()
    return tuple(layer_sums) + (
        norm[..., 0:2],
        norm[..., 2],
        norm[..., 3],
        sums(first.T, 2),
        sums(enc[:, :512].T, 2),
        sums(enc[:, 512:1536].T, 2),
        sums(enc[:, 1536:1553].T, 2),
    )


def on_device(
    frames, action_ids, delta_ids, seq_len, enc_w1, enc_w2, codebook, action_table,
    ln_gain, ln_bias, w_qkv, w_out, w_up, w_down, cotangent,
):
    micro, steps = frames.shape[1], frames.shape[2]
    count = micro * steps
    frame = jnp.arange(count, dtype=I32).reshape(micro, steps, 1)
    pool_ids = POOL_AT + (frame // FRAMES_BLOCK) * 32 + frame % FRAMES_BLOCK
    ids = jnp.concatenate([pool_ids, action_ids[0][:, :, None] + ACT_AT, delta_ids[0]], axis=2)
    ids = ids.reshape(micro, steps * TPS)
    ids = jnp.pad(ids, ((0, 0), (0, 256 - steps * TPS)), constant_values=-1).reshape(512, 1)
    lnp = jnp.concatenate([ln_gain, ln_bias], axis=2).transpose(0, 2, 1)

    tok, xl, blocks, g1, g2 = enc_forward(
        frames.reshape((count,) + frames.shape[3:]), enc_w1, enc_w2, codebook, action_table, ids
    )
    if lax.axis_size("dp") == 2 * CHIPS:
        parts = train(
            tok, cotangent[0], seq_len, lnp, w_qkv, w_out, w_up, w_down,
            xl, blocks, g1, g2, enc_w2, ids,
        )
        return spread_outputs(*parts)
    act, eg, g, gl = run_layers(tok, cotangent[0], seq_len, lnp, w_qkv, w_out, w_up, w_down)
    embed_grad = eg.reshape(micro, 256, WIDTH)[None, :, : steps * TPS]
    e = enc_backward(eg, xl, blocks, g1, g2, enc_w2, ids)
    return (act[None], embed_grad) + scatter_plain(g, gl, e)


def solution(mesh):
    return jax.shard_map(
        on_device,
        mesh=mesh,
        in_specs=(
            P("section", "dp", None, None, None),
            P("section", "dp", None),
            P("section", "dp", None, None),
            P(None, "dp"),
            P(), P(), P(), P(), P(), P(), P(), P(), P(), P(),
            P("section", "dp", None, None),
        ),
        out_specs=(
            P("section", "dp", None, None),
            P("section", "dp", None, None),
            P("section", None, "dp", None),
            P("section", None, "dp", None),
            P("section", None, "dp", None),
            P("section", None, "dp", None),
            P("section", None, "dp", None),
            P("section", None, "dp"),
            P("section", None, "dp"),
            P("section", None, "dp"),
            P("section", None, "dp"),
            P("section", None, "dp"),
            P("section", None, "dp"),
        ),
        check_vma=False,
    )
```

```python
import functools

import jax
import jax.numpy as jnp
from jax import lax
from jax.experimental import pallas as pl
from jax.experimental.pallas import tpu as pltpu
from jax.sharding import PartitionSpec as P

HEADS = 8
HEAD_DIM = 64
TPS = 6
EPS = 1e-05
BF = jnp.bfloat16
F32 = jnp.float32
I32 = jnp.int32

WIDTH = 512
CODES = 1024
FRAMES_BLOCK = 28
BLOCK_ROWS = FRAMES_BLOCK * 8
TABLE = 1152
POOL_AT = 1056
ACT_AT = 1024
LAYER_COLS = 6144
ENC_COLS = 1664
VMEM_LIMIT = 60 << 20
TRAIN_VMEM = 63 << 20
PLAN = "00000000010111000000001111110101010101012"


def dot(a, b):
    return jnp.dot(a, b, preferred_element_type=F32)


def dot_rows(a, b):
    return lax.dot_general(a, b, (((0,), (0,)), ((), ())), preferred_element_type=F32)


def dot_lanes(a, b):
    return lax.dot_general(a, b, (((1,), (1,)), ((), ())), preferred_element_type=F32)


def iota(shape, axis):
    return lax.broadcasted_iota(I32, shape, axis)


def gelu_pair(v):
    cdf = 0.5 + 0.5 * lax.erf(v * 0.7071067811865476)
    bell = jnp.exp2(v * v * (-0.5 * 1.4426950408889634))
    return v * cdf, cdf + v * (bell * 0.3989422804014327)


def gelu(v):
    return v * (0.5 + 0.5 * lax.erf(v * 0.7071067811865476))


def gelu_slope(v):
    return gelu_pair(v.astype(F32))[1]


def patch_index(rows):
    k = iota((rows, 48), 0)
    dy = (k * 2731) >> 16
    rest = k - dy * 24
    j = jnp.where(rest >= 12, rest - 12, rest)
    return jnp.where((iota((rows, 48), 1) == dy * 12 + j) & (k < 96), 1.0, 0.0), rest


def encoder_weights(w1):
    hot, rest = patch_index(128)
    wide = dot(hot.astype(BF), w1)
    first = jnp.where(rest[:, :1] < 12, wide, 0.0)
    second = jnp.where(rest[:, :1] >= 12, wide, 0.0)
    block = jnp.concatenate([first, second], axis=1)
    zero = jnp.zeros_like(block)
    return jnp.concatenate(
        [jnp.concatenate([block, zero], axis=1), jnp.concatenate([zero, block], axis=1)], axis=0
    ).astype(BF)


def token_ids(s, names, deltas):
    steps = names.shape[1]
    frame = s * steps + iota((1, steps), 1)
    block = (frame * 2341) >> 16
    pool = POOL_AT + block * 32 + frame - FRAMES_BLOCK * block
    kinds = jnp.concatenate([pool, names[s : s + 1] + ACT_AT, deltas[s]], axis=0).astype(F32)
    row = iota((256, 1), 0)
    step = (row * 10923) >> 16
    hot = jnp.where(iota((256, steps), 1) == step, 1.0, 0.0)
    each = lax.dot_general(
        hot, kinds, (((1,), (1,)), ((), ())), preferred_element_type=F32,
        precision=lax.Precision.HIGHEST,
    )
    mine = jnp.where(iota((256, TPS), 1) == row - TPS * step, each, 0.0)
    found = (jnp.sum(mine, axis=1, keepdims=True) + 0.5).astype(I32)
    return jnp.where(row < TPS * steps, found, -1)


def enc_fwd_kernel(
    frames, w1, w2, book, acts, names, deltas,
    tok, ids, xl, blocks, z1, z2, perm, lanes, big, xs, acc, table,
):
    step = pl.program_id(0)

    @pl.when(step == 0)
    def _():
        a, b = iota((256, 256), 0), iota((256, 256), 1)
        perm[...] = jnp.where(b == 8 * (a & 31) + (a >> 5), 1.0, 0.0).astype(BF)
        src = iota((256, 1024), 0)
        px = (src * 5462) >> 16
        at = (px >> 1) * 128 + (px & 1) * 12 + (src - px * 12)
        out = jnp.where(src < 192, iota((256, 1024), 1) - at, -1)
        for dy in range(4):
            lanes[pl.ds(256 * dy, 256), :] = jnp.where(out == dy * 24, 1.0, 0.0).astype(BF)
        xs[...] = jnp.zeros_like(xs)
        big[...] = encoder_weights(w1[...])
        table[pl.ds(0, CODES), :] = book[...]
        named = acts[...].astype(F32)
        pad = jnp.zeros((TABLE - ACT_AT - named.shape[0], WIDTH), F32)
        table[pl.ds(ACT_AT, TABLE - ACT_AT), :] = jnp.concatenate([named, pad], axis=0).astype(BF)

    for group in range(FRAMES_BLOCK // 4):
        rows = frames[pl.ds(group * 4, 4)].reshape(256, 192)
        moved = dot(perm[...], rows).astype(BF).reshape(2, 4, 32, 192)
        for dy in range(4):
            xs[:, pl.ds(group * 32, 32), pl.ds(256 * dy, 192)] = moved[:, dy]
    for dy2 in range(2):
        spread = dot(xs[dy2], lanes[...]).astype(BF)
        for bx in range(8):
            xl[0, pl.ds(bx * BLOCK_ROWS, BLOCK_ROWS), pl.ds(dy2 * 128, 128)] = spread[
                :, bx * 128 : (bx + 1) * 128
            ]
    acc[...] = jnp.zeros_like(acc)

    def part(bx, _):
        rows = pl.ds(pl.multiple_of(bx * BLOCK_ROWS, BLOCK_ROWS), BLOCK_ROWS)
        first = dot(xl[0, rows, :], big[...])
        z1[0, rows, :] = first.astype(BF)
        value = gelu(first).astype(BF)
        blocks[0, rows, :] = value
        second = dot(value, w2[...])
        z2[0, rows, :] = second.astype(BF)
        acc[...] += gelu(second)
        return 0

    lax.fori_loop(0, 8, part, 0, unroll=True)
    pooled = jnp.sum(acc[...].reshape(FRAMES_BLOCK, 8, WIDTH), axis=1) * (1.0 / 64.0)
    pooled = jnp.concatenate([pooled, jnp.zeros((32 - FRAMES_BLOCK, WIDTH), F32)], axis=0)
    table[pl.ds(pl.multiple_of(POOL_AT + step * 32, 32), 32), :] = pooled.astype(BF)

    @pl.when(step == pl.num_programs(0) - 1)
    def _():
        for s in range(2):
            rows = pl.ds(s * 256, 256)
            found = token_ids(s, names[...], deltas[...])
            ids[rows, :] = found
            hot = jnp.where(iota((256, TABLE), 1) == found, 1.0, 0.0).astype(BF)
            tok[rows, :] = dot(hot, table[...]).astype(BF)


def enc_forward(frames, w1, w2, book, acts, names, deltas):
    count = frames.shape[0]
    grid = count // FRAMES_BLOCK
    rows = 8 * BLOCK_ROWS

    def whole(shape):
        return pl.BlockSpec(shape, lambda i: (0,) * len(shape))

    def saved(lanes):
        return pl.BlockSpec((1, rows, lanes), lambda i: (i, 0, 0))

    return pl.pallas_call(
        enc_fwd_kernel,
        grid=(grid,),
        in_specs=[
            pl.BlockSpec((FRAMES_BLOCK, 64, 192), lambda i: (i, 0, 0)),
            whole(w1.shape),
            whole(w2.shape),
            whole(book.shape),
            whole(acts.shape),
            whole(names.shape),
            whole(deltas.shape),
        ],
        out_specs=[
            whole((512, WIDTH)), whole((512, 1)), saved(256), saved(512), saved(512), saved(512),
        ],
        out_shape=[
            jax.ShapeDtypeStruct((512, WIDTH), BF),
            jax.ShapeDtypeStruct((512, 1), I32),
            jax.ShapeDtypeStruct((grid, rows, 256), BF),
            jax.ShapeDtypeStruct((grid, rows, 512), BF),
            jax.ShapeDtypeStruct((grid, rows, 512), BF),
            jax.ShapeDtypeStruct((grid, rows, 512), BF),
        ],
        scratch_shapes=[
            pltpu.VMEM((256, 256), BF),
            pltpu.VMEM((1024, 1024), BF),
            pltpu.VMEM((256, 512), BF),
            pltpu.VMEM((2, BLOCK_ROWS, 1024), BF),
            pltpu.VMEM((BLOCK_ROWS, WIDTH), F32),
            pltpu.VMEM((TABLE, WIDTH), BF),
        ],
        compiler_params=pltpu.CompilerParams(vmem_limit_bytes=VMEM_LIMIT),
        name="enc_fwd",
    )(frames, w1, w2, book, acts, names, deltas)


def ln_parts(x):
    mean = jnp.mean(x, axis=-1, keepdims=True)
    center = x - mean
    var = jnp.mean(center * center, axis=-1, keepdims=True)
    scale = lax.rsqrt(var + EPS)
    return center * scale, scale


def ln_back(x, d, gain):
    hat, scale = ln_parts(x)
    dh = d * gain
    one = jnp.mean(dh, axis=-1, keepdims=True)
    two = jnp.mean(dh * hat, axis=-1, keepdims=True)
    back = scale * (dh - one - hat * two)
    return back, jnp.sum(d * hat, axis=0, keepdims=True), jnp.sum(d, axis=0, keepdims=True)


def head_mask(h):
    lane = iota((1, 256), 1) >> 6
    return lane == h


def stacked(rows, scale):
    out = []
    for h in range(4):
        mask = jnp.where(head_mask(h), scale, 0.0).astype(BF)
        out.append(rows * mask)
    return jnp.concatenate(out, axis=0)


def unstacked(rows):
    out = rows[768:]
    for h in range(3):
        out = jnp.where(head_mask(h), rows[h * 256 : (h + 1) * 256], out)
    return out


def scatter_rows(g, d, cols, value, dests=16):
    shaped = value.astype(BF).reshape(dests // 2, 2, 32, value.shape[1])
    for core in range(2):
        g[d, core, :, :, cols] = shaped[:, core]


def layers_kernel(
    tok, cot_h, lens, lnp, wq_h, wo_h, wu_h, wd_h,
    act, eg, g, gl,
    wq, wo, wu, wd, stream, normed, packed, probs, att, normed2, gated, slope, bias,
    up, back_up, back_att, back_packed, lng, cot, mine, theirs, sems, cross_sem,
):
    layers = wq.shape[0]
    section = lax.axis_index("section")
    barrier = pltpu.get_barrier_semaphore()
    pl.semaphore_signal(
        barrier, inc=1, device_id=(1 - section, lax.axis_index("dp")), device_id_type=MESH
    )
    pl.semaphore_wait(barrier, 1)
    cot_copy = cross_copy(cot_h, cot, cross_sem.at[0])
    cot_copy.start()
    act_copy = cross_copy(mine, theirs, cross_sem.at[1])
    copies = []
    for d in range(layers):
        for k, (src, dst) in enumerate(((wq_h, wq), (wo_h, wo), (wu_h, wu), (wd_h, wd))):
            copy = pltpu.make_async_copy(src.at[d], dst.at[d], sems.at[d, k])
            copy.start()
            copies.append(copy)

    stream[0, 0] = tok[...].astype(F32)
    row = iota((256, 1), 0)
    col = iota((1, 256), 1)
    q_step = ((row * 10923) >> 16).astype(F32)
    k_step = ((col * 10923) >> 16).astype(F32)
    for s in range(2):
        inv = 1.0 / lens[section, s].astype(F32)
        q_seq = jnp.floor((q_step + 0.5) * inv)
        k_seq = jnp.floor((k_step + 0.5) * inv)
        bias[s] = jnp.where((k_step <= q_step) & (q_seq == k_seq), 0.0, -1e30)
    for copy in copies:
        copy.wait()

    def forward(d, _):
        x = stream[d, 0]
        hat, _ = ln_parts(x)
        normed[d] = (hat * lnp[d, 0:1] + lnp[d, 2:3]).astype(BF)
        for c in range(3):
            cols = pl.ds(c * 512, 512)
            packed[d, :, cols] = dot(normed[d], wq[d, :, cols]).astype(BF)
        for s in range(2):
            rows = pl.ds(s * 256, 256)
            for quad in range(2):
                q = stacked(packed[d, rows, pl.ds(quad * 256, 256)], HEAD_DIM**-0.5)
                k = packed[d, rows, pl.ds(512 + quad * 256, 256)]
                v = packed[d, rows, pl.ds(1024 + quad * 256, 256)]
                scores = dot_lanes(q, k).reshape(4, 256, 256) + bias[s][None]
                top = jnp.max(scores, axis=-1, keepdims=True)
                e = jnp.exp(scores - top)
                total = jnp.sum(e, axis=-1, keepdims=True)
                p = (e * (1.0 / total)).astype(BF).reshape(1024, 256)
                probs[d, s * 2 + quad] = p
                att[d, rows, pl.ds(quad * 256, 256)] = unstacked(dot(p, v)).astype(BF)
        middle = stream[d, 0] + dot(att[d], wo[d])
        stream[d, 1] = middle
        hat, _ = ln_parts(middle)
        normed2[d] = (hat * lnp[d, 1:2] + lnp[d, 3:4]).astype(BF)

        def chunk(c, _):
            cols = pl.ds(pl.multiple_of(c * 512, 512), 512)
            value, grad = gelu_pair(dot(normed2[d], wu[d, :, cols]))
            gated[d, :, cols] = value.astype(BF)
            slope[d, :, cols] = grad.astype(BF)
            return 0

        lax.fori_loop(0, 4, chunk, 0)
        stream[d + 1, 0] = stream[d, 1] + dot(gated[d], wd[d])
        return 0

    lax.fori_loop(0, layers, forward, 0)
    cot_copy.wait()
    mine[...] = stream[layers, 0].astype(BF)
    act_copy.start()
    for s in range(2):
        up[pl.ds(s * 256, 252), :] = cot[s].astype(F32)
        up[pl.ds(s * 256 + 252, 4), :] = jnp.zeros((4, WIDTH), F32)
    lng[...] = jnp.zeros_like(lng)

    def backward(i, _):
        d = layers - 1 - i
        down = up[...].astype(BF)

        def chunk(c, _):
            cols = pl.ds(pl.multiple_of(c * 256, 256), 256)
            part = dot_rows(gated[d, :, cols], down).astype(BF).reshape(2, 4, 32, WIDTH)
            for core in range(2):
                for j in range(4):
                    g[d, core, c, :, pl.ds(4096 + 512 * j, 512)] = part[core, j]
            back = dot_lanes(down, wd[d, cols, :])
            back = (back * slope[d, :, cols].astype(F32)).astype(BF)
            back_up[:, cols] = back
            part = dot_rows(normed2[d], back).astype(BF).reshape(8, 2, 32, 256)
            out = pl.ds(pl.multiple_of(2048 + c * 256, 256), 256)
            for core in range(2):
                g[d, core, :, :, out] = part[:, core]
            return 0

        lax.fori_loop(0, 8, chunk, 0)
        back, gain, shift = ln_back(stream[d, 1], dot_lanes(back_up[...], wu[d]), lnp[d, 1:2])
        lng[pl.ds(d * 4 + 1, 1), :] = gain
        lng[pl.ds(d * 4 + 3, 1), :] = shift
        up[...] += back
        branch = up[...].astype(BF)
        scatter_rows(g, d, pl.ds(1536, 512), dot_rows(att[d], branch))
        back_att[...] = dot_lanes(branch, wo[d]).astype(BF)
        for s in range(2):
            rows = pl.ds(s * 256, 256)
            for quad in range(2):
                lanes = pl.ds(quad * 256, 256)
                qs = stacked(packed[d, rows, lanes], HEAD_DIM**-0.5)
                k = packed[d, rows, pl.ds(512 + quad * 256, 256)]
                v = packed[d, rows, pl.ds(1024 + quad * 256, 256)]
                outs = stacked(back_att[rows, lanes], 1.0)
                p = probs[d, s * 2 + quad]
                dp = dot_lanes(outs, v)
                pf = p.astype(F32)
                weighted = pf * dp
                total = jnp.sum(weighted, axis=-1, keepdims=True)
                ds = (weighted - pf * total).astype(BF)
                back_packed[rows, lanes] = (unstacked(dot(ds, k)) * HEAD_DIM**-0.5).astype(BF)
                back_packed[rows, pl.ds(512 + quad * 256, 256)] = dot_rows(ds, qs).astype(BF)
                back_packed[rows, pl.ds(1024 + quad * 256, 256)] = dot_rows(p, outs).astype(BF)
        for c in range(3):
            cols = pl.ds(c * 512, 512)
            scatter_rows(g, d, cols, dot_rows(normed[d], back_packed[:, cols]))
        back, gain, shift = ln_back(stream[d, 0], dot_lanes(back_packed[...], wq[d]), lnp[d, 0:1])
        lng[pl.ds(d * 4, 1), :] = gain
        lng[pl.ds(d * 4 + 2, 1), :] = shift
        up[...] += back
        return 0

    lax.fori_loop(0, layers, backward, 0)
    eg[...] = up[...].astype(BF)
    act_copy.wait()
    for s in range(2):
        act[s] = theirs[pl.ds(s * 256, 256), :].astype(F32)[:252].astype(BF)
    turned = jnp.transpose(lng[...]).astype(BF).reshape(8, 2, 32, 128)
    for core in range(2):
        gl[core] = turned[:, core]


def run_layers(tok, cot, lens, lnp, wq, wo, wu, wd):
    layers = wq.shape[0]
    vm = pl.BlockSpec(memory_space=pltpu.VMEM)
    sm = pl.BlockSpec(memory_space=pltpu.SMEM)
    hb = pl.BlockSpec(memory_space=pl.ANY)
    rows = 512
    return pl.pallas_call(
        layers_kernel,
        in_specs=[vm, hb, sm, vm, hb, hb, hb, hb],
        out_specs=[vm, vm, vm, vm],
        out_shape=[
            jax.ShapeDtypeStruct((2, 252, WIDTH), BF),
            jax.ShapeDtypeStruct((rows, WIDTH), BF),
            jax.ShapeDtypeStruct((layers, 2, 8, 32, LAYER_COLS), BF),
            jax.ShapeDtypeStruct((2, 8, 32, 128), BF),
        ],
        scratch_shapes=[
            pltpu.VMEM(wq.shape, BF),
            pltpu.VMEM(wo.shape, BF),
            pltpu.VMEM(wu.shape, BF),
            pltpu.VMEM(wd.shape, BF),
            pltpu.VMEM((layers + 1, 2, rows, WIDTH), F32),
            pltpu.VMEM((layers, rows, WIDTH), BF),
            pltpu.VMEM((layers, rows, 3 * WIDTH), BF),
            pltpu.VMEM((layers, 4, 1024, 256), BF),
            pltpu.VMEM((layers, rows, WIDTH), BF),
            pltpu.VMEM((layers, rows, WIDTH), BF),
            pltpu.VMEM((layers, rows, 4 * WIDTH), BF),
            pltpu.VMEM((layers, rows, 4 * WIDTH), BF),
            pltpu.VMEM((2, 256, 256), F32),
            pltpu.VMEM((rows, WIDTH), F32),
            pltpu.VMEM((rows, 4 * WIDTH), BF),
            pltpu.VMEM((rows, WIDTH), BF),
            pltpu.VMEM((rows, 3 * WIDTH), BF),
            pltpu.VMEM((128, WIDTH), F32),
            pltpu.VMEM(cot.shape, BF),
            pltpu.VMEM((rows, WIDTH), BF),
            pltpu.VMEM((rows, WIDTH), BF),
            pltpu.SemaphoreType.DMA((layers, 4)),
            pltpu.SemaphoreType.DMA((2, 2)),
        ],
        compiler_params=pltpu.CompilerParams(
            collective_id=1, has_side_effects=True, vmem_limit_bytes=VMEM_LIMIT
        ),
        name="layers",
    )(tok, cot, lens, lnp, wq, wo, wu, wd)


def enc_bwd_kernel(eg, xl, blocks, g1, g2, w2, ids, e, dpool, bs, bf, acc2, acc1):
    step = pl.program_id(0)

    @pl.when(step == 0)
    def _():
        hot = jnp.where(iota((512, TABLE), 1) == ids[...], 1.0, 0.0).astype(BF)
        code = dot_rows(eg[...], hot[:, :POOL_AT + 96]).astype(BF)
        dpool[...] = dot_rows(hot[:, POOL_AT : POOL_AT + 96], eg[...])
        parts = code[:, :CODES].reshape(8, 2, 32, CODES)
        tail = code[:, CODES : CODES + 128].reshape(8, 2, 32, 128)
        for core in range(2):
            e[core, :, :, pl.ds(512, CODES)] = parts[:, core]
            e[core, :, :, pl.ds(1536, 128)] = tail[:, core]
        acc2[...] = jnp.zeros_like(acc2)
        acc1[...] = jnp.zeros_like(acc1)

    pooled = dpool[pl.ds(pl.multiple_of(step * 32, 32), 32), :][:FRAMES_BLOCK] * (1.0 / 64.0)
    wide = jnp.broadcast_to(pooled[:, None, :], (FRAMES_BLOCK, 8, WIDTH)).reshape(BLOCK_ROWS, WIDTH)

    def part(bx, _):
        rows = pl.ds(pl.multiple_of(bx * BLOCK_ROWS, BLOCK_ROWS), BLOCK_ROWS)
        back = (wide * gelu_slope(g2[0, rows, :])).astype(BF)
        bs[rows, :] = back
        bf[rows, :] = (dot_lanes(back, w2[...]) * gelu_slope(g1[0, rows, :])).astype(BF)
        return 0

    lax.fori_loop(0, 8, part, 0)
    acc2[...] += dot_rows(bs[...], blocks[0])
    for dy2 in range(2):
        acc1[:, pl.ds(dy2 * 256, 256)] += dot_rows(
            xl[0, :, pl.ds(dy2 * 128, 128)], bf[:, pl.ds(dy2 * 256, 256)]
        )

    @pl.when(step == pl.num_programs(0) - 1)
    def _():
        parts = acc2[...].astype(BF).reshape(8, 2, 32, WIDTH)
        both = acc1[:, pl.ds(0, 256)] + acc1[:, pl.ds(256, 256)]
        hot, rest = patch_index(128)
        first = jnp.where(rest[:, :1] < 12, both[:, :128], both[:, 128:])
        first = lax.dot_general(
            first, hot, (((0,), (0,)), ((), ())), preferred_element_type=F32,
            precision=lax.Precision.HIGHEST,
        )
        first = first.reshape(8, 2, 8, 48)
        first = jnp.concatenate([first, jnp.zeros((8, 2, 24, 48), F32)], axis=2).astype(BF)
        for core in range(2):
            e[core, :, :, pl.ds(0, WIDTH)] = parts[:, core]
            e[core, :, :, pl.ds(1536 + 64, 48)] = first[:, core]


def enc_backward(eg, xl, blocks, g1, g2, w2, ids):
    grid, rows, _ = xl.shape

    def whole(shape):
        return pl.BlockSpec(shape, lambda i: (0,) * len(shape))

    def saved(lanes):
        return pl.BlockSpec((1, rows, lanes), lambda i: (i, 0, 0))

    return pl.pallas_call(
        enc_bwd_kernel,
        grid=(grid,),
        in_specs=[
            whole(eg.shape), saved(256), saved(512), saved(512), saved(512),
            whole(w2.shape), whole(ids.shape),
        ],
        out_specs=whole((2, 8, 32, ENC_COLS)),
        out_shape=jax.ShapeDtypeStruct((2, 8, 32, ENC_COLS), BF),
        scratch_shapes=[
            pltpu.VMEM((96, WIDTH), F32),
            pltpu.VMEM((rows, WIDTH), BF),
            pltpu.VMEM((rows, WIDTH), BF),
            pltpu.VMEM((WIDTH, WIDTH), F32),
            pltpu.VMEM((128, WIDTH), F32),
        ],
        compiler_params=pltpu.CompilerParams(vmem_limit_bytes=VMEM_LIMIT),
        name="enc_bwd",
    )(eg, xl, blocks, g1, g2, w2, ids)


CHIPS = 8
HOPS = CHIPS // 2
MESH = pl.DeviceIdType.MESH


def ring_place(chip):
    z, x = chip // 2, chip % 2
    return z * (1 - x) + (7 - z) * x


def ring_chip(place):
    half = place // 4
    return (1 - half) * (2 * place) + half * (15 - 2 * place)


def where_am_i():
    section, me = lax.axis_index("section"), lax.axis_index("dp")
    core, chip = me % 2, me // 2
    place = ring_place(chip)
    ahead = ring_chip((place + 1) % CHIPS) * 2 + core
    behind = ring_chip((place + CHIPS - 1) % CHIPS) * 2 + core
    sibling = chip * 2 + (1 - core)
    return section, me, core, place, ahead, behind, sibling


def greet():
    section, me, _, _, ahead, behind, sibling = where_am_i()
    barrier = pltpu.get_barrier_semaphore()
    for target in ((section, sibling), (section, ahead), (section, behind), (1 - section, me)):
        pl.semaphore_signal(barrier, inc=1, device_id=target, device_id_type=MESH)
    pl.semaphore_wait(barrier, 4)


def cross_copy(src, dst, sem):
    section, me = lax.axis_index("section"), lax.axis_index("dp")
    return pltpu.make_async_remote_copy(
        src_ref=src, dst_ref=dst, send_sem=sem.at[0], recv_sem=sem.at[1],
        device_id=(1 - section, me), device_id_type=MESH,
    )


def turn(rows):
    tall = jnp.concatenate([rows, jnp.zeros((96, rows.shape[1]), F32)], axis=0)
    return jnp.transpose(tall)[:, :32]


ACT_NORMED, ACT_Q, ACT_PROBS, ACT_ATT, ACT_NORMED2, ACT_GATED, ACT_SLOPE = 0, 1, 4, 8, 9, 10, 14
ACT_PANELS = 18
W_QKV, W_OUT, W_UP, W_DOWN = 0, 3, 4, 8
W_PANELS = 12


def panel(ref, d, p):
    return ref[d, pl.ds(2 * p, 2)].reshape(512, WIDTH)


def put_panel(ref, d, p, value):
    ref[d, pl.ds(2 * p, 2)] = value.astype(BF).reshape(2, 8, 32, WIDTH)


def quarter(ref, d, p, s, quad):
    return ref[d, 2 * p + s, :, :, pl.ds(256 * quad, 256)].reshape(256, 256)


def put_quarter(ref, d, p, s, quad, value):
    ref[d, 2 * p + s, :, :, pl.ds(256 * quad, 256)] = value.astype(BF).reshape(8, 32, 256)


def side_by_side(ref, d, p, count):
    return jnp.concatenate([panel(ref, d, p + c) for c in range(count)], axis=1)


class Piece:
    def __init__(self, own, pair, hop, mine, sems):
        self.own, self.pair, self.hop, self.mine = own, pair, hop, mine
        self.pair_sem, self.send_sem, self.recv_sem = sems

    def pair_copy(self):
        section, _, core, _, _, _, sibling = where_am_i()
        return pltpu.make_async_remote_copy(
            src_ref=self.own(1 - core), dst_ref=self.pair,
            send_sem=self.pair_sem.at[0], recv_sem=self.pair_sem.at[1],
            device_id=(section, sibling), device_id_type=MESH,
        )

    def target(self, way, step):
        place, far = where_am_i()[3], HOPS - step
        return ring_chip((place + (far if way == 0 else CHIPS - far)) % CHIPS)

    def rows(self, way, step):
        return pl.ds(0, 32) if step else pl.ds(16 * way, 16)

    def hop_copy(self, way, step):
        section, _, _, _, ahead, behind, _ = where_am_i()
        return pltpu.make_async_remote_copy(
            src_ref=self.pair.at[:, self.target(way, step), self.rows(way, step), :],
            dst_ref=self.hop(way, step),
            send_sem=self.send_sem.at[way, step], recv_sem=self.recv_sem.at[way, step],
            device_id=(section, ahead if way == 0 else behind), device_id_type=MESH,
        )

    def both(self, at, rows):
        core = where_am_i()[2]
        return self.own(core)[:, at, rows, :].astype(F32) + self.pair[:, at, rows, :].astype(F32)

    def send(self, step):
        for way in range(2):
            if step:
                self.hop_copy(way, step - 1).wait()
            at = self.target(way, step)
            for half in range(2):
                if step == 0 and half != way:
                    continue
                rows = pl.ds(16 * half, 16)
                value = self.both(at, rows)
                if step == 1 and half == way:
                    value += self.hop(way, 0)[...].astype(F32)
                elif step > 1:
                    value += self.hop(way, step - 1)[:, rows, :].astype(F32)
                self.pair[:, at, rows, :] = value.astype(BF)
            self.hop_copy(way, step).start()

    def close(self):
        at = ring_chip(where_am_i()[3])
        value = self.both(at, pl.ds(0, 32))
        for way in range(2):
            self.hop_copy(way, HOPS - 1).wait()
            value += self.hop(way, HOPS - 1)[...].astype(F32)
        self.mine[...] = value.astype(self.mine.dtype)


class Stream:
    def __init__(self, pieces, crossings):
        self.pieces, self.crossings = pieces, crossings

    def pair(self):
        for piece in self.pieces:
            piece.pair_copy().start()

    def open(self):
        for piece in self.pieces:
            piece.pair_copy().wait()
            piece.send(0)

    def send(self, step):
        for piece in self.pieces:
            piece.send(step)

    def close(self):
        for piece in self.pieces:
            piece.close()
        for crossing in self.crossings:
            cross_copy(*crossing).start()


class Traffic:
    def __init__(self, plan):
        self.queue, self.plan = [], plan

    def open(self, stream):
        stream.open()
        self.queue.append((stream, 1))

    def tick(self, count=None):
        if count is None:
            count, self.plan = int(self.plan[0]), self.plan[1:]
        for _ in range(count):
            if not self.queue:
                return
            stream, step = self.queue.pop(0)
            if step < HOPS:
                stream.send(step)
                self.queue.append((stream, step + 1))
            else:
                stream.close()

    def finish(self):
        while self.queue:
            self.tick(1)


def train_kernel(
    tok, cot_h, lens, gains, shifts, wq_h, wo_h, wu_h, wd_h, xl_h, bl_h, z1_h, z2_h, w2, ids,
    act, eg, late, early, norm, enc, misc,
    wts, acts, g1st, pair1, hop1, xin, mid, bias, back_att, lng, cot, act_mine, act_theirs,
    mine1, theirs1, mine0, theirs0, lnown, lnpair, lnhop, lnmine, lntheirs,
    genc, enc_mine, miscown, miscpair, mischop, miscmine, acc2, acc1, dpool,
    load_sem, stream_sem, cross_sem, pair_sem, send_sem, recv_sem, free_sem,
):
    section, me, core, _, ahead, behind, sibling = where_am_i()
    greet()
    cot_copy = cross_copy(cot_h, cot, cross_sem.at[0])
    cot_copy.start()
    act_copy = cross_copy(act_mine, act_theirs, cross_sem.at[1])
    for d in range(2):
        for c in range(W_PANELS):
            if c < 3:
                src = wq_h.at[d, :, :, :, pl.ds(512 * c, 512)]
            elif c == 3:
                src = wo_h.at[d]
            elif c < 8:
                src = wu_h.at[d, :, :, :, pl.ds(512 * (c - 4), 512)]
            else:
                src = wd_h.at[d, pl.ds(2 * (c - 8), 2)]
            pltpu.make_async_copy(src, wts.at[d, pl.ds(2 * c, 2)], load_sem.at[d, c]).start()

    xin[0] = tok[...].astype(F32)
    row, col = iota((256, 1), 0), iota((1, 256), 1)
    q_step = ((row * 10923) >> 16).astype(F32)
    k_step = ((col * 10923) >> 16).astype(F32)
    for s in range(2):
        inv = 1.0 / lens[section, s].astype(F32)
        q_seq = jnp.floor((q_step + 0.5) * inv)
        k_seq = jnp.floor((k_step + 0.5) * inv)
        bias[s] = jnp.where((k_step <= q_step) & (q_seq == k_seq), 0.0, -1e30)
    def loaded(d, first, count):
        for c in range(first, first + count):
            at = wts.at[d, pl.ds(2 * c, 2)]
            pltpu.make_async_copy(at, at, load_sem.at[d, c]).wait()

    def forward(d, _):
        loaded(d, W_QKV, 3)
        hat, _ = ln_parts(xin[d])
        normed = (hat * gains[d, 0:1] + shifts[d, 0:1]).astype(BF)
        put_panel(acts, d, ACT_NORMED, normed)
        for c in range(3):
            put_panel(acts, d, ACT_Q + c, dot(normed, panel(wts, d, W_QKV + c)))
        for s in range(2):
            for quad in range(2):
                q = stacked(quarter(acts, d, ACT_Q, s, quad), HEAD_DIM**-0.5)
                k = quarter(acts, d, ACT_Q + 1, s, quad)
                v = quarter(acts, d, ACT_Q + 2, s, quad)
                scores = dot_lanes(q, k).reshape(4, 256, 256) + bias[s][None]
                top = jnp.max(scores, axis=-1, keepdims=True)
                e = jnp.exp(scores - top)
                total = jnp.sum(e, axis=-1, keepdims=True)
                p = (e * (1.0 / total)).astype(BF)
                for h in range(4):
                    put_quarter(acts, d, ACT_PROBS + s * 2 + quad, h // 2, h % 2, p[h])
                out = unstacked(dot(p.reshape(1024, 256), v))
                put_quarter(acts, d, ACT_ATT, s, quad, out)
        loaded(d, W_OUT, 1)
        middle = xin[d] + dot(panel(acts, d, ACT_ATT), panel(wts, d, W_OUT))
        mid[d] = middle
        loaded(d, W_UP, 4)
        hat, _ = ln_parts(middle)
        put_panel(acts, d, ACT_NORMED2, hat * gains[d, 1:2] + shifts[d, 1:2])

        def chunk(c, _):
            value, grad = gelu_pair(dot(panel(acts, d, ACT_NORMED2), panel(wts, d, W_UP + c)))
            put_panel(acts, d, ACT_GATED + c, value)
            put_panel(acts, d, ACT_SLOPE + c, grad)
            return 0

        lax.fori_loop(0, 4, chunk, 0)
        loaded(d, W_DOWN, 4)
        down = wts[d, pl.ds(2 * W_DOWN, 8)].reshape(4 * WIDTH, WIDTH)
        xin[d + 1] = mid[d] + dot(side_by_side(acts, d, ACT_GATED, 4), down)
        return 0

    lax.fori_loop(0, 2, forward, 0)
    act_mine[...] = xin[2].astype(BF)
    cot_copy.wait()
    act_copy.start()
    up = xin.at[2]
    for s in range(2):
        up[pl.ds(s * 256, 252), :] = cot[s].astype(F32)
        up[pl.ds(s * 256 + 252, 4), :] = jnp.zeros((4, WIDTH), F32)
    lng[...] = jnp.zeros_like(lng)

    def sems(k):
        return pair_sem.at[k], send_sem.at[k], recv_sem.at[k]

    def hop_rows(step):
        return pl.ds(0, 32 if step else 16)

    def piece1(k, first, hop_at):
        return Piece(
            lambda c: g1st.at[pl.ds(c * 12 + first, 4)],
            pair1.at[pl.ds(first, 4)],
            lambda way, step: hop1.at[hop_at + step, pl.ds(4 * way, 4), hop_rows(step), :],
            mine1.at[pl.ds(first, 4)], sems(k),
        )

    def piece0(k, first, hop_at):
        return Piece(
            lambda c: acts.at[1, pl.ds(c * 12 + first, 4)],
            acts.at[1, pl.ds(24 + first, 4)],
            lambda way, step: wts.at[1, hop_at + step, pl.ds(4 * way, 4), hop_rows(step), :],
            mine0.at[pl.ds(first, 4)], sems(k),
        )

    def crossing(mine, theirs, first, k):
        return mine.at[pl.ds(first, 4)], theirs.at[pl.ds(first, 4)], cross_sem.at[k]

    down1 = Stream([piece1(0, W_DOWN, 0)], [crossing(mine1, theirs1, W_DOWN, 2)])
    up1 = Stream([piece1(1, W_UP, HOPS)], [crossing(mine1, theirs1, W_UP, 3)])
    att1 = Stream([piece1(2, 0, 2 * HOPS)], [crossing(mine1, theirs1, 0, 4)])
    down0 = Stream([piece0(3, W_DOWN, 0)], [crossing(mine0, theirs0, W_DOWN, 5)])
    up0 = Stream([piece0(4, W_UP, HOPS)], [crossing(mine0, theirs0, W_UP, 6)])
    norms = Piece(
        lambda c: lnown.at[c], lnpair, lambda way, step: lnhop.at[way, step, :, hop_rows(step), :], lnmine, sems(5)
    )
    att0 = Stream(
        [piece0(6, 0, 2 * HOPS), norms],
        [crossing(mine0, theirs0, 0, 7), (lnmine, lntheirs, cross_sem.at[8])],
    )
    encoder = Stream(
        [
            Piece(
                lambda c: genc.at[c], wts.at[1, pl.ds(21, 3)],
                lambda way, step: wts.at[1, 3 * HOPS + step, pl.ds(4 * way, 3), hop_rows(step), :],
                enc_mine, sems(7),
            ),
            Piece(
                lambda c: miscown.at[c], miscpair, lambda way, step: mischop.at[way, step, :, hop_rows(step), :],
                miscmine, sems(8),
            ),
        ],
        [],
    )
    traffic = Traffic(PLAN)

    def backward(d, put, put_down, streams, before):
        down = up[...].astype(BF)
        for c in range(4):
            part = dot_rows(panel(acts, d, ACT_GATED + c), down).astype(BF).reshape(4, 4, 32, WIDTH)
            put_down(c, part)
            traffic.tick()
        before()
        streams[0].pair()
        for c in range(4):
            back = dot_lanes(down, panel(wts, d, W_DOWN + c))
            back = (back * panel(acts, d, ACT_SLOPE + c).astype(F32)).astype(BF)
            put_panel(acts, d, ACT_SLOPE + c, back)
            put(W_UP + c, dot_rows(panel(acts, d, ACT_NORMED2), back))
            traffic.tick()
        streams[1].pair()
        traffic.open(streams[0])
        back = dot_lanes(side_by_side(acts, d, ACT_SLOPE, 4), side_by_side(wts, d, W_UP, 4))
        back, gain, shift = ln_back(mid[d], back, gains[d, 1:2])
        lng[pl.ds(d * 4 + 1, 1), :] = gain
        lng[pl.ds(d * 4 + 3, 1), :] = shift
        up[...] += back
        branch = up[...].astype(BF)
        put(W_OUT, dot_rows(panel(acts, d, ACT_ATT), branch))
        back_att[...] = dot_lanes(branch, panel(wts, d, W_OUT)).astype(BF)
        traffic.open(streams[1])
        for s in range(2):
            for quad in range(2):
                rows, lanes = pl.ds(s * 256, 256), pl.ds(quad * 256, 256)
                qs = stacked(quarter(acts, d, ACT_Q, s, quad), HEAD_DIM**-0.5)
                k = quarter(acts, d, ACT_Q + 1, s, quad)
                v = quarter(acts, d, ACT_Q + 2, s, quad)
                outs = stacked(back_att[rows, lanes], 1.0)
                at = ACT_PROBS + s * 2 + quad
                p = jnp.concatenate([quarter(acts, d, at, h // 2, h % 2) for h in range(4)], axis=0)
                dp = dot_lanes(outs, v)
                pf = p.astype(F32)
                weighted = pf * dp
                total = jnp.sum(weighted, axis=-1, keepdims=True)
                ds = (weighted - pf * total).astype(BF)
                put_quarter(acts, d, ACT_Q, s, quad, unstacked(dot(ds, k)) * HEAD_DIM**-0.5)
                put_quarter(acts, d, ACT_Q + 1, s, quad, dot_rows(ds, qs))
                put_quarter(acts, d, ACT_Q + 2, s, quad, dot_rows(p, outs))
                traffic.tick()
        for c in range(3):
            put(c, dot_rows(panel(acts, d, ACT_NORMED), panel(acts, d, ACT_Q + c)))
        streams[2].pieces[0].pair_copy().start()
        traffic.tick()
        back = dot_lanes(side_by_side(acts, d, ACT_Q, 3), side_by_side(wts, d, W_QKV, 3))
        back, gain, shift = ln_back(xin[d], back, gains[d, 0:1])
        lng[pl.ds(d * 4, 1), :] = gain
        lng[pl.ds(d * 4 + 2, 1), :] = shift
        up[...] += back

    def split(value):
        return value.astype(BF).reshape(8, 2, 32, WIDTH)

    def put1(p, value):
        shaped = split(value)
        for c in range(2):
            g1st[c * 12 + p] = shaped[:, c]

    def put0(p, value):
        shaped = split(value)
        for c in range(2):
            acts[1, c * 12 + p] = shaped[:, c]

    def put_down1(c, part):
        for e in range(4):
            for j in range(4):
                g1st[(e % 2) * 12 + W_DOWN + j, 2 * c + e // 2] = part[e, j]

    def put_down0(c, part):
        for e in range(4):
            for j in range(4):
                acts[1, (e % 2) * 12 + W_DOWN + j, 2 * c + e // 2] = part[e, j]

    backward(1, put1, put_down1, (down1, up1, att1), lambda: None)
    for target in (sibling, ahead, behind):
        pl.semaphore_signal(free_sem, inc=1, device_id=(section, target), device_id_type=MESH)
    traffic.open(att1)
    traffic.tick()
    backward(0, put0, put_down0, (down0, up0, att0), lambda: pl.semaphore_wait(free_sem, 3))
    eg[...] = up[...].astype(BF)
    turned = jnp.transpose(lng[...]).astype(BF).reshape(8, 2, 32, 128)
    for c in range(2):
        lnown[c, 0] = turned[:, c]
    norms.pair_copy().start()

    def fetch(k):
        i, half, base = k // 2, k % 2, 16 * (k % 2)
        copies = []
        for n, (src, lanes) in enumerate(((xl_h, 256), (bl_h, 512), (z1_h, 512), (z2_h, 512))):
            copies.append(
                pltpu.make_async_copy(
                    src.at[i, pl.ds(4 * half, 4)],
                    acts.at[0, pl.ds(base + 4 * n, 4), pl.ds(0, 7), :, pl.ds(0, lanes)],
                    stream_sem.at[k % 2, n],
                )
            )
        return copies

    for copy in fetch(0):
        copy.start()
    traffic.open(att0)
    hot = jnp.where(iota((512, TABLE), 1) == ids[...], 1.0, 0.0).astype(BF)
    code = dot_rows(eg[...], hot)
    for c in range(2):
        for half in range(2):
            genc[c, 1 + half] = split(code[:, 512 * half : 512 * (half + 1)])[:, c]
        miscown[c, 0] = code[:, CODES:].astype(BF).reshape(8, 2, 32, 128)[:, c]
    dpool[...] = dot_rows(hot[:, POOL_AT : POOL_AT + 96], eg[...])
    traffic.tick()
    rows = 4 * BLOCK_ROWS

    def held(ref, d, at, lanes=512):
        return ref[d, pl.ds(at, 4), pl.ds(0, 7), :, pl.ds(0, lanes)].reshape(rows, lanes)

    for k in range(6):
        base = 16 * (k % 2)
        for copy in fetch(k):
            copy.wait()
        if k < 5:
            for copy in fetch(k + 1):
                copy.start()
        pooled = dpool[pl.ds((k // 2) * 32, FRAMES_BLOCK), :] * (1.0 / 64.0)
        wide = jnp.broadcast_to(pooled[:, None, :], (FRAMES_BLOCK, 8, WIDTH))
        wide = wide.reshape(BLOCK_ROWS, WIDTH)

        def part(bx, _):
            value = acts[0, base + 12 + bx, pl.ds(0, 7)].reshape(BLOCK_ROWS, WIDTH)
            back = (wide * gelu_slope(value)).astype(BF)
            wts[0, bx, pl.ds(0, 7)] = back.reshape(7, 32, WIDTH)
            value = acts[0, base + 8 + bx, pl.ds(0, 7)].reshape(BLOCK_ROWS, WIDTH)
            back = (dot_lanes(back, w2[...]) * gelu_slope(value)).astype(BF)
            wts[0, 4 + bx, pl.ds(0, 7)] = back.reshape(7, 32, WIDTH)
            return 0

        lax.fori_loop(0, 4, part, 0)
        traffic.tick()
        second = dot_rows(held(wts, 0, 0), held(acts, 0, base + 4))
        back = held(wts, 0, 4)
        patch = held(acts, 0, base, 256)
        first = [
            dot_rows(patch[:, 128 * dy2 : 128 * (dy2 + 1)], back[:, 256 * dy2 : 256 * (dy2 + 1)])
            for dy2 in range(2)
        ]
        first = first[0] + first[1]
        if k == 0:
            acc2[...] = second
            acc1[...] = first
        else:
            acc2[...] += second
            acc1[...] += first
        traffic.tick()
    shaped = split(acc2[...])
    hot, rest = patch_index(128)
    first = jnp.where(rest[:, :1] < 12, acc1[:, pl.ds(0, 128)], acc1[:, pl.ds(128, 128)])
    first = lax.dot_general(
        first, hot, (((0,), (0,)), ((), ())), preferred_element_type=F32,
        precision=lax.Precision.HIGHEST,
    )
    first = first.reshape(8, 2, 8, 48)
    first = jnp.concatenate([first, jnp.zeros((8, 2, 24, 48), F32)], axis=2).astype(BF)
    for c in range(2):
        genc[c, 0] = shaped[:, c]
        miscown[c, 0, :, :, pl.ds(64, 48)] = first[:, c]
    encoder.pair()
    traffic.tick()
    traffic.open(encoder)
    traffic.finish()
    for stream in (down1, up1, att1, down0, up0, att0):
        for crossed in stream.crossings:
            cross_copy(*crossed).wait()
    act_copy.wait()
    act[...] = act_theirs[...]
    late[...] = theirs1[...]
    early[...] = theirs0[...]
    norm[...] = lntheirs[0]
    enc[...] = enc_mine[...]
    misc[...] = miscmine[0]


def train(tok, cot, lens, gains, shifts, wq, wo, wu, wd, xl, bl, g1, g2, w2, ids):
    vm = pl.BlockSpec(memory_space=pltpu.VMEM)
    sm = pl.BlockSpec(memory_space=pltpu.SMEM)
    hb = pl.BlockSpec(memory_space=pl.ANY)

    def panels(w):
        return w.reshape(2, w.shape[1] // 256, 8, 32, w.shape[2])

    def parts(saved):
        return saved.reshape(saved.shape[0], 8, 7, 32, saved.shape[2])

    half = (8, 32, WIDTH)
    pieces = 9
    return pl.pallas_call(
        train_kernel,
        in_specs=[vm, hb, sm, vm, vm] + [hb] * 8 + [vm, vm],
        out_specs=[vm] * 7,
        out_shape=[
            jax.ShapeDtypeStruct((512, WIDTH), BF),
            jax.ShapeDtypeStruct((512, WIDTH), BF),
            jax.ShapeDtypeStruct((12, 32, WIDTH), BF),
            jax.ShapeDtypeStruct((12, 32, WIDTH), BF),
            jax.ShapeDtypeStruct((32, 128), BF),
            jax.ShapeDtypeStruct((3, 32, WIDTH), BF),
            jax.ShapeDtypeStruct((32, 128), BF),
        ],
        scratch_shapes=[
            pltpu.VMEM((2, 2 * W_PANELS) + half, BF),
            pltpu.VMEM((2, 2 * ACT_PANELS) + half, BF),
            pltpu.VMEM((24,) + half, BF),
            pltpu.VMEM((12,) + half, BF),
            pltpu.VMEM((3 * HOPS,) + half, BF),
            pltpu.VMEM((3, 512, WIDTH), F32),
            pltpu.VMEM((2, 512, WIDTH), F32),
            pltpu.VMEM((2, 256, 256), F32),
            pltpu.VMEM((512, WIDTH), BF),
            pltpu.VMEM((128, WIDTH), F32),
            pltpu.VMEM(cot.shape, BF),
            pltpu.VMEM((512, WIDTH), BF),
            pltpu.VMEM((512, WIDTH), BF),
            pltpu.VMEM((12, 32, WIDTH), BF),
            pltpu.VMEM((12, 32, WIDTH), BF),
            pltpu.VMEM((12, 32, WIDTH), BF),
            pltpu.VMEM((12, 32, WIDTH), BF),
            pltpu.VMEM((2, 1, 8, 32, 128), BF),
            pltpu.VMEM((1, 8, 32, 128), BF),
            pltpu.VMEM((2, HOPS, 1, 32, 128), BF),
            pltpu.VMEM((1, 32, 128), BF),
            pltpu.VMEM((1, 32, 128), BF),
            pltpu.VMEM((2, 3) + half, BF),
            pltpu.VMEM((3, 32, WIDTH), BF),
            pltpu.VMEM((2, 1, 8, 32, 128), BF),
            pltpu.VMEM((1, 8, 32, 128), BF),
            pltpu.VMEM((2, HOPS, 1, 32, 128), BF),
            pltpu.VMEM((1, 32, 128), BF),
            pltpu.VMEM((512, WIDTH), F32),
            pltpu.VMEM((128, 256), F32),
            pltpu.VMEM((96, WIDTH), F32),
            pltpu.SemaphoreType.DMA((2, W_PANELS)),
            pltpu.SemaphoreType.DMA((2, 4)),
            pltpu.SemaphoreType.DMA((9, 2)),
            pltpu.SemaphoreType.DMA((pieces, 2)),
            pltpu.SemaphoreType.DMA((pieces, 2, HOPS)),
            pltpu.SemaphoreType.DMA((pieces, 2, HOPS)),
            pltpu.SemaphoreType.REGULAR,
        ],
        compiler_params=pltpu.CompilerParams(
            collective_id=2, has_side_effects=True, vmem_limit_bytes=TRAIN_VMEM
        ),
        name="train",
    )(
        tok, cot, lens, gains, shifts, panels(wq), panels(wo), panels(wu), panels(wd),
        parts(xl), parts(bl), parts(g1), parts(g2), w2, ids,
    )


def outputs_kernel(act_in, eg_in, late, early, norm, enc, misc, *outs):
    act, eg, qkv, out, up, down, gain, bias, bias2, enc1, enc2, book, names = outs
    for s in range(2):
        act[0, s] = act_in[pl.ds(s * 256, 256), :].astype(F32)[:252].astype(BF)
        eg[0, s] = eg_in[pl.ds(s * 256, 256), :].astype(F32)[:252].astype(BF)
    for d, rows in enumerate((early, late)):
        for c in range(3):
            qkv[0, d, :, pl.ds(512 * c, 512)] = rows[W_QKV + c].astype(F32)
        out[0, d] = rows[W_OUT].astype(F32)
        for c in range(4):
            up[0, d, :, pl.ds(512 * c, 512)] = rows[W_UP + c].astype(F32)
            down[0, d, pl.ds(32 * c, 32), :] = rows[W_DOWN + c].astype(F32)
    turned = turn(norm[...].astype(F32))
    for d in range(2):
        gain[0, d] = turned[4 * d : 4 * d + 2]
        bias[0, pl.ds(d, 1)] = turned[4 * d + 2 : 4 * d + 3]
        bias2[0, pl.ds(d, 1)] = turned[4 * d + 3 : 4 * d + 4]
    enc2[0] = enc[0].astype(F32)
    for c in range(2):
        book[0, :, pl.ds(512 * c, 512)] = enc[1 + c].astype(F32)
    enc1[0] = misc[...].astype(F32)[:8, 64:112]
    turned = turn(misc[...].astype(F32))
    for a in range(17):
        names[a] = turned[a : a + 1]


def spread_outputs(*parts):
    vm = pl.BlockSpec(memory_space=pltpu.VMEM)
    shapes = [
        (1, 2, 32, 1536), (1, 2, 32, 512), (1, 2, 32, 2048), (1, 2, 128, 512), (1, 2, 2, 32),
        (1, 2, 32), (1, 2, 32), (1, 8, 48), (1, 32, 512), (1, 32, 1024), (17, 1, 32),
    ]
    acts = [jax.ShapeDtypeStruct((1, 2, 252, WIDTH), BF)] * 2
    outs = pl.pallas_call(
        outputs_kernel,
        in_specs=[vm] * len(parts),
        out_specs=[vm] * (len(shapes) + 2),
        out_shape=acts + [jax.ShapeDtypeStruct(shape, F32) for shape in shapes],
        compiler_params=pltpu.CompilerParams(vmem_limit_bytes=VMEM_LIMIT),
        name="outputs",
    )(*parts)
    outs = list(outs)
    outs[6] = outs[6].transpose(0, 1, 3, 2)
    for k in (9, 10, 11):
        outs[k] = outs[k].transpose(0, 2, 1)
    outs[12] = outs[12].transpose(1, 0, 2)
    return tuple(outs)


def swap(array):
    return lax.ppermute(array, "section", [(0, 1), (1, 0)])


def whole_rows(g):
    return g.transpose(1, 0, 2, 3).reshape(512, g.shape[-1])


def scatter_plain(g, gl, e):
    def sums(array, axis):
        return lax.psum_scatter(array.astype(F32)[None], "dp", scatter_dimension=axis, tiled=True)

    layers = [whole_rows(g[d]) for d in range(g.shape[0])]
    qkv = jnp.stack([rows[:, :1536] for rows in layers])
    out = jnp.stack([rows[:, 1536:2048] for rows in layers])
    up = jnp.stack([rows[:, 2048:4096] for rows in layers])
    down = jnp.stack(
        [
            rows[:, 4096:].reshape(16, 32, 4, WIDTH).transpose(0, 2, 1, 3).reshape(2048, WIDTH)
            for rows in layers
        ]
    )
    norm = whole_rows(gl)[:, :8].reshape(512, 2, 4).transpose(1, 0, 2)
    enc = whole_rows(e)
    first = e.transpose(1, 0, 2, 3)[:, :, :8, 1600:1648].reshape(128, 48)
    layer_sums = [sums(x, 2) for x in (qkv, out, up, down, norm)]
    layer_sums = [swap(x) for x in layer_sums]
    norm = layer_sums.pop()
    return tuple(layer_sums) + (
        norm[..., 0:2],
        norm[..., 2],
        norm[..., 3],
        sums(first.T, 2),
        sums(enc[:, :512].T, 2),
        sums(enc[:, 512:1536].T, 2),
        sums(enc[:, 1536:1553].T, 2),
    )


def on_device(
    frames, action_ids, delta_ids, seq_len, enc_w1, enc_w2, codebook, action_table,
    ln_gain, ln_bias, w_qkv, w_out, w_up, w_down, cotangent,
):
    micro, steps = frames.shape[1], frames.shape[2]
    count = micro * steps
    gains, shifts = ln_gain.transpose(0, 2, 1), ln_bias.transpose(0, 2, 1)
    tok, ids, xl, blocks, z1, z2 = enc_forward(
        frames.reshape((count,) + frames.shape[3:]), enc_w1, enc_w2, codebook, action_table,
        action_ids[0], delta_ids[0].transpose(0, 2, 1),
    )
    if lax.axis_size("dp") == 2 * CHIPS:
        parts = train(
            tok, cotangent[0], seq_len, gains, shifts, w_qkv, w_out, w_up, w_down,
            xl, blocks, z1, z2, enc_w2, ids,
        )
        return spread_outputs(*parts)
    lnp = jnp.concatenate([gains, shifts], axis=1)
    act, eg, g, gl = run_layers(tok, cotangent[0], seq_len, lnp, w_qkv, w_out, w_up, w_down)
    embed_grad = eg.reshape(micro, 256, WIDTH)[None, :, : steps * TPS]
    e = enc_backward(eg, xl, blocks, z1, z2, enc_w2, ids)
    return (act[None], embed_grad) + scatter_plain(g, gl, e)


def solution(mesh):
    return jax.shard_map(
        on_device,
        mesh=mesh,
        in_specs=(
            P("section", "dp", None, None, None),
            P("section", "dp", None),
            P("section", "dp", None, None),
            P(None, "dp"),
            P(), P(), P(), P(), P(), P(), P(), P(), P(), P(),
            P("section", "dp", None, None),
        ),
        out_specs=(
            P("section", "dp", None, None),
            P("section", "dp", None, None),
            P("section", None, "dp", None),
            P("section", None, "dp", None),
            P("section", None, "dp", None),
            P("section", None, "dp", None),
            P("section", None, "dp", None),
            P("section", None, "dp"),
            P("section", None, "dp"),
            P("section", None, "dp"),
            P("section", None, "dp"),
            P("section", None, "dp"),
            P("section", None, "dp"),
        ),
        check_vma=False,
    )
```

```python
import functools

import jax
import jax.numpy as jnp
from jax import lax
from jax.experimental import pallas as pl
from jax.experimental.pallas import tpu as pltpu
from jax.sharding import PartitionSpec as P

HEADS = 8
HEAD_DIM = 64
TPS = 6
EPS = 1e-05
BF = jnp.bfloat16
F32 = jnp.float32
I32 = jnp.int32

WIDTH = 512
CODES = 1024
FRAMES_BLOCK = 28
BLOCK_ROWS = FRAMES_BLOCK * 8
TABLE = 1152
POOL_AT = 1056
ACT_AT = 1024
LAYER_COLS = 6144
ENC_COLS = 1664
VMEM_LIMIT = 60 << 20
TRAIN_VMEM = 63 << 20
PLAN = "00000000010111000000001111110101010101012"


def dot(a, b):
    return jnp.dot(a, b, preferred_element_type=F32)


def dot_rows(a, b):
    return lax.dot_general(a, b, (((0,), (0,)), ((), ())), preferred_element_type=F32)


def dot_lanes(a, b):
    return lax.dot_general(a, b, (((1,), (1,)), ((), ())), preferred_element_type=F32)


def iota(shape, axis):
    return lax.broadcasted_iota(I32, shape, axis)


def gelu_pair(v):
    cdf = 0.5 + 0.5 * lax.erf(v * 0.7071067811865476)
    bell = jnp.exp2(v * v * (-0.5 * 1.4426950408889634))
    return v * cdf, cdf + v * (bell * 0.3989422804014327)


def gelu(v):
    return v * (0.5 + 0.5 * lax.erf(v * 0.7071067811865476))


def gelu_slope(v):
    return gelu_pair(v.astype(F32))[1]


def patch_index(rows):
    k = iota((rows, 48), 0)
    dy = (k * 2731) >> 16
    rest = k - dy * 24
    j = jnp.where(rest >= 12, rest - 12, rest)
    return jnp.where((iota((rows, 48), 1) == dy * 12 + j) & (k < 96), 1.0, 0.0), rest


def encoder_weights(w1):
    hot, rest = patch_index(128)
    wide = dot(hot.astype(BF), w1)
    first = jnp.where(rest[:, :1] < 12, wide, 0.0)
    second = jnp.where(rest[:, :1] >= 12, wide, 0.0)
    block = jnp.concatenate([first, second], axis=1)
    zero = jnp.zeros_like(block)
    return jnp.concatenate(
        [jnp.concatenate([block, zero], axis=1), jnp.concatenate([zero, block], axis=1)], axis=0
    ).astype(BF)


def token_ids(s, names, deltas):
    steps = names.shape[1]
    frame = s * steps + iota((1, steps), 1)
    block = (frame * 2341) >> 16
    pool = POOL_AT + block * 32 + frame - FRAMES_BLOCK * block
    kinds = jnp.concatenate([pool, names[s : s + 1] + ACT_AT, deltas[s]], axis=0).astype(F32)
    row = iota((256, 1), 0)
    step = (row * 10923) >> 16
    hot = jnp.where(iota((256, steps), 1) == step, 1.0, 0.0)
    each = lax.dot_general(
        hot, kinds, (((1,), (1,)), ((), ())), preferred_element_type=F32,
        precision=lax.Precision.HIGHEST,
    )
    mine = jnp.where(iota((256, TPS), 1) == row - TPS * step, each, 0.0)
    found = (jnp.sum(mine, axis=1, keepdims=True) + 0.5).astype(I32)
    return jnp.where(row < TPS * steps, found, -1)


def enc_fwd_kernel(
    frames, w1, w2, book, acts, names, deltas,
    tok, ids, xl, blocks, z1, z2, perm, lanes, big, xs, acc, table,
):
    step = pl.program_id(0)

    @pl.when(step == 0)
    def _():
        a, b = iota((256, 256), 0), iota((256, 256), 1)
        perm[...] = jnp.where(b == 8 * (a & 31) + (a >> 5), 1.0, 0.0).astype(BF)
        src = iota((256, 1024), 0)
        px = (src * 5462) >> 16
        at = (px >> 1) * 128 + (px & 1) * 12 + (src - px * 12)
        out = jnp.where(src < 192, iota((256, 1024), 1) - at, -1)
        for dy in range(4):
            lanes[pl.ds(256 * dy, 256), :] = jnp.where(out == dy * 24, 1.0, 0.0).astype(BF)
        xs[...] = jnp.zeros_like(xs)
        big[...] = encoder_weights(w1[...])
        table[pl.ds(0, CODES), :] = book[...]
        named = acts[...].astype(F32)
        pad = jnp.zeros((TABLE - ACT_AT - named.shape[0], WIDTH), F32)
        table[pl.ds(ACT_AT, TABLE - ACT_AT), :] = jnp.concatenate([named, pad], axis=0).astype(BF)

    for group in range(FRAMES_BLOCK // 4):
        rows = frames[pl.ds(group * 4, 4)].reshape(256, 192)
        moved = dot(perm[...], rows).astype(BF).reshape(2, 4, 32, 192)
        for dy in range(4):
            xs[:, pl.ds(group * 32, 32), pl.ds(256 * dy, 192)] = moved[:, dy]
    for dy2 in range(2):
        spread = dot(xs[dy2], lanes[...]).astype(BF)
        for bx in range(8):
            xl[0, pl.ds(bx * BLOCK_ROWS, BLOCK_ROWS), pl.ds(dy2 * 128, 128)] = spread[
                :, bx * 128 : (bx + 1) * 128
            ]
    acc[...] = jnp.zeros_like(acc)

    def part(bx, _):
        rows = pl.ds(pl.multiple_of(bx * BLOCK_ROWS, BLOCK_ROWS), BLOCK_ROWS)
        first = dot(xl[0, rows, :], big[...])
        z1[0, rows, :] = first.astype(BF)
        value = gelu(first).astype(BF)
        blocks[0, rows, :] = value
        second = dot(value, w2[...])
        z2[0, rows, :] = second.astype(BF)
        acc[...] += gelu(second)
        return 0

    lax.fori_loop(0, 8, part, 0, unroll=True)
    pooled = jnp.sum(acc[...].reshape(FRAMES_BLOCK, 8, WIDTH), axis=1) * (1.0 / 64.0)
    pooled = jnp.concatenate([pooled, jnp.zeros((32 - FRAMES_BLOCK, WIDTH), F32)], axis=0)
    table[pl.ds(pl.multiple_of(POOL_AT + step * 32, 32), 32), :] = pooled.astype(BF)

    @pl.when(step == pl.num_programs(0) - 1)
    def _():
        for s in range(2):
            rows = pl.ds(s * 256, 256)
            found = token_ids(s, names[...], deltas[...])
            ids[rows, :] = found
            hot = jnp.where(iota((256, TABLE), 1) == found, 1.0, 0.0).astype(BF)
            tok[rows, :] = dot(hot, table[...]).astype(BF)


def enc_forward(frames, w1, w2, book, acts, names, deltas):
    count = frames.shape[0]
    grid = count // FRAMES_BLOCK
    rows = 8 * BLOCK_ROWS

    def whole(shape):
        return pl.BlockSpec(shape, lambda i: (0,) * len(shape))

    def saved(lanes):
        return pl.BlockSpec((1, rows, lanes), lambda i: (i, 0, 0))

    return pl.pallas_call(
        enc_fwd_kernel,
        grid=(grid,),
        in_specs=[
            pl.BlockSpec((FRAMES_BLOCK, 64, 192), lambda i: (i, 0, 0)),
            whole(w1.shape),
            whole(w2.shape),
            whole(book.shape),
            whole(acts.shape),
            whole(names.shape),
            whole(deltas.shape),
        ],
        out_specs=[
            whole((512, WIDTH)), whole((512, 1)), saved(256), saved(512), saved(512), saved(512),
        ],
        out_shape=[
            jax.ShapeDtypeStruct((512, WIDTH), BF),
            jax.ShapeDtypeStruct((512, 1), I32),
            jax.ShapeDtypeStruct((grid, rows, 256), BF),
            jax.ShapeDtypeStruct((grid, rows, 512), BF),
            jax.ShapeDtypeStruct((grid, rows, 512), BF),
            jax.ShapeDtypeStruct((grid, rows, 512), BF),
        ],
        scratch_shapes=[
            pltpu.VMEM((256, 256), BF),
            pltpu.VMEM((1024, 1024), BF),
            pltpu.VMEM((256, 512), BF),
            pltpu.VMEM((2, BLOCK_ROWS, 1024), BF),
            pltpu.VMEM((BLOCK_ROWS, WIDTH), F32),
            pltpu.VMEM((TABLE, WIDTH), BF),
        ],
        compiler_params=pltpu.CompilerParams(vmem_limit_bytes=VMEM_LIMIT),
        name="enc_fwd",
    )(frames, w1, w2, book, acts, names, deltas)


def ln_parts(x):
    mean = jnp.mean(x, axis=-1, keepdims=True)
    center = x - mean
    var = jnp.mean(center * center, axis=-1, keepdims=True)
    scale = lax.rsqrt(var + EPS)
    return center * scale, scale


def ln_back(x, d, gain):
    hat, scale = ln_parts(x)
    dh = d * gain
    one = jnp.mean(dh, axis=-1, keepdims=True)
    two = jnp.mean(dh * hat, axis=-1, keepdims=True)
    back = scale * (dh - one - hat * two)
    return back, jnp.sum(d * hat, axis=0, keepdims=True), jnp.sum(d, axis=0, keepdims=True)


def head_mask(h):
    lane = iota((1, 256), 1) >> 6
    return lane == h


def stacked(rows, scale):
    out = []
    for h in range(4):
        mask = jnp.where(head_mask(h), scale, 0.0).astype(BF)
        out.append(rows * mask)
    return jnp.concatenate(out, axis=0)


def unstacked(rows):
    out = rows[768:]
    for h in range(3):
        out = jnp.where(head_mask(h), rows[h * 256 : (h + 1) * 256], out)
    return out


def scatter_rows(g, d, cols, value, dests=16):
    shaped = value.astype(BF).reshape(dests // 2, 2, 32, value.shape[1])
    for core in range(2):
        g[d, core, :, :, cols] = shaped[:, core]


def layers_kernel(
    tok, cot_h, lens, lnp, wq_h, wo_h, wu_h, wd_h,
    act, eg, g, gl,
    wq, wo, wu, wd, stream, normed, packed, probs, att, normed2, gated, slope, bias,
    up, back_up, back_att, back_packed, lng, cot, mine, theirs, sems, cross_sem,
):
    layers = wq.shape[0]
    section = lax.axis_index("section")
    barrier = pltpu.get_barrier_semaphore()
    pl.semaphore_signal(
        barrier, inc=1, device_id=(1 - section, lax.axis_index("dp")), device_id_type=MESH
    )
    pl.semaphore_wait(barrier, 1)
    cot_copy = cross_copy(cot_h, cot, cross_sem.at[0])
    cot_copy.start()
    act_copy = cross_copy(mine, theirs, cross_sem.at[1])
    copies = []
    for d in range(layers):
        for k, (src, dst) in enumerate(((wq_h, wq), (wo_h, wo), (wu_h, wu), (wd_h, wd))):
            copy = pltpu.make_async_copy(src.at[d], dst.at[d], sems.at[d, k])
            copy.start()
            copies.append(copy)

    stream[0, 0] = tok[...].astype(F32)
    row = iota((256, 1), 0)
    col = iota((1, 256), 1)
    q_step = ((row * 10923) >> 16).astype(F32)
    k_step = ((col * 10923) >> 16).astype(F32)
    for s in range(2):
        inv = 1.0 / lens[section, s].astype(F32)
        q_seq = jnp.floor((q_step + 0.5) * inv)
        k_seq = jnp.floor((k_step + 0.5) * inv)
        bias[s] = jnp.where((k_step <= q_step) & (q_seq == k_seq), 0.0, -1e30)
    for copy in copies:
        copy.wait()

    def forward(d, _):
        x = stream[d, 0]
        hat, _ = ln_parts(x)
        normed[d] = (hat * lnp[d, 0:1] + lnp[d, 2:3]).astype(BF)
        for c in range(3):
            cols = pl.ds(c * 512, 512)
            packed[d, :, cols] = dot(normed[d], wq[d, :, cols]).astype(BF)
        for s in range(2):
            rows = pl.ds(s * 256, 256)
            for quad in range(2):
                q = stacked(packed[d, rows, pl.ds(quad * 256, 256)], HEAD_DIM**-0.5)
                k = packed[d, rows, pl.ds(512 + quad * 256, 256)]
                v = packed[d, rows, pl.ds(1024 + quad * 256, 256)]
                scores = dot_lanes(q, k).reshape(4, 256, 256) + bias[s][None]
                top = jnp.max(scores, axis=-1, keepdims=True)
                e = jnp.exp(scores - top)
                total = jnp.sum(e, axis=-1, keepdims=True)
                p = (e * (1.0 / total)).astype(BF).reshape(1024, 256)
                probs[d, s * 2 + quad] = p
                att[d, rows, pl.ds(quad * 256, 256)] = unstacked(dot(p, v)).astype(BF)
        middle = stream[d, 0] + dot(att[d], wo[d])
        stream[d, 1] = middle
        hat, _ = ln_parts(middle)
        normed2[d] = (hat * lnp[d, 1:2] + lnp[d, 3:4]).astype(BF)

        def chunk(c, _):
            cols = pl.ds(pl.multiple_of(c * 512, 512), 512)
            value, grad = gelu_pair(dot(normed2[d], wu[d, :, cols]))
            gated[d, :, cols] = value.astype(BF)
            slope[d, :, cols] = grad.astype(BF)
            return 0

        lax.fori_loop(0, 4, chunk, 0)
        stream[d + 1, 0] = stream[d, 1] + dot(gated[d], wd[d])
        return 0

    lax.fori_loop(0, layers, forward, 0)
    cot_copy.wait()
    mine[...] = stream[layers, 0].astype(BF)
    act_copy.start()
    for s in range(2):
        up[pl.ds(s * 256, 252), :] = cot[s].astype(F32)
        up[pl.ds(s * 256 + 252, 4), :] = jnp.zeros((4, WIDTH), F32)
    lng[...] = jnp.zeros_like(lng)

    def backward(i, _):
        d = layers - 1 - i
        down = up[...].astype(BF)

        def chunk(c, _):
            cols = pl.ds(pl.multiple_of(c * 256, 256), 256)
            part = dot_rows(gated[d, :, cols], down).astype(BF).reshape(2, 4, 32, WIDTH)
            for core in range(2):
                for j in range(4):
                    g[d, core, c, :, pl.ds(4096 + 512 * j, 512)] = part[core, j]
            back = dot_lanes(down, wd[d, cols, :])
            back = (back * slope[d, :, cols].astype(F32)).astype(BF)
            back_up[:, cols] = back
            part = dot_rows(normed2[d], back).astype(BF).reshape(8, 2, 32, 256)
            out = pl.ds(pl.multiple_of(2048 + c * 256, 256), 256)
            for core in range(2):
                g[d, core, :, :, out] = part[:, core]
            return 0

        lax.fori_loop(0, 8, chunk, 0)
        back, gain, shift = ln_back(stream[d, 1], dot_lanes(back_up[...], wu[d]), lnp[d, 1:2])
        lng[pl.ds(d * 4 + 1, 1), :] = gain
        lng[pl.ds(d * 4 + 3, 1), :] = shift
        up[...] += back
        branch = up[...].astype(BF)
        scatter_rows(g, d, pl.ds(1536, 512), dot_rows(att[d], branch))
        back_att[...] = dot_lanes(branch, wo[d]).astype(BF)
        for s in range(2):
            rows = pl.ds(s * 256, 256)
            for quad in range(2):
                lanes = pl.ds(quad * 256, 256)
                qs = stacked(packed[d, rows, lanes], HEAD_DIM**-0.5)
                k = packed[d, rows, pl.ds(512 + quad * 256, 256)]
                v = packed[d, rows, pl.ds(1024 + quad * 256, 256)]
                outs = stacked(back_att[rows, lanes], 1.0)
                p = probs[d, s * 2 + quad]
                dp = dot_lanes(outs, v)
                pf = p.astype(F32)
                weighted = pf * dp
                total = jnp.sum(weighted, axis=-1, keepdims=True)
                ds = (weighted - pf * total).astype(BF)
                back_packed[rows, lanes] = (unstacked(dot(ds, k)) * HEAD_DIM**-0.5).astype(BF)
                back_packed[rows, pl.ds(512 + quad * 256, 256)] = dot_rows(ds, qs).astype(BF)
                back_packed[rows, pl.ds(1024 + quad * 256, 256)] = dot_rows(p, outs).astype(BF)
        for c in range(3):
            cols = pl.ds(c * 512, 512)
            scatter_rows(g, d, cols, dot_rows(normed[d], back_packed[:, cols]))
        back, gain, shift = ln_back(stream[d, 0], dot_lanes(back_packed[...], wq[d]), lnp[d, 0:1])
        lng[pl.ds(d * 4, 1), :] = gain
        lng[pl.ds(d * 4 + 2, 1), :] = shift
        up[...] += back
        return 0

    lax.fori_loop(0, layers, backward, 0)
    eg[...] = up[...].astype(BF)
    act_copy.wait()
    for s in range(2):
        act[s] = theirs[pl.ds(s * 256, 256), :].astype(F32)[:252].astype(BF)
    turned = jnp.transpose(lng[...]).astype(BF).reshape(8, 2, 32, 128)
    for core in range(2):
        gl[core] = turned[:, core]


def run_layers(tok, cot, lens, lnp, wq, wo, wu, wd):
    layers = wq.shape[0]
    vm = pl.BlockSpec(memory_space=pltpu.VMEM)
    sm = pl.BlockSpec(memory_space=pltpu.SMEM)
    hb = pl.BlockSpec(memory_space=pl.ANY)
    rows = 512
    return pl.pallas_call(
        layers_kernel,
        in_specs=[vm, hb, sm, vm, hb, hb, hb, hb],
        out_specs=[vm, vm, vm, vm],
        out_shape=[
            jax.ShapeDtypeStruct((2, 252, WIDTH), BF),
            jax.ShapeDtypeStruct((rows, WIDTH), BF),
            jax.ShapeDtypeStruct((layers, 2, 8, 32, LAYER_COLS), BF),
            jax.ShapeDtypeStruct((2, 8, 32, 128), BF),
        ],
        scratch_shapes=[
            pltpu.VMEM(wq.shape, BF),
            pltpu.VMEM(wo.shape, BF),
            pltpu.VMEM(wu.shape, BF),
            pltpu.VMEM(wd.shape, BF),
            pltpu.VMEM((layers + 1, 2, rows, WIDTH), F32),
            pltpu.VMEM((layers, rows, WIDTH), BF),
            pltpu.VMEM((layers, rows, 3 * WIDTH), BF),
            pltpu.VMEM((layers, 4, 1024, 256), BF),
            pltpu.VMEM((layers, rows, WIDTH), BF),
            pltpu.VMEM((layers, rows, WIDTH), BF),
            pltpu.VMEM((layers, rows, 4 * WIDTH), BF),
            pltpu.VMEM((layers, rows, 4 * WIDTH), BF),
            pltpu.VMEM((2, 256, 256), F32),
            pltpu.VMEM((rows, WIDTH), F32),
            pltpu.VMEM((rows, 4 * WIDTH), BF),
            pltpu.VMEM((rows, WIDTH), BF),
            pltpu.VMEM((rows, 3 * WIDTH), BF),
            pltpu.VMEM((128, WIDTH), F32),
            pltpu.VMEM(cot.shape, BF),
            pltpu.VMEM((rows, WIDTH), BF),
            pltpu.VMEM((rows, WIDTH), BF),
            pltpu.SemaphoreType.DMA((layers, 4)),
            pltpu.SemaphoreType.DMA((2, 2)),
        ],
        compiler_params=pltpu.CompilerParams(
            collective_id=1, has_side_effects=True, vmem_limit_bytes=VMEM_LIMIT
        ),
        name="layers",
    )(tok, cot, lens, lnp, wq, wo, wu, wd)


def enc_bwd_kernel(eg, xl, blocks, g1, g2, w2, ids, e, dpool, bs, bf, acc2, acc1):
    step = pl.program_id(0)

    @pl.when(step == 0)
    def _():
        hot = jnp.where(iota((512, TABLE), 1) == ids[...], 1.0, 0.0).astype(BF)
        code = dot_rows(eg[...], hot[:, :POOL_AT + 96]).astype(BF)
        dpool[...] = dot_rows(hot[:, POOL_AT : POOL_AT + 96], eg[...])
        parts = code[:, :CODES].reshape(8, 2, 32, CODES)
        tail = code[:, CODES : CODES + 128].reshape(8, 2, 32, 128)
        for core in range(2):
            e[core, :, :, pl.ds(512, CODES)] = parts[:, core]
            e[core, :, :, pl.ds(1536, 128)] = tail[:, core]
        acc2[...] = jnp.zeros_like(acc2)
        acc1[...] = jnp.zeros_like(acc1)

    pooled = dpool[pl.ds(pl.multiple_of(step * 32, 32), 32), :][:FRAMES_BLOCK] * (1.0 / 64.0)
    wide = jnp.broadcast_to(pooled[:, None, :], (FRAMES_BLOCK, 8, WIDTH)).reshape(BLOCK_ROWS, WIDTH)

    def part(bx, _):
        rows = pl.ds(pl.multiple_of(bx * BLOCK_ROWS, BLOCK_ROWS), BLOCK_ROWS)
        back = (wide * gelu_slope(g2[0, rows, :])).astype(BF)
        bs[rows, :] = back
        bf[rows, :] = (dot_lanes(back, w2[...]) * gelu_slope(g1[0, rows, :])).astype(BF)
        return 0

    lax.fori_loop(0, 8, part, 0)
    acc2[...] += dot_rows(bs[...], blocks[0])
    for dy2 in range(2):
        acc1[:, pl.ds(dy2 * 256, 256)] += dot_rows(
            xl[0, :, pl.ds(dy2 * 128, 128)], bf[:, pl.ds(dy2 * 256, 256)]
        )

    @pl.when(step == pl.num_programs(0) - 1)
    def _():
        parts = acc2[...].astype(BF).reshape(8, 2, 32, WIDTH)
        both = acc1[:, pl.ds(0, 256)] + acc1[:, pl.ds(256, 256)]
        hot, rest = patch_index(128)
        first = jnp.where(rest[:, :1] < 12, both[:, :128], both[:, 128:])
        first = lax.dot_general(
            first, hot, (((0,), (0,)), ((), ())), preferred_element_type=F32,
            precision=lax.Precision.HIGHEST,
        )
        first = first.reshape(8, 2, 8, 48)
        first = jnp.concatenate([first, jnp.zeros((8, 2, 24, 48), F32)], axis=2).astype(BF)
        for core in range(2):
            e[core, :, :, pl.ds(0, WIDTH)] = parts[:, core]
            e[core, :, :, pl.ds(1536 + 64, 48)] = first[:, core]


def enc_backward(eg, xl, blocks, g1, g2, w2, ids):
    grid, rows, _ = xl.shape

    def whole(shape):
        return pl.BlockSpec(shape, lambda i: (0,) * len(shape))

    def saved(lanes):
        return pl.BlockSpec((1, rows, lanes), lambda i: (i, 0, 0))

    return pl.pallas_call(
        enc_bwd_kernel,
        grid=(grid,),
        in_specs=[
            whole(eg.shape), saved(256), saved(512), saved(512), saved(512),
            whole(w2.shape), whole(ids.shape),
        ],
        out_specs=whole((2, 8, 32, ENC_COLS)),
        out_shape=jax.ShapeDtypeStruct((2, 8, 32, ENC_COLS), BF),
        scratch_shapes=[
            pltpu.VMEM((96, WIDTH), F32),
            pltpu.VMEM((rows, WIDTH), BF),
            pltpu.VMEM((rows, WIDTH), BF),
            pltpu.VMEM((WIDTH, WIDTH), F32),
            pltpu.VMEM((128, WIDTH), F32),
        ],
        compiler_params=pltpu.CompilerParams(vmem_limit_bytes=VMEM_LIMIT),
        name="enc_bwd",
    )(eg, xl, blocks, g1, g2, w2, ids)


CHIPS = 8
HOPS = CHIPS // 2
MESH = pl.DeviceIdType.MESH


def ring_place(chip):
    z, x = chip // 2, chip % 2
    return z * (1 - x) + (7 - z) * x


def ring_chip(place):
    half = place // 4
    return (1 - half) * (2 * place) + half * (15 - 2 * place)


def where_am_i():
    section, me = lax.axis_index("section"), lax.axis_index("dp")
    core, chip = me % 2, me // 2
    place = ring_place(chip)
    ahead = ring_chip((place + 1) % CHIPS) * 2 + core
    behind = ring_chip((place + CHIPS - 1) % CHIPS) * 2 + core
    sibling = chip * 2 + (1 - core)
    return section, me, core, place, ahead, behind, sibling


def greet():
    section, me, _, _, ahead, behind, sibling = where_am_i()
    barrier = pltpu.get_barrier_semaphore()
    for target in ((section, sibling), (section, ahead), (section, behind), (1 - section, me)):
        pl.semaphore_signal(barrier, inc=1, device_id=target, device_id_type=MESH)
    pl.semaphore_wait(barrier, 4)


def cross_copy(src, dst, sem):
    section, me = lax.axis_index("section"), lax.axis_index("dp")
    return pltpu.make_async_remote_copy(
        src_ref=src, dst_ref=dst, send_sem=sem.at[0], recv_sem=sem.at[1],
        device_id=(1 - section, me), device_id_type=MESH,
    )


def turn(rows):
    tall = jnp.concatenate([rows, jnp.zeros((96, rows.shape[1]), F32)], axis=0)
    return jnp.transpose(tall)[:, :32]


ACT_NORMED, ACT_Q, ACT_PROBS, ACT_ATT, ACT_NORMED2, ACT_GATED, ACT_SLOPE = 0, 1, 4, 8, 9, 10, 14
ACT_PANELS = 18
W_QKV, W_OUT, W_UP, W_DOWN = 0, 3, 4, 8
W_PANELS = 12


def panel(ref, d, p):
    return ref[d, pl.ds(2 * p, 2)].reshape(512, WIDTH)


def put_panel(ref, d, p, value):
    ref[d, pl.ds(2 * p, 2)] = value.astype(BF).reshape(2, 8, 32, WIDTH)


def quarter(ref, d, p, s, quad):
    return ref[d, 2 * p + s, :, :, pl.ds(256 * quad, 256)].reshape(256, 256)


def put_quarter(ref, d, p, s, quad, value):
    ref[d, 2 * p + s, :, :, pl.ds(256 * quad, 256)] = value.astype(BF).reshape(8, 32, 256)


def side_by_side(ref, d, p, count):
    return jnp.concatenate([panel(ref, d, p + c) for c in range(count)], axis=1)


class Piece:
    def __init__(self, own, pair, hop, mine, sems):
        self.own, self.pair, self.hop, self.mine = own, pair, hop, mine
        self.pair_sem, self.send_sem, self.recv_sem = sems

    def pair_copy(self):
        section, _, core, _, _, _, sibling = where_am_i()
        return pltpu.make_async_remote_copy(
            src_ref=self.own(1 - core), dst_ref=self.pair,
            send_sem=self.pair_sem.at[0], recv_sem=self.pair_sem.at[1],
            device_id=(section, sibling), device_id_type=MESH,
        )

    def target(self, way, step):
        place, far = where_am_i()[3], HOPS - step
        return ring_chip((place + (far if way == 0 else CHIPS - far)) % CHIPS)

    def rows(self, way, step):
        return pl.ds(0, 32) if step else pl.ds(16 * way, 16)

    def hop_copy(self, way, step):
        section, _, _, _, ahead, behind, _ = where_am_i()
        return pltpu.make_async_remote_copy(
            src_ref=self.pair.at[:, self.target(way, step), self.rows(way, step), :],
            dst_ref=self.hop(way, step),
            send_sem=self.send_sem.at[way, step], recv_sem=self.recv_sem.at[way, step],
            device_id=(section, ahead if way == 0 else behind), device_id_type=MESH,
        )

    def both(self, n, at, rows):
        core = where_am_i()[2]
        return self.own(core)[n, at, rows, :].astype(F32) + self.pair[n, at, rows, :].astype(F32)

    def each(self, body):
        def run(n, _):
            body(n)
            return 0

        lax.fori_loop(0, self.pair.shape[0], run, 0)

    def send(self, step):
        for way in range(2):
            if step:
                self.hop_copy(way, step - 1).wait()
            at = self.target(way, step)

            def add(n):
                for half in range(2):
                    if step == 0 and half != way:
                        continue
                    rows = pl.ds(16 * half, 16)
                    value = self.both(n, at, rows)
                    if step == 1 and half == way:
                        value += self.hop(way, 0)[n].astype(F32)
                    elif step > 1:
                        value += self.hop(way, step - 1)[n, rows, :].astype(F32)
                    self.pair[n, at, rows, :] = value.astype(BF)

            self.each(add)
            self.hop_copy(way, step).start()

    def close(self):
        at = ring_chip(where_am_i()[3])
        for way in range(2):
            self.hop_copy(way, HOPS - 1).wait()

        def add(n):
            value = self.both(n, at, pl.ds(0, 32))
            for way in range(2):
                value += self.hop(way, HOPS - 1)[n].astype(F32)
            self.mine[n] = value.astype(self.mine.dtype)

        self.each(add)


class Stream:
    def __init__(self, pieces, crossings):
        self.pieces, self.crossings = pieces, crossings

    def pair(self):
        for piece in self.pieces:
            piece.pair_copy().start()

    def open(self):
        for piece in self.pieces:
            piece.pair_copy().wait()
            piece.send(0)

    def send(self, step):
        for piece in self.pieces:
            piece.send(step)

    def close(self):
        for piece in self.pieces:
            piece.close()
        for crossing in self.crossings:
            cross_copy(*crossing).start()


class Traffic:
    def __init__(self, plan):
        self.queue, self.plan = [], plan

    def add(self, stream):
        self.queue.append((stream, 1))

    def take(self, count=None):
        if count is None:
            count, self.plan = int(self.plan[0]), self.plan[1:]
        hops = []
        while count and self.queue:
            stream, step = self.queue.pop(0)
            hops.append((stream, step))
            if step < HOPS:
                self.queue.append((stream, step + 1))
            count -= 1
        return hops


def issue(hops):
    for stream, step in hops:
        if step < HOPS:
            stream.send(step)
        else:
            stream.close()


def train_kernel(
    tok, cot_h, lens, gains, shifts, wq_h, wo_h, wu_h, wd_h, xl_h, bl_h, z1_h, z2_h, w2, ids,
    act, eg, late, early, norm, enc, misc,
    wts, acts, hop1, xin, mid, bias, back_att, lng, cot, act_mine, act_theirs,
    mine1, theirs1, mine0, theirs0, lnown, lnpair, lnhop, lnmine, lntheirs,
    genc, enc_mine, miscown, miscpair, mischop, miscmine, acc2, acc1, dpool,
    load_sem, stream_sem, cross_sem, pair_sem, send_sem, recv_sem, free_sem,
):
    section, me, core, _, ahead, behind, sibling = where_am_i()
    greet()
    cot_copy = cross_copy(cot_h, cot, cross_sem.at[0])
    cot_copy.start()
    act_copy = cross_copy(act_mine, act_theirs, cross_sem.at[1])
    for d in range(2):
        for c in range(W_PANELS):
            if c < 3:
                src = wq_h.at[d, :, :, :, pl.ds(512 * c, 512)]
            elif c == 3:
                src = wo_h.at[d]
            elif c < 8:
                src = wu_h.at[d, :, :, :, pl.ds(512 * (c - 4), 512)]
            else:
                src = wd_h.at[d, pl.ds(2 * (c - 8), 2)]
            pltpu.make_async_copy(src, wts.at[d, pl.ds(2 * c, 2)], load_sem.at[d, c]).start()

    xin[0] = tok[...].astype(F32)
    row, col = iota((256, 1), 0), iota((1, 256), 1)
    q_step = ((row * 10923) >> 16).astype(F32)
    k_step = ((col * 10923) >> 16).astype(F32)
    for s in range(2):
        inv = 1.0 / lens[section, s].astype(F32)
        q_seq = jnp.floor((q_step + 0.5) * inv)
        k_seq = jnp.floor((k_step + 0.5) * inv)
        bias[s] = jnp.where((k_step <= q_step) & (q_seq == k_seq), 0.0, -1e30)
    def loaded(d, first, count):
        for c in range(first, first + count):
            at = wts.at[d, pl.ds(2 * c, 2)]
            pltpu.make_async_copy(at, at, load_sem.at[d, c]).wait()

    def forward(d, _):
        loaded(d, W_QKV, 3)
        hat, _ = ln_parts(xin[d])
        normed = (hat * gains[d, 0:1] + shifts[d, 0:1]).astype(BF)
        put_panel(acts, d, ACT_NORMED, normed)
        for c in range(3):
            put_panel(acts, d, ACT_Q + c, dot(normed, panel(wts, d, W_QKV + c)))
        for s in range(2):
            for quad in range(2):
                q = stacked(quarter(acts, d, ACT_Q, s, quad), HEAD_DIM**-0.5)
                k = quarter(acts, d, ACT_Q + 1, s, quad)
                v = quarter(acts, d, ACT_Q + 2, s, quad)
                scores = dot_lanes(q, k).reshape(4, 256, 256) + bias[s][None]
                top = jnp.max(scores, axis=-1, keepdims=True)
                e = jnp.exp(scores - top)
                total = jnp.sum(e, axis=-1, keepdims=True)
                p = (e * (1.0 / total)).astype(BF)
                for h in range(4):
                    put_quarter(acts, d, ACT_PROBS + s * 2 + quad, h // 2, h % 2, p[h])
                out = unstacked(dot(p.reshape(1024, 256), v))
                put_quarter(acts, d, ACT_ATT, s, quad, out)
        loaded(d, W_OUT, 1)
        middle = xin[d] + dot(panel(acts, d, ACT_ATT), panel(wts, d, W_OUT))
        mid[d] = middle
        loaded(d, W_UP, 4)
        hat, _ = ln_parts(middle)
        put_panel(acts, d, ACT_NORMED2, hat * gains[d, 1:2] + shifts[d, 1:2])

        def chunk(c, _):
            value, grad = gelu_pair(dot(panel(acts, d, ACT_NORMED2), panel(wts, d, W_UP + c)))
            put_panel(acts, d, ACT_GATED + c, value)
            put_panel(acts, d, ACT_SLOPE + c, grad)
            return 0

        lax.fori_loop(0, 4, chunk, 0)
        loaded(d, W_DOWN, 4)
        down = wts[d, pl.ds(2 * W_DOWN, 8)].reshape(4 * WIDTH, WIDTH)
        xin[d + 1] = mid[d] + dot(side_by_side(acts, d, ACT_GATED, 4), down)
        return 0

    lax.fori_loop(0, 2, forward, 0)
    act_mine[...] = xin[2].astype(BF)
    cot_copy.wait()
    act_copy.start()
    up = xin.at[2]
    for s in range(2):
        up[pl.ds(s * 256, 252), :] = cot[s].astype(F32)
        up[pl.ds(s * 256 + 252, 4), :] = jnp.zeros((4, WIDTH), F32)
    lng[...] = jnp.zeros_like(lng)

    def sems(k):
        return pair_sem.at[k], send_sem.at[k], recv_sem.at[k]

    def hop_rows(step):
        return pl.ds(0, 32 if step else 16)

    def piece1(k, first, hop_at):
        return Piece(
            lambda c: acts.at[2, pl.ds(c * 12 + first, 4)],
            acts.at[2, pl.ds(24 + first, 4)],
            lambda way, step: hop1.at[hop_at + step, pl.ds(4 * way, 4), hop_rows(step), :],
            mine1.at[pl.ds(first, 4)], sems(k),
        )

    def piece0(k, first, hop_at):
        return Piece(
            lambda c: acts.at[1, pl.ds(c * 12 + first, 4)],
            acts.at[1, pl.ds(24 + first, 4)],
            lambda way, step: wts.at[1, hop_at + step, pl.ds(4 * way, 4), hop_rows(step), :],
            mine0.at[pl.ds(first, 4)], sems(k),
        )

    def crossing(mine, theirs, first, k):
        return mine.at[pl.ds(first, 4)], theirs.at[pl.ds(first, 4)], cross_sem.at[k]

    down1 = Stream([piece1(0, W_DOWN, 0)], [crossing(mine1, theirs1, W_DOWN, 2)])
    up1 = Stream([piece1(1, W_UP, HOPS)], [crossing(mine1, theirs1, W_UP, 3)])
    att1 = Stream([piece1(2, 0, 2 * HOPS)], [crossing(mine1, theirs1, 0, 4)])
    down0 = Stream([piece0(3, W_DOWN, 0)], [crossing(mine0, theirs0, W_DOWN, 5)])
    up0 = Stream([piece0(4, W_UP, HOPS)], [crossing(mine0, theirs0, W_UP, 6)])
    norms = Piece(
        lambda c: lnown.at[c], lnpair, lambda way, step: lnhop.at[way, step, :, hop_rows(step), :], lnmine, sems(5)
    )
    att0 = Stream(
        [piece0(6, 0, 2 * HOPS), norms],
        [crossing(mine0, theirs0, 0, 7), (lnmine, lntheirs, cross_sem.at[8])],
    )
    encoder = Stream(
        [
            Piece(
                lambda c: genc.at[c], wts.at[1, pl.ds(21, 3)],
                lambda way, step: wts.at[1, 3 * HOPS + step, pl.ds(4 * way, 3), hop_rows(step), :],
                enc_mine, sems(7),
            ),
            Piece(
                lambda c: miscown.at[c], miscpair, lambda way, step: mischop.at[way, step, :, hop_rows(step), :],
                miscmine, sems(8),
            ),
        ],
        [],
    )
    traffic = Traffic(PLAN)

    def split(value):
        return value.astype(BF).reshape(8, 2, 32, WIDTH)

    layer_streams = {1: (down1, up1, att1), 0: (down0, up0, att0)}
    plan = {}
    for d in (1, 0):
        for n in range(8):
            plan[d, n] = traffic.take()
        traffic.add(layer_streams[d][0])
        traffic.add(layer_streams[d][1])
        for n in range(8, 13):
            plan[d, n] = traffic.take()
        if d == 1:
            traffic.add(att1)
            plan[d, 13] = traffic.take()

    def backward(i, _):
        d = 1 - i

        def each(act):
            for which in (1, 0):
                pl.when(d == which)(functools.partial(act, layer_streams[which]))

        def tick(n):
            for which in (1, 0):
                if plan[which, n]:
                    pl.when(d == which)(functools.partial(issue, plan[which, n]))

        def put(p, value):
            shaped = split(value)
            for c in range(2):
                acts[d + 1, c * 12 + p] = shaped[:, c]

        down = up[...].astype(BF)
        for c in range(4):
            part = dot_rows(panel(acts, d, ACT_GATED + c), down).astype(BF).reshape(4, 4, 32, WIDTH)
            for e in range(4):
                for j in range(4):
                    acts[d + 1, (e % 2) * 12 + W_DOWN + j, 2 * c + e // 2] = part[e, j]
            tick(c)

        @pl.when(d == 0)
        def _():
            pl.semaphore_wait(free_sem, 3)

        each(lambda streams: streams[0].pair())
        for c in range(4):
            back = dot_lanes(down, panel(wts, d, W_DOWN + c))
            back = (back * panel(acts, d, ACT_SLOPE + c).astype(F32)).astype(BF)
            put_panel(acts, d, ACT_SLOPE + c, back)
            put(W_UP + c, dot_rows(panel(acts, d, ACT_NORMED2), back))
            tick(4 + c)
        each(lambda streams: streams[1].pair())
        each(lambda streams: streams[0].open())
        back = dot_lanes(side_by_side(acts, d, ACT_SLOPE, 4), side_by_side(wts, d, W_UP, 4))
        back, gain, shift = ln_back(mid[d], back, gains[d, 1:2])
        lng[pl.ds(d * 4 + 1, 1), :] = gain
        lng[pl.ds(d * 4 + 3, 1), :] = shift
        up[...] += back
        branch = up[...].astype(BF)
        put(W_OUT, dot_rows(panel(acts, d, ACT_ATT), branch))
        back_att[...] = dot_lanes(branch, panel(wts, d, W_OUT)).astype(BF)
        each(lambda streams: streams[1].open())
        for s in range(2):
            for quad in range(2):
                rows, lanes = pl.ds(s * 256, 256), pl.ds(quad * 256, 256)
                qs = stacked(quarter(acts, d, ACT_Q, s, quad), HEAD_DIM**-0.5)
                k = quarter(acts, d, ACT_Q + 1, s, quad)
                v = quarter(acts, d, ACT_Q + 2, s, quad)
                outs = stacked(back_att[rows, lanes], 1.0)
                at = ACT_PROBS + s * 2 + quad
                p = jnp.concatenate([quarter(acts, d, at, h // 2, h % 2) for h in range(4)], axis=0)
                dp = dot_lanes(outs, v)
                pf = p.astype(F32)
                weighted = pf * dp
                total = jnp.sum(weighted, axis=-1, keepdims=True)
                ds = (weighted - pf * total).astype(BF)
                put_quarter(acts, d, ACT_Q, s, quad, unstacked(dot(ds, k)) * HEAD_DIM**-0.5)
                put_quarter(acts, d, ACT_Q + 1, s, quad, dot_rows(ds, qs))
                put_quarter(acts, d, ACT_Q + 2, s, quad, dot_rows(p, outs))
                tick(8 + 2 * s + quad)
        for c in range(3):
            put(c, dot_rows(panel(acts, d, ACT_NORMED), panel(acts, d, ACT_Q + c)))
        each(lambda streams: streams[2].pieces[0].pair_copy().start())
        tick(12)
        back = dot_lanes(side_by_side(acts, d, ACT_Q, 3), side_by_side(wts, d, W_QKV, 3))
        back, gain, shift = ln_back(xin[d], back, gains[d, 0:1])
        lng[pl.ds(d * 4, 1), :] = gain
        lng[pl.ds(d * 4 + 2, 1), :] = shift
        up[...] += back

        @pl.when(d == 1)
        def _():
            for target in (sibling, ahead, behind):
                pl.semaphore_signal(
                    free_sem, inc=1, device_id=(section, target), device_id_type=MESH
                )
            att1.open()
            issue(plan[1, 13])

        return 0

    lax.fori_loop(0, 2, backward, 0)
    eg[...] = up[...].astype(BF)
    turned = jnp.transpose(lng[...]).astype(BF).reshape(8, 2, 32, 128)
    for c in range(2):
        lnown[c, 0] = turned[:, c]
    norms.pair_copy().start()

    def fetch(k):
        i, half = k // 2, k % 2
        base = 16 * half
        copies = []
        for n, (src, lanes) in enumerate(((xl_h, 256), (bl_h, 512), (z1_h, 512), (z2_h, 512))):
            copies.append(
                pltpu.make_async_copy(
                    src.at[i, pl.ds(4 * half, 4)],
                    acts.at[0, pl.ds(base + 4 * n, 4), pl.ds(0, 7), :, pl.ds(0, lanes)],
                    stream_sem.at[half, n],
                )
            )
        return copies

    for copy in fetch(0):
        copy.start()
    att0.open()
    traffic.add(att0)
    hot = jnp.where(iota((512, TABLE), 1) == ids[...], 1.0, 0.0).astype(BF)
    code = dot_rows(eg[...], hot)
    for c in range(2):
        for half in range(2):
            genc[c, 1 + half] = split(code[:, 512 * half : 512 * (half + 1)])[:, c]
        miscown[c, 0] = code[:, CODES:].astype(BF).reshape(8, 2, 32, 128)[:, c]
    dpool[...] = dot_rows(hot[:, POOL_AT : POOL_AT + 96], eg[...])
    issue(traffic.take())
    rows = 4 * BLOCK_ROWS

    def held(ref, d, at, lanes=512):
        return ref[d, pl.ds(at, 4), pl.ds(0, 7), :, pl.ds(0, lanes)].reshape(rows, lanes)

    enc_plan = [(k, half, traffic.take()) for k in range(6) for half in range(2)]
    acc2[...] = jnp.zeros_like(acc2)
    acc1[...] = jnp.zeros_like(acc1)

    def block(k, _):
        base = 16 * (k % 2)

        def tick(half):
            for at, when, hops in enc_plan:
                if hops and when == half:
                    pl.when(k == at)(functools.partial(issue, hops))

        for copy in fetch(k):
            copy.wait()

        @pl.when(k < 5)
        def _():
            for copy in fetch(k + 1):
                copy.start()

        pooled = dpool[pl.ds(pl.multiple_of((k // 2) * 32, 32), FRAMES_BLOCK), :] * (1.0 / 64.0)
        wide = jnp.broadcast_to(pooled[:, None, :], (FRAMES_BLOCK, 8, WIDTH))
        wide = wide.reshape(BLOCK_ROWS, WIDTH)

        def part(bx, _):
            value = acts[0, base + 12 + bx, pl.ds(0, 7)].reshape(BLOCK_ROWS, WIDTH)
            back = (wide * gelu_slope(value)).astype(BF)
            wts[0, bx, pl.ds(0, 7)] = back.reshape(7, 32, WIDTH)
            value = acts[0, base + 8 + bx, pl.ds(0, 7)].reshape(BLOCK_ROWS, WIDTH)
            back = (dot_lanes(back, w2[...]) * gelu_slope(value)).astype(BF)
            wts[0, 4 + bx, pl.ds(0, 7)] = back.reshape(7, 32, WIDTH)
            return 0

        lax.fori_loop(0, 4, part, 0)
        tick(0)
        second = dot_rows(held(wts, 0, 0), held(acts, 0, base + 4))
        back = held(wts, 0, 4)
        patch = held(acts, 0, base, 256)
        first = [
            dot_rows(patch[:, 128 * dy2 : 128 * (dy2 + 1)], back[:, 256 * dy2 : 256 * (dy2 + 1)])
            for dy2 in range(2)
        ]
        first = first[0] + first[1]
        acc2[...] += second
        acc1[...] += first
        tick(1)
        return 0

    lax.fori_loop(0, 6, block, 0)
    shaped = split(acc2[...])
    hot, rest = patch_index(128)
    first = jnp.where(rest[:, :1] < 12, acc1[:, pl.ds(0, 128)], acc1[:, pl.ds(128, 128)])
    first = lax.dot_general(
        first, hot, (((0,), (0,)), ((), ())), preferred_element_type=F32,
        precision=lax.Precision.HIGHEST,
    )
    first = first.reshape(8, 2, 8, 48)
    first = jnp.concatenate([first, jnp.zeros((8, 2, 24, 48), F32)], axis=2).astype(BF)
    for c in range(2):
        genc[c, 0] = shaped[:, c]
        miscown[c, 0, :, :, pl.ds(64, 48)] = first[:, c]
    encoder.pair()
    issue(traffic.take())
    encoder.open()
    traffic.add(encoder)
    issue(traffic.take(99))
    for stream in (down1, up1, att1, down0, up0, att0):
        for crossed in stream.crossings:
            cross_copy(*crossed).wait()
    act_copy.wait()
    act[...] = act_theirs[...]
    late[...] = theirs1[...]
    early[...] = theirs0[...]
    norm[...] = lntheirs[0]
    enc[...] = enc_mine[...]
    misc[...] = miscmine[0]


def train(tok, cot, lens, gains, shifts, wq, wo, wu, wd, xl, bl, g1, g2, w2, ids):
    vm = pl.BlockSpec(memory_space=pltpu.VMEM)
    sm = pl.BlockSpec(memory_space=pltpu.SMEM)
    hb = pl.BlockSpec(memory_space=pl.ANY)

    def panels(w):
        return w.reshape(2, w.shape[1] // 256, 8, 32, w.shape[2])

    def parts(saved):
        return saved.reshape(saved.shape[0], 8, 7, 32, saved.shape[2])

    half = (8, 32, WIDTH)
    pieces = 9
    return pl.pallas_call(
        train_kernel,
        in_specs=[vm, hb, sm, vm, vm] + [hb] * 8 + [vm, vm],
        out_specs=[vm] * 7,
        out_shape=[
            jax.ShapeDtypeStruct((512, WIDTH), BF),
            jax.ShapeDtypeStruct((512, WIDTH), BF),
            jax.ShapeDtypeStruct((12, 32, WIDTH), BF),
            jax.ShapeDtypeStruct((12, 32, WIDTH), BF),
            jax.ShapeDtypeStruct((32, 128), BF),
            jax.ShapeDtypeStruct((3, 32, WIDTH), BF),
            jax.ShapeDtypeStruct((32, 128), BF),
        ],
        scratch_shapes=[
            pltpu.VMEM((2, 2 * W_PANELS) + half, BF),
            pltpu.VMEM((3, 2 * ACT_PANELS) + half, BF),
            pltpu.VMEM((3 * HOPS,) + half, BF),
            pltpu.VMEM((3, 512, WIDTH), F32),
            pltpu.VMEM((2, 512, WIDTH), F32),
            pltpu.VMEM((2, 256, 256), F32),
            pltpu.VMEM((512, WIDTH), BF),
            pltpu.VMEM((128, WIDTH), F32),
            pltpu.VMEM(cot.shape, BF),
            pltpu.VMEM((512, WIDTH), BF),
            pltpu.VMEM((512, WIDTH), BF),
            pltpu.VMEM((12, 32, WIDTH), BF),
            pltpu.VMEM((12, 32, WIDTH), BF),
            pltpu.VMEM((12, 32, WIDTH), BF),
            pltpu.VMEM((12, 32, WIDTH), BF),
            pltpu.VMEM((2, 1, 8, 32, 128), BF),
            pltpu.VMEM((1, 8, 32, 128), BF),
            pltpu.VMEM((2, HOPS, 1, 32, 128), BF),
            pltpu.VMEM((1, 32, 128), BF),
            pltpu.VMEM((1, 32, 128), BF),
            pltpu.VMEM((2, 3) + half, BF),
            pltpu.VMEM((3, 32, WIDTH), BF),
            pltpu.VMEM((2, 1, 8, 32, 128), BF),
            pltpu.VMEM((1, 8, 32, 128), BF),
            pltpu.VMEM((2, HOPS, 1, 32, 128), BF),
            pltpu.VMEM((1, 32, 128), BF),
            pltpu.VMEM((512, WIDTH), F32),
            pltpu.VMEM((128, 256), F32),
            pltpu.VMEM((96, WIDTH), F32),
            pltpu.SemaphoreType.DMA((2, W_PANELS)),
            pltpu.SemaphoreType.DMA((2, 4)),
            pltpu.SemaphoreType.DMA((9, 2)),
            pltpu.SemaphoreType.DMA((pieces, 2)),
            pltpu.SemaphoreType.DMA((pieces, 2, HOPS)),
            pltpu.SemaphoreType.DMA((pieces, 2, HOPS)),
            pltpu.SemaphoreType.REGULAR,
        ],
        compiler_params=pltpu.CompilerParams(
            collective_id=2, has_side_effects=True, vmem_limit_bytes=TRAIN_VMEM
        ),
        name="train",
    )(
        tok, cot, lens, gains, shifts, panels(wq), panels(wo), panels(wu), panels(wd),
        parts(xl), parts(bl), parts(g1), parts(g2), w2, ids,
    )


def outputs_kernel(act_in, eg_in, late, early, norm, enc, misc, *outs):
    act, eg, qkv, out, up, down, gain, bias, bias2, enc1, enc2, book, names = outs
    for s in range(2):
        act[0, s] = act_in[pl.ds(s * 256, 256), :].astype(F32)[:252].astype(BF)
        eg[0, s] = eg_in[pl.ds(s * 256, 256), :].astype(F32)[:252].astype(BF)
    for d, rows in enumerate((early, late)):
        for c in range(3):
            qkv[0, d, :, pl.ds(512 * c, 512)] = rows[W_QKV + c].astype(F32)
        out[0, d] = rows[W_OUT].astype(F32)
        for c in range(4):
            up[0, d, :, pl.ds(512 * c, 512)] = rows[W_UP + c].astype(F32)
            down[0, d, pl.ds(32 * c, 32), :] = rows[W_DOWN + c].astype(F32)
    turned = turn(norm[...].astype(F32))
    for d in range(2):
        gain[0, d] = turned[4 * d : 4 * d + 2]
        bias[0, pl.ds(d, 1)] = turned[4 * d + 2 : 4 * d + 3]
        bias2[0, pl.ds(d, 1)] = turned[4 * d + 3 : 4 * d + 4]
    enc2[0] = enc[0].astype(F32)
    for c in range(2):
        book[0, :, pl.ds(512 * c, 512)] = enc[1 + c].astype(F32)
    enc1[0] = misc[...].astype(F32)[:8, 64:112]
    turned = turn(misc[...].astype(F32))
    for a in range(17):
        names[a] = turned[a : a + 1]


def spread_outputs(*parts):
    vm = pl.BlockSpec(memory_space=pltpu.VMEM)
    shapes = [
        (1, 2, 32, 1536), (1, 2, 32, 512), (1, 2, 32, 2048), (1, 2, 128, 512), (1, 2, 2, 32),
        (1, 2, 32), (1, 2, 32), (1, 8, 48), (1, 32, 512), (1, 32, 1024), (17, 1, 32),
    ]
    acts = [jax.ShapeDtypeStruct((1, 2, 252, WIDTH), BF)] * 2
    outs = pl.pallas_call(
        outputs_kernel,
        in_specs=[vm] * len(parts),
        out_specs=[vm] * (len(shapes) + 2),
        out_shape=acts + [jax.ShapeDtypeStruct(shape, F32) for shape in shapes],
        compiler_params=pltpu.CompilerParams(vmem_limit_bytes=VMEM_LIMIT),
        name="outputs",
    )(*parts)
    outs = list(outs)
    outs[6] = outs[6].transpose(0, 1, 3, 2)
    for k in (9, 10, 11):
        outs[k] = outs[k].transpose(0, 2, 1)
    outs[12] = outs[12].transpose(1, 0, 2)
    return tuple(outs)


def swap(array):
    return lax.ppermute(array, "section", [(0, 1), (1, 0)])


def whole_rows(g):
    return g.transpose(1, 0, 2, 3).reshape(512, g.shape[-1])


def scatter_plain(g, gl, e):
    def sums(array, axis):
        return lax.psum_scatter(array.astype(F32)[None], "dp", scatter_dimension=axis, tiled=True)

    layers = [whole_rows(g[d]) for d in range(g.shape[0])]
    qkv = jnp.stack([rows[:, :1536] for rows in layers])
    out = jnp.stack([rows[:, 1536:2048] for rows in layers])
    up = jnp.stack([rows[:, 2048:4096] for rows in layers])
    down = jnp.stack(
        [
            rows[:, 4096:].reshape(16, 32, 4, WIDTH).transpose(0, 2, 1, 3).reshape(2048, WIDTH)
            for rows in layers
        ]
    )
    norm = whole_rows(gl)[:, :8].reshape(512, 2, 4).transpose(1, 0, 2)
    enc = whole_rows(e)
    first = e.transpose(1, 0, 2, 3)[:, :, :8, 1600:1648].reshape(128, 48)
    layer_sums = [sums(x, 2) for x in (qkv, out, up, down, norm)]
    layer_sums = [swap(x) for x in layer_sums]
    norm = layer_sums.pop()
    return tuple(layer_sums) + (
        norm[..., 0:2],
        norm[..., 2],
        norm[..., 3],
        sums(first.T, 2),
        sums(enc[:, :512].T, 2),
        sums(enc[:, 512:1536].T, 2),
        sums(enc[:, 1536:1553].T, 2),
    )


def on_device(
    frames, action_ids, delta_ids, seq_len, enc_w1, enc_w2, codebook, action_table,
    ln_gain, ln_bias, w_qkv, w_out, w_up, w_down, cotangent,
):
    micro, steps = frames.shape[1], frames.shape[2]
    count = micro * steps
    gains, shifts = ln_gain.transpose(0, 2, 1), ln_bias.transpose(0, 2, 1)
    tok, ids, xl, blocks, z1, z2 = enc_forward(
        frames.reshape((count,) + frames.shape[3:]), enc_w1, enc_w2, codebook, action_table,
        action_ids[0], delta_ids[0].transpose(0, 2, 1),
    )
    if lax.axis_size("dp") == 2 * CHIPS:
        parts = train(
            tok, cotangent[0], seq_len, gains, shifts, w_qkv, w_out, w_up, w_down,
            xl, blocks, z1, z2, enc_w2, ids,
        )
        return spread_outputs(*parts)
    lnp = jnp.concatenate([gains, shifts], axis=1)
    act, eg, g, gl = run_layers(tok, cotangent[0], seq_len, lnp, w_qkv, w_out, w_up, w_down)
    embed_grad = eg.reshape(micro, 256, WIDTH)[None, :, : steps * TPS]
    e = enc_backward(eg, xl, blocks, z1, z2, enc_w2, ids)
    return (act[None], embed_grad) + scatter_plain(g, gl, e)


def solution(mesh):
    return jax.shard_map(
        on_device,
        mesh=mesh,
        in_specs=(
            P("section", "dp", None, None, None),
            P("section", "dp", None),
            P("section", "dp", None, None),
            P(None, "dp"),
            P(), P(), P(), P(), P(), P(), P(), P(), P(), P(),
            P("section", "dp", None, None),
        ),
        out_specs=(
            P("section", "dp", None, None),
            P("section", "dp", None, None),
            P("section", None, "dp", None),
            P("section", None, "dp", None),
            P("section", None, "dp", None),
            P("section", None, "dp", None),
            P("section", None, "dp", None),
            P("section", None, "dp"),
            P("section", None, "dp"),
            P("section", None, "dp"),
            P("section", None, "dp"),
            P("section", None, "dp"),
            P("section", None, "dp"),
        ),
        check_vma=False,
    )
```

```python
import functools

import jax
import jax.numpy as jnp
from jax import lax
from jax.experimental import pallas as pl
from jax.experimental.pallas import tpu as pltpu
from jax.sharding import PartitionSpec as P

HEADS = 8
HEAD_DIM = 64
TPS = 6
EPS = 1e-05
BF = jnp.bfloat16
F32 = jnp.float32
I32 = jnp.int32

WIDTH = 512
CODES = 1024
FRAMES_BLOCK = 28
BLOCK_ROWS = FRAMES_BLOCK * 8
TABLE = 1152
POOL_AT = 1056
ACT_AT = 1024
LAYER_COLS = 6144
ENC_COLS = 1664
VMEM_LIMIT = 60 << 20
TRAIN_VMEM = 63 << 20
PLAN = "00000000010111000000001111110101010101012"


def dot(a, b):
    return jnp.dot(a, b, preferred_element_type=F32)


def dot_rows(a, b):
    return lax.dot_general(a, b, (((0,), (0,)), ((), ())), preferred_element_type=F32)


def dot_lanes(a, b):
    return lax.dot_general(a, b, (((1,), (1,)), ((), ())), preferred_element_type=F32)


def iota(shape, axis):
    return lax.broadcasted_iota(I32, shape, axis)


def gelu_pair(v):
    cdf = 0.5 + 0.5 * lax.erf(v * 0.7071067811865476)
    bell = jnp.exp2(v * v * (-0.5 * 1.4426950408889634))
    return v * cdf, cdf + v * (bell * 0.3989422804014327)


def gelu(v):
    return v * (0.5 + 0.5 * lax.erf(v * 0.7071067811865476))


def gelu_slope(v):
    return gelu_pair(v.astype(F32))[1]


def patch_index(rows):
    k = iota((rows, 48), 0)
    dy = (k * 2731) >> 16
    rest = k - dy * 24
    j = jnp.where(rest >= 12, rest - 12, rest)
    return jnp.where((iota((rows, 48), 1) == dy * 12 + j) & (k < 96), 1.0, 0.0), rest


def encoder_weights(w1):
    hot, rest = patch_index(128)
    wide = dot(hot.astype(BF), w1)
    first = jnp.where(rest[:, :1] < 12, wide, 0.0)
    second = jnp.where(rest[:, :1] >= 12, wide, 0.0)
    block = jnp.concatenate([first, second], axis=1)
    zero = jnp.zeros_like(block)
    return jnp.concatenate(
        [jnp.concatenate([block, zero], axis=1), jnp.concatenate([zero, block], axis=1)], axis=0
    ).astype(BF)


def token_ids(s, names, deltas):
    steps = names.shape[1]
    frame = s * steps + iota((1, steps), 1)
    block = (frame * 2341) >> 16
    pool = POOL_AT + block * 32 + frame - FRAMES_BLOCK * block
    kinds = jnp.concatenate([pool, names[s : s + 1] + ACT_AT, deltas[s]], axis=0).astype(F32)
    row = iota((256, 1), 0)
    step = (row * 10923) >> 16
    hot = jnp.where(iota((256, steps), 1) == step, 1.0, 0.0)
    each = lax.dot_general(
        hot, kinds, (((1,), (1,)), ((), ())), preferred_element_type=F32,
        precision=lax.Precision.HIGHEST,
    )
    mine = jnp.where(iota((256, TPS), 1) == row - TPS * step, each, 0.0)
    found = (jnp.sum(mine, axis=1, keepdims=True) + 0.5).astype(I32)
    return jnp.where(row < TPS * steps, found, -1)


def enc_fwd_kernel(
    frames, w1, w2, book, acts, names, deltas,
    tok, ids, xl_h, bl_h, z1_h, z2_h,
    perm, lanes, big, xs, acc, table, xl, blocks, z1, z2, sem, book_sem,
):
    step = pl.program_id(0)
    book_copy = pltpu.make_async_copy(book, table.at[pl.ds(0, CODES)], book_sem)

    def part_rows(bx):
        return pl.ds(pl.multiple_of(bx * BLOCK_ROWS, BLOCK_ROWS), BLOCK_ROWS)

    def save(at, bx):
        rows = part_rows(bx)
        return [
            pltpu.make_async_copy(held.at[at, rows], out.at[at, rows], sem.at[at, bx, n])
            for n, (held, out) in enumerate(((blocks, bl_h), (z1, z1_h), (z2, z2_h)))
        ]

    def save_patches(at):
        return pltpu.make_async_copy(xl.at[at], xl_h.at[at], sem.at[at, 0, 3])

    @pl.when(step == 0)
    def _():
        a, b = iota((256, 256), 0), iota((256, 256), 1)
        perm[...] = jnp.where(b == 8 * (a & 31) + (a >> 5), 1.0, 0.0).astype(BF)
        src = iota((256, 1024), 0)
        px = (src * 5462) >> 16
        at = (px >> 1) * 128 + (px & 1) * 12 + (src - px * 12)
        out = jnp.where(src < 192, iota((256, 1024), 1) - at, -1)
        for dy in range(4):
            lanes[pl.ds(256 * dy, 256), :] = jnp.where(out == dy * 24, 1.0, 0.0).astype(BF)
        xs[...] = jnp.zeros_like(xs)
        big[...] = encoder_weights(w1[...])
        book_copy.start()
        named = acts[...].astype(F32)
        pad = jnp.zeros((TABLE - ACT_AT - named.shape[0], WIDTH), F32)
        table[pl.ds(ACT_AT, TABLE - ACT_AT), :] = jnp.concatenate([named, pad], axis=0).astype(BF)

    for group in range(FRAMES_BLOCK // 4):
        rows = frames[pl.ds(group * 4, 4)].reshape(256, 192)
        moved = dot(perm[...], rows).astype(BF).reshape(2, 4, 32, 192)
        for dy in range(4):
            xs[:, pl.ds(group * 32, 32), pl.ds(256 * dy, 192)] = moved[:, dy]
    for dy2 in range(2):
        spread = dot(xs[dy2], lanes[...]).astype(BF)
        for bx in range(8):
            xl[step, pl.ds(bx * BLOCK_ROWS, BLOCK_ROWS), pl.ds(dy2 * 128, 128)] = spread[
                :, bx * 128 : (bx + 1) * 128
            ]
    save_patches(step).start()
    acc[...] = jnp.zeros_like(acc)

    def part(bx, _):
        rows = part_rows(bx)
        first = dot(xl[step, rows, :], big[...])
        z1[step, rows, :] = first.astype(BF)
        value = gelu(first).astype(BF)
        blocks[step, rows, :] = value
        second = dot(value, w2[...])
        z2[step, rows, :] = second.astype(BF)
        acc[...] += gelu(second)
        for copy in save(step, bx):
            copy.start()
        return 0

    lax.fori_loop(0, 8, part, 0, unroll=True)
    pooled = jnp.sum(acc[...].reshape(FRAMES_BLOCK, 8, WIDTH), axis=1) * (1.0 / 64.0)
    pooled = jnp.concatenate([pooled, jnp.zeros((32 - FRAMES_BLOCK, WIDTH), F32)], axis=0)
    table[pl.ds(pl.multiple_of(POOL_AT + step * 32, 32), 32), :] = pooled.astype(BF)

    @pl.when(step == pl.num_programs(0) - 1)
    def _():
        book_copy.wait()
        for s in range(2):
            rows = pl.ds(s * 256, 256)
            found = token_ids(s, names[...], deltas[...])
            ids[rows, :] = found
            hot = jnp.where(iota((256, TABLE), 1) == found, 1.0, 0.0).astype(BF)
            tok[rows, :] = dot(hot, table[...]).astype(BF)
        for at in range(xl.shape[0]):
            save_patches(at).wait()
            for bx in range(8):
                for copy in save(at, bx):
                    copy.wait()


def enc_forward(frames, w1, w2, book, acts, names, deltas):
    count = frames.shape[0]
    grid = count // FRAMES_BLOCK
    rows = 8 * BLOCK_ROWS

    def whole(shape):
        return pl.BlockSpec(shape, lambda i: (0,) * len(shape))

    hb = pl.BlockSpec(memory_space=pl.ANY)
    return pl.pallas_call(
        enc_fwd_kernel,
        grid=(grid,),
        in_specs=[
            pl.BlockSpec((FRAMES_BLOCK, 64, 192), lambda i: (i, 0, 0)),
            whole(w1.shape),
            whole(w2.shape),
            hb,
            whole(acts.shape),
            whole(names.shape),
            whole(deltas.shape),
        ],
        out_specs=[
            whole((512, WIDTH)), whole((512, 1)), hb, hb, hb, hb,
        ],
        out_shape=[
            jax.ShapeDtypeStruct((512, WIDTH), BF),
            jax.ShapeDtypeStruct((512, 1), I32),
            jax.ShapeDtypeStruct((grid, rows, 256), BF),
            jax.ShapeDtypeStruct((grid, rows, 512), BF),
            jax.ShapeDtypeStruct((grid, rows, 512), BF),
            jax.ShapeDtypeStruct((grid, rows, 512), BF),
        ],
        scratch_shapes=[
            pltpu.VMEM((256, 256), BF),
            pltpu.VMEM((1024, 1024), BF),
            pltpu.VMEM((256, 512), BF),
            pltpu.VMEM((2, BLOCK_ROWS, 1024), BF),
            pltpu.VMEM((BLOCK_ROWS, WIDTH), F32),
            pltpu.VMEM((TABLE, WIDTH), BF),
            pltpu.VMEM((grid, rows, 256), BF),
            pltpu.VMEM((grid, rows, 512), BF),
            pltpu.VMEM((grid, rows, 512), BF),
            pltpu.VMEM((grid, rows, 512), BF),
            pltpu.SemaphoreType.DMA((grid, 8, 4)),
            pltpu.SemaphoreType.DMA,
        ],
        compiler_params=pltpu.CompilerParams(vmem_limit_bytes=VMEM_LIMIT),
        name="enc_fwd",
    )(frames, w1, w2, book, acts, names, deltas)


def ln_parts(x):
    mean = jnp.mean(x, axis=-1, keepdims=True)
    center = x - mean
    var = jnp.mean(center * center, axis=-1, keepdims=True)
    scale = lax.rsqrt(var + EPS)
    return center * scale, scale


def ln_back(x, d, gain):
    hat, scale = ln_parts(x)
    dh = d * gain
    one = jnp.mean(dh, axis=-1, keepdims=True)
    two = jnp.mean(dh * hat, axis=-1, keepdims=True)
    back = scale * (dh - one - hat * two)
    return back, jnp.sum(d * hat, axis=0, keepdims=True), jnp.sum(d, axis=0, keepdims=True)


def head_mask(h):
    lane = iota((1, 256), 1) >> 6
    return lane == h


def stacked(rows, scale):
    out = []
    for h in range(4):
        mask = jnp.where(head_mask(h), scale, 0.0).astype(BF)
        out.append(rows * mask)
    return jnp.concatenate(out, axis=0)


def unstacked(rows):
    out = rows[768:]
    for h in range(3):
        out = jnp.where(head_mask(h), rows[h * 256 : (h + 1) * 256], out)
    return out


def scatter_rows(g, d, cols, value, dests=16):
    shaped = value.astype(BF).reshape(dests // 2, 2, 32, value.shape[1])
    for core in range(2):
        g[d, core, :, :, cols] = shaped[:, core]


def layers_kernel(
    tok, cot_h, lens, lnp, wq_h, wo_h, wu_h, wd_h,
    act, eg, g, gl,
    wq, wo, wu, wd, stream, normed, packed, probs, att, normed2, gated, slope, bias,
    up, back_up, back_att, back_packed, lng, cot, mine, theirs, sems, cross_sem,
):
    layers = wq.shape[0]
    section = lax.axis_index("section")
    barrier = pltpu.get_barrier_semaphore()
    pl.semaphore_signal(
        barrier, inc=1, device_id=(1 - section, lax.axis_index("dp")), device_id_type=MESH
    )
    pl.semaphore_wait(barrier, 1)
    cot_copy = cross_copy(cot_h, cot, cross_sem.at[0])
    cot_copy.start()
    act_copy = cross_copy(mine, theirs, cross_sem.at[1])
    copies = []
    for d in range(layers):
        for k, (src, dst) in enumerate(((wq_h, wq), (wo_h, wo), (wu_h, wu), (wd_h, wd))):
            copy = pltpu.make_async_copy(src.at[d], dst.at[d], sems.at[d, k])
            copy.start()
            copies.append(copy)

    stream[0, 0] = tok[...].astype(F32)
    row = iota((256, 1), 0)
    col = iota((1, 256), 1)
    q_step = ((row * 10923) >> 16).astype(F32)
    k_step = ((col * 10923) >> 16).astype(F32)
    for s in range(2):
        inv = 1.0 / lens[section, s].astype(F32)
        q_seq = jnp.floor((q_step + 0.5) * inv)
        k_seq = jnp.floor((k_step + 0.5) * inv)
        bias[s] = jnp.where((k_step <= q_step) & (q_seq == k_seq), 0.0, -1e30)
    for copy in copies:
        copy.wait()

    def forward(d, _):
        x = stream[d, 0]
        hat, _ = ln_parts(x)
        normed[d] = (hat * lnp[d, 0:1] + lnp[d, 2:3]).astype(BF)
        for c in range(3):
            cols = pl.ds(c * 512, 512)
            packed[d, :, cols] = dot(normed[d], wq[d, :, cols]).astype(BF)
        for s in range(2):
            rows = pl.ds(s * 256, 256)
            for quad in range(2):
                q = stacked(packed[d, rows, pl.ds(quad * 256, 256)], HEAD_DIM**-0.5)
                k = packed[d, rows, pl.ds(512 + quad * 256, 256)]
                v = packed[d, rows, pl.ds(1024 + quad * 256, 256)]
                scores = dot_lanes(q, k).reshape(4, 256, 256) + bias[s][None]
                top = jnp.max(scores, axis=-1, keepdims=True)
                e = jnp.exp(scores - top)
                total = jnp.sum(e, axis=-1, keepdims=True)
                p = (e * (1.0 / total)).astype(BF).reshape(1024, 256)
                probs[d, s * 2 + quad] = p
                att[d, rows, pl.ds(quad * 256, 256)] = unstacked(dot(p, v)).astype(BF)
        middle = stream[d, 0] + dot(att[d], wo[d])
        stream[d, 1] = middle
        hat, _ = ln_parts(middle)
        normed2[d] = (hat * lnp[d, 1:2] + lnp[d, 3:4]).astype(BF)

        def chunk(c, _):
            cols = pl.ds(pl.multiple_of(c * 512, 512), 512)
            value, grad = gelu_pair(dot(normed2[d], wu[d, :, cols]))
            gated[d, :, cols] = value.astype(BF)
            slope[d, :, cols] = grad.astype(BF)
            return 0

        lax.fori_loop(0, 4, chunk, 0)
        stream[d + 1, 0] = stream[d, 1] + dot(gated[d], wd[d])
        return 0

    lax.fori_loop(0, layers, forward, 0)
    cot_copy.wait()
    mine[...] = stream[layers, 0].astype(BF)
    act_copy.start()
    for s in range(2):
        up[pl.ds(s * 256, 252), :] = cot[s].astype(F32)
        up[pl.ds(s * 256 + 252, 4), :] = jnp.zeros((4, WIDTH), F32)
    lng[...] = jnp.zeros_like(lng)

    def backward(i, _):
        d = layers - 1 - i
        down = up[...].astype(BF)

        def chunk(c, _):
            cols = pl.ds(pl.multiple_of(c * 256, 256), 256)
            part = dot_rows(gated[d, :, cols], down).astype(BF).reshape(2, 4, 32, WIDTH)
            for core in range(2):
                for j in range(4):
                    g[d, core, c, :, pl.ds(4096 + 512 * j, 512)] = part[core, j]
            back = dot_lanes(down, wd[d, cols, :])
            back = (back * slope[d, :, cols].astype(F32)).astype(BF)
            back_up[:, cols] = back
            part = dot_rows(normed2[d], back).astype(BF).reshape(8, 2, 32, 256)
            out = pl.ds(pl.multiple_of(2048 + c * 256, 256), 256)
            for core in range(2):
                g[d, core, :, :, out] = part[:, core]
            return 0

        lax.fori_loop(0, 8, chunk, 0)
        back, gain, shift = ln_back(stream[d, 1], dot_lanes(back_up[...], wu[d]), lnp[d, 1:2])
        lng[pl.ds(d * 4 + 1, 1), :] = gain
        lng[pl.ds(d * 4 + 3, 1), :] = shift
        up[...] += back
        branch = up[...].astype(BF)
        scatter_rows(g, d, pl.ds(1536, 512), dot_rows(att[d], branch))
        back_att[...] = dot_lanes(branch, wo[d]).astype(BF)
        for s in range(2):
            rows = pl.ds(s * 256, 256)
            for quad in range(2):
                lanes = pl.ds(quad * 256, 256)
                qs = stacked(packed[d, rows, lanes], HEAD_DIM**-0.5)
                k = packed[d, rows, pl.ds(512 + quad * 256, 256)]
                v = packed[d, rows, pl.ds(1024 + quad * 256, 256)]
                outs = stacked(back_att[rows, lanes], 1.0)
                p = probs[d, s * 2 + quad]
                dp = dot_lanes(outs, v)
                pf = p.astype(F32)
                weighted = pf * dp
                total = jnp.sum(weighted, axis=-1, keepdims=True)
                ds = (weighted - pf * total).astype(BF)
                back_packed[rows, lanes] = (unstacked(dot(ds, k)) * HEAD_DIM**-0.5).astype(BF)
                back_packed[rows, pl.ds(512 + quad * 256, 256)] = dot_rows(ds, qs).astype(BF)
                back_packed[rows, pl.ds(1024 + quad * 256, 256)] = dot_rows(p, outs).astype(BF)
        for c in range(3):
            cols = pl.ds(c * 512, 512)
            scatter_rows(g, d, cols, dot_rows(normed[d], back_packed[:, cols]))
        back, gain, shift = ln_back(stream[d, 0], dot_lanes(back_packed[...], wq[d]), lnp[d, 0:1])
        lng[pl.ds(d * 4, 1), :] = gain
        lng[pl.ds(d * 4 + 2, 1), :] = shift
        up[...] += back
        return 0

    lax.fori_loop(0, layers, backward, 0)
    eg[...] = up[...].astype(BF)
    act_copy.wait()
    for s in range(2):
        act[s] = theirs[pl.ds(s * 256, 256), :].astype(F32)[:252].astype(BF)
    turned = jnp.transpose(lng[...]).astype(BF).reshape(8, 2, 32, 128)
    for core in range(2):
        gl[core] = turned[:, core]


def run_layers(tok, cot, lens, lnp, wq, wo, wu, wd):
    layers = wq.shape[0]
    vm = pl.BlockSpec(memory_space=pltpu.VMEM)
    sm = pl.BlockSpec(memory_space=pltpu.SMEM)
    hb = pl.BlockSpec(memory_space=pl.ANY)
    rows = 512
    return pl.pallas_call(
        layers_kernel,
        in_specs=[vm, hb, sm, vm, hb, hb, hb, hb],
        out_specs=[vm, vm, vm, vm],
        out_shape=[
            jax.ShapeDtypeStruct((2, 252, WIDTH), BF),
            jax.ShapeDtypeStruct((rows, WIDTH), BF),
            jax.ShapeDtypeStruct((layers, 2, 8, 32, LAYER_COLS), BF),
            jax.ShapeDtypeStruct((2, 8, 32, 128), BF),
        ],
        scratch_shapes=[
            pltpu.VMEM(wq.shape, BF),
            pltpu.VMEM(wo.shape, BF),
            pltpu.VMEM(wu.shape, BF),
            pltpu.VMEM(wd.shape, BF),
            pltpu.VMEM((layers + 1, 2, rows, WIDTH), F32),
            pltpu.VMEM((layers, rows, WIDTH), BF),
            pltpu.VMEM((layers, rows, 3 * WIDTH), BF),
            pltpu.VMEM((layers, 4, 1024, 256), BF),
            pltpu.VMEM((layers, rows, WIDTH), BF),
            pltpu.VMEM((layers, rows, WIDTH), BF),
            pltpu.VMEM((layers, rows, 4 * WIDTH), BF),
            pltpu.VMEM((layers, rows, 4 * WIDTH), BF),
            pltpu.VMEM((2, 256, 256), F32),
            pltpu.VMEM((rows, WIDTH), F32),
            pltpu.VMEM((rows, 4 * WIDTH), BF),
            pltpu.VMEM((rows, WIDTH), BF),
            pltpu.VMEM((rows, 3 * WIDTH), BF),
            pltpu.VMEM((128, WIDTH), F32),
            pltpu.VMEM(cot.shape, BF),
            pltpu.VMEM((rows, WIDTH), BF),
            pltpu.VMEM((rows, WIDTH), BF),
            pltpu.SemaphoreType.DMA((layers, 4)),
            pltpu.SemaphoreType.DMA((2, 2)),
        ],
        compiler_params=pltpu.CompilerParams(
            collective_id=1, has_side_effects=True, vmem_limit_bytes=VMEM_LIMIT
        ),
        name="layers",
    )(tok, cot, lens, lnp, wq, wo, wu, wd)


def enc_bwd_kernel(eg, xl, blocks, g1, g2, w2, ids, e, dpool, bs, bf, acc2, acc1):
    step = pl.program_id(0)

    @pl.when(step == 0)
    def _():
        hot = jnp.where(iota((512, TABLE), 1) == ids[...], 1.0, 0.0).astype(BF)
        code = dot_rows(eg[...], hot[:, :POOL_AT + 96]).astype(BF)
        dpool[...] = dot_rows(hot[:, POOL_AT : POOL_AT + 96], eg[...])
        parts = code[:, :CODES].reshape(8, 2, 32, CODES)
        tail = code[:, CODES : CODES + 128].reshape(8, 2, 32, 128)
        for core in range(2):
            e[core, :, :, pl.ds(512, CODES)] = parts[:, core]
            e[core, :, :, pl.ds(1536, 128)] = tail[:, core]
        acc2[...] = jnp.zeros_like(acc2)
        acc1[...] = jnp.zeros_like(acc1)

    pooled = dpool[pl.ds(pl.multiple_of(step * 32, 32), 32), :][:FRAMES_BLOCK] * (1.0 / 64.0)
    wide = jnp.broadcast_to(pooled[:, None, :], (FRAMES_BLOCK, 8, WIDTH)).reshape(BLOCK_ROWS, WIDTH)

    def part(bx, _):
        rows = pl.ds(pl.multiple_of(bx * BLOCK_ROWS, BLOCK_ROWS), BLOCK_ROWS)
        back = (wide * gelu_slope(g2[0, rows, :])).astype(BF)
        bs[rows, :] = back
        bf[rows, :] = (dot_lanes(back, w2[...]) * gelu_slope(g1[0, rows, :])).astype(BF)
        return 0

    lax.fori_loop(0, 8, part, 0)
    acc2[...] += dot_rows(bs[...], blocks[0])
    for dy2 in range(2):
        acc1[:, pl.ds(dy2 * 256, 256)] += dot_rows(
            xl[0, :, pl.ds(dy2 * 128, 128)], bf[:, pl.ds(dy2 * 256, 256)]
        )

    @pl.when(step == pl.num_programs(0) - 1)
    def _():
        parts = acc2[...].astype(BF).reshape(8, 2, 32, WIDTH)
        both = acc1[:, pl.ds(0, 256)] + acc1[:, pl.ds(256, 256)]
        hot, rest = patch_index(128)
        first = jnp.where(rest[:, :1] < 12, both[:, :128], both[:, 128:])
        first = lax.dot_general(
            first, hot, (((0,), (0,)), ((), ())), preferred_element_type=F32,
            precision=lax.Precision.HIGHEST,
        )
        first = first.reshape(8, 2, 8, 48)
        first = jnp.concatenate([first, jnp.zeros((8, 2, 24, 48), F32)], axis=2).astype(BF)
        for core in range(2):
            e[core, :, :, pl.ds(0, WIDTH)] = parts[:, core]
            e[core, :, :, pl.ds(1536 + 64, 48)] = first[:, core]


def enc_backward(eg, xl, blocks, g1, g2, w2, ids):
    grid, rows, _ = xl.shape

    def whole(shape):
        return pl.BlockSpec(shape, lambda i: (0,) * len(shape))

    def saved(lanes):
        return pl.BlockSpec((1, rows, lanes), lambda i: (i, 0, 0))

    return pl.pallas_call(
        enc_bwd_kernel,
        grid=(grid,),
        in_specs=[
            whole(eg.shape), saved(256), saved(512), saved(512), saved(512),
            whole(w2.shape), whole(ids.shape),
        ],
        out_specs=whole((2, 8, 32, ENC_COLS)),
        out_shape=jax.ShapeDtypeStruct((2, 8, 32, ENC_COLS), BF),
        scratch_shapes=[
            pltpu.VMEM((96, WIDTH), F32),
            pltpu.VMEM((rows, WIDTH), BF),
            pltpu.VMEM((rows, WIDTH), BF),
            pltpu.VMEM((WIDTH, WIDTH), F32),
            pltpu.VMEM((128, WIDTH), F32),
        ],
        compiler_params=pltpu.CompilerParams(vmem_limit_bytes=VMEM_LIMIT),
        name="enc_bwd",
    )(eg, xl, blocks, g1, g2, w2, ids)


CHIPS = 8
HOPS = CHIPS // 2
MESH = pl.DeviceIdType.MESH


def ring_place(chip):
    z, x = chip // 2, chip % 2
    return z * (1 - x) + (7 - z) * x


def ring_chip(place):
    half = place // 4
    return (1 - half) * (2 * place) + half * (15 - 2 * place)


def where_am_i():
    section, me = lax.axis_index("section"), lax.axis_index("dp")
    core, chip = me % 2, me // 2
    place = ring_place(chip)
    ahead = ring_chip((place + 1) % CHIPS) * 2 + core
    behind = ring_chip((place + CHIPS - 1) % CHIPS) * 2 + core
    sibling = chip * 2 + (1 - core)
    return section, me, core, place, ahead, behind, sibling


def greet():
    section, me, _, _, ahead, behind, sibling = where_am_i()
    barrier = pltpu.get_barrier_semaphore()
    for target in ((section, sibling), (section, ahead), (section, behind), (1 - section, me)):
        pl.semaphore_signal(barrier, inc=1, device_id=target, device_id_type=MESH)
    pl.semaphore_wait(barrier, 4)


def cross_copy(src, dst, sem):
    section, me = lax.axis_index("section"), lax.axis_index("dp")
    return pltpu.make_async_remote_copy(
        src_ref=src, dst_ref=dst, send_sem=sem.at[0], recv_sem=sem.at[1],
        device_id=(1 - section, me), device_id_type=MESH,
    )


def turn(rows):
    tall = jnp.concatenate([rows, jnp.zeros((96, rows.shape[1]), F32)], axis=0)
    return jnp.transpose(tall)[:, :32]


ACT_NORMED, ACT_Q, ACT_PROBS, ACT_ATT, ACT_NORMED2, ACT_GATED, ACT_SLOPE = 0, 1, 4, 8, 9, 10, 14
ACT_PANELS = 18
W_QKV, W_OUT, W_UP, W_DOWN = 0, 3, 4, 8
W_PANELS = 12


def panel(ref, d, p):
    return ref[d, pl.ds(2 * p, 2)].reshape(512, WIDTH)


def put_panel(ref, d, p, value):
    ref[d, pl.ds(2 * p, 2)] = value.astype(BF).reshape(2, 8, 32, WIDTH)


def quarter(ref, d, p, s, quad):
    return ref[d, 2 * p + s, :, :, pl.ds(256 * quad, 256)].reshape(256, 256)


def put_quarter(ref, d, p, s, quad, value):
    ref[d, 2 * p + s, :, :, pl.ds(256 * quad, 256)] = value.astype(BF).reshape(8, 32, 256)


def side_by_side(ref, d, p, count):
    return jnp.concatenate([panel(ref, d, p + c) for c in range(count)], axis=1)


class Piece:
    def __init__(self, own, pair, hop, mine, sems):
        self.own, self.pair, self.hop, self.mine = own, pair, hop, mine
        self.pair_sem, self.send_sem, self.recv_sem = sems

    def pair_copy(self):
        section, _, core, _, _, _, sibling = where_am_i()
        return pltpu.make_async_remote_copy(
            src_ref=self.own(1 - core), dst_ref=self.pair,
            send_sem=self.pair_sem.at[0], recv_sem=self.pair_sem.at[1],
            device_id=(section, sibling), device_id_type=MESH,
        )

    def target(self, way, step):
        place, far = where_am_i()[3], HOPS - step
        return ring_chip((place + (far if way == 0 else CHIPS - far)) % CHIPS)

    def rows(self, way, step):
        return pl.ds(0, 32) if step else pl.ds(16 * way, 16)

    def hop_copy(self, way, step):
        section, _, _, _, ahead, behind, _ = where_am_i()
        return pltpu.make_async_remote_copy(
            src_ref=self.pair.at[:, self.target(way, step), self.rows(way, step), :],
            dst_ref=self.hop(way, step),
            send_sem=self.send_sem.at[way, step], recv_sem=self.recv_sem.at[way, step],
            device_id=(section, ahead if way == 0 else behind), device_id_type=MESH,
        )

    def both(self, n, at, rows):
        core = where_am_i()[2]
        return self.own(core)[n, at, rows, :].astype(F32) + self.pair[n, at, rows, :].astype(F32)

    def each(self, body):
        def run(n, _):
            body(n)
            return 0

        lax.fori_loop(0, self.pair.shape[0], run, 0)

    def send(self, step):
        for way in range(2):
            if step:
                self.hop_copy(way, step - 1).wait()
            at = self.target(way, step)

            def add(n):
                for half in range(2):
                    if step == 0 and half != way:
                        continue
                    rows = pl.ds(16 * half, 16)
                    value = self.both(n, at, rows)
                    if step == 1 and half == way:
                        value += self.hop(way, 0)[n].astype(F32)
                    elif step > 1:
                        value += self.hop(way, step - 1)[n, rows, :].astype(F32)
                    self.pair[n, at, rows, :] = value.astype(BF)

            self.each(add)
            self.hop_copy(way, step).start()

    def close(self):
        at = ring_chip(where_am_i()[3])
        for way in range(2):
            self.hop_copy(way, HOPS - 1).wait()

        def add(n):
            value = self.both(n, at, pl.ds(0, 32))
            for way in range(2):
                value += self.hop(way, HOPS - 1)[n].astype(F32)
            self.mine[n] = value.astype(self.mine.dtype)

        self.each(add)


class Stream:
    def __init__(self, pieces, crossings):
        self.pieces, self.crossings = pieces, crossings

    def pair(self):
        for piece in self.pieces:
            piece.pair_copy().start()

    def open(self):
        for piece in self.pieces:
            piece.pair_copy().wait()
            piece.send(0)

    def send(self, step):
        for piece in self.pieces:
            piece.send(step)

    def close(self):
        for piece in self.pieces:
            piece.close()
        for crossing in self.crossings:
            cross_copy(*crossing).start()


class Traffic:
    def __init__(self, plan):
        self.queue, self.plan = [], plan

    def add(self, stream):
        self.queue.append((stream, 1))

    def take(self, count=None):
        if count is None:
            count, self.plan = int(self.plan[0]), self.plan[1:]
        hops = []
        while count and self.queue:
            stream, step = self.queue.pop(0)
            hops.append((stream, step))
            if step < HOPS:
                self.queue.append((stream, step + 1))
            count -= 1
        return hops


def issue(hops):
    for stream, step in hops:
        if step < HOPS:
            stream.send(step)
        else:
            stream.close()


def train_kernel(
    tok, cot_h, lens, gains, shifts, wq_h, wo_h, wu_h, wd_h, xl_h, bl_h, z1_h, z2_h, w2, ids,
    act, eg, late, early, norm, enc, misc,
    wts, acts, hop1, xin, mid, bias, back_att, lng, cot, act_mine, act_theirs,
    mine1, theirs1, mine0, theirs0, lnown, lnpair, lnhop, lnmine, lntheirs,
    genc, enc_mine, miscown, miscpair, mischop, miscmine, acc2, acc1, dpool,
    load_sem, stream_sem, cross_sem, pair_sem, send_sem, recv_sem, free_sem,
):
    section, me, core, _, ahead, behind, sibling = where_am_i()
    greet()
    cot_copy = cross_copy(cot_h, cot, cross_sem.at[0])
    cot_copy.start()
    act_copy = cross_copy(act_mine, act_theirs, cross_sem.at[1])
    for d in range(2):
        for c in range(W_PANELS):
            if c < 3:
                src = wq_h.at[d, :, :, :, pl.ds(512 * c, 512)]
            elif c == 3:
                src = wo_h.at[d]
            elif c < 8:
                src = wu_h.at[d, :, :, :, pl.ds(512 * (c - 4), 512)]
            else:
                src = wd_h.at[d, pl.ds(2 * (c - 8), 2)]
            pltpu.make_async_copy(src, wts.at[d, pl.ds(2 * c, 2)], load_sem.at[d, c]).start()

    xin[0] = tok[...].astype(F32)
    row, col = iota((256, 1), 0), iota((1, 256), 1)
    q_step = ((row * 10923) >> 16).astype(F32)
    k_step = ((col * 10923) >> 16).astype(F32)
    for s in range(2):
        inv = 1.0 / lens[section, s].astype(F32)
        q_seq = jnp.floor((q_step + 0.5) * inv)
        k_seq = jnp.floor((k_step + 0.5) * inv)
        bias[s] = jnp.where((k_step <= q_step) & (q_seq == k_seq), 0.0, -1e30)
    def loaded(d, first, count):
        for c in range(first, first + count):
            at = wts.at[d, pl.ds(2 * c, 2)]
            pltpu.make_async_copy(at, at, load_sem.at[d, c]).wait()

    def forward(d, _):
        loaded(d, W_QKV, 3)
        hat, _ = ln_parts(xin[d])
        normed = (hat * gains[d, 0:1] + shifts[d, 0:1]).astype(BF)
        put_panel(acts, d, ACT_NORMED, normed)
        for c in range(3):
            put_panel(acts, d, ACT_Q + c, dot(normed, panel(wts, d, W_QKV + c)))
        for s in range(2):
            for quad in range(2):
                q = stacked(quarter(acts, d, ACT_Q, s, quad), HEAD_DIM**-0.5)
                k = quarter(acts, d, ACT_Q + 1, s, quad)
                v = quarter(acts, d, ACT_Q + 2, s, quad)
                scores = dot_lanes(q, k).reshape(4, 256, 256) + bias[s][None]
                top = jnp.max(scores, axis=-1, keepdims=True)
                e = jnp.exp(scores - top)
                total = jnp.sum(e, axis=-1, keepdims=True)
                p = (e * (1.0 / total)).astype(BF)
                for h in range(4):
                    put_quarter(acts, d, ACT_PROBS + s * 2 + quad, h // 2, h % 2, p[h])
                out = unstacked(dot(p.reshape(1024, 256), v))
                put_quarter(acts, d, ACT_ATT, s, quad, out)
        loaded(d, W_OUT, 1)
        middle = xin[d] + dot(panel(acts, d, ACT_ATT), panel(wts, d, W_OUT))
        mid[d] = middle
        loaded(d, W_UP, 4)
        hat, _ = ln_parts(middle)
        put_panel(acts, d, ACT_NORMED2, hat * gains[d, 1:2] + shifts[d, 1:2])

        def chunk(c, _):
            value, grad = gelu_pair(dot(panel(acts, d, ACT_NORMED2), panel(wts, d, W_UP + c)))
            put_panel(acts, d, ACT_GATED + c, value)
            put_panel(acts, d, ACT_SLOPE + c, grad)
            return 0

        lax.fori_loop(0, 4, chunk, 0, unroll=True)
        loaded(d, W_DOWN, 4)
        down = wts[d, pl.ds(2 * W_DOWN, 8)].reshape(4 * WIDTH, WIDTH)
        xin[d + 1] = mid[d] + dot(side_by_side(acts, d, ACT_GATED, 4), down)
        return 0

    lax.fori_loop(0, 2, forward, 0)
    act_mine[...] = xin[2].astype(BF)
    cot_copy.wait()
    act_copy.start()
    up = xin.at[2]
    wide = cot[...].astype(F32)
    for s in range(2):
        up[pl.ds(s * 256, 252), :] = wide[:, s]
        up[pl.ds(s * 256 + 252, 4), :] = jnp.zeros((4, WIDTH), F32)
    lng[...] = jnp.zeros_like(lng)

    def sems(k):
        return pair_sem.at[k], send_sem.at[k], recv_sem.at[k]

    def hop_rows(step):
        return pl.ds(0, 32 if step else 16)

    def piece1(k, first, hop_at):
        return Piece(
            lambda c: acts.at[2, pl.ds(c * 12 + first, 4)],
            acts.at[2, pl.ds(24 + first, 4)],
            lambda way, step: hop1.at[hop_at + step, pl.ds(4 * way, 4), hop_rows(step), :],
            mine1.at[pl.ds(first, 4)], sems(k),
        )

    def piece0(k, first, hop_at):
        return Piece(
            lambda c: acts.at[1, pl.ds(c * 12 + first, 4)],
            acts.at[1, pl.ds(24 + first, 4)],
            lambda way, step: wts.at[1, hop_at + step, pl.ds(4 * way, 4), hop_rows(step), :],
            mine0.at[pl.ds(first, 4)], sems(k),
        )

    def crossing(mine, theirs, first, k):
        return mine.at[pl.ds(first, 4)], theirs.at[pl.ds(first, 4)], cross_sem.at[k]

    down1 = Stream([piece1(0, W_DOWN, 0)], [crossing(mine1, theirs1, W_DOWN, 2)])
    up1 = Stream([piece1(1, W_UP, HOPS)], [crossing(mine1, theirs1, W_UP, 3)])
    att1 = Stream([piece1(2, 0, 2 * HOPS)], [crossing(mine1, theirs1, 0, 4)])
    down0 = Stream([piece0(3, W_DOWN, 0)], [crossing(mine0, theirs0, W_DOWN, 5)])
    up0 = Stream([piece0(4, W_UP, HOPS)], [crossing(mine0, theirs0, W_UP, 6)])
    norms = Piece(
        lambda c: lnown.at[c], lnpair, lambda way, step: lnhop.at[way, step, :, hop_rows(step), :], lnmine, sems(5)
    )
    att0 = Stream(
        [piece0(6, 0, 2 * HOPS), norms],
        [crossing(mine0, theirs0, 0, 7), (lnmine, lntheirs, cross_sem.at[8])],
    )
    encoder = Stream(
        [
            Piece(
                lambda c: genc.at[c], wts.at[1, pl.ds(21, 3)],
                lambda way, step: wts.at[1, 3 * HOPS + step, pl.ds(4 * way, 3), hop_rows(step), :],
                enc_mine, sems(7),
            ),
            Piece(
                lambda c: miscown.at[c], miscpair, lambda way, step: mischop.at[way, step, :, hop_rows(step), :],
                miscmine, sems(8),
            ),
        ],
        [],
    )
    traffic = Traffic(PLAN)

    def split(value):
        return value.astype(BF).reshape(8, 2, 32, WIDTH)

    layer_streams = {1: (down1, up1, att1), 0: (down0, up0, att0)}
    plan = {}
    for d in (1, 0):
        for n in range(8):
            plan[d, n] = traffic.take()
        traffic.add(layer_streams[d][0])
        traffic.add(layer_streams[d][1])
        for n in range(8, 13):
            plan[d, n] = traffic.take()
        if d == 1:
            traffic.add(att1)
            plan[d, 13] = traffic.take()

    def backward(i, _):
        d = 1 - i

        def each(act):
            for which in (1, 0):
                pl.when(d == which)(functools.partial(act, layer_streams[which]))

        def tick(n):
            for which in (1, 0):
                if plan[which, n]:
                    pl.when(d == which)(functools.partial(issue, plan[which, n]))

        def put(p, value):
            shaped = split(value)
            for c in range(2):
                acts[d + 1, c * 12 + p] = shaped[:, c]

        down = up[...].astype(BF)
        for c in range(4):
            part = dot_rows(panel(acts, d, ACT_GATED + c), down).astype(BF).reshape(4, 4, 32, WIDTH)
            for e in range(4):
                for j in range(4):
                    acts[d + 1, (e % 2) * 12 + W_DOWN + j, 2 * c + e // 2] = part[e, j]
            tick(c)

        @pl.when(d == 0)
        def _():
            pl.semaphore_wait(free_sem, 3)

        each(lambda streams: streams[0].pair())
        for c in range(4):
            back = dot_lanes(down, panel(wts, d, W_DOWN + c))
            back = (back * panel(acts, d, ACT_SLOPE + c).astype(F32)).astype(BF)
            put_panel(acts, d, ACT_SLOPE + c, back)
            put(W_UP + c, dot_rows(panel(acts, d, ACT_NORMED2), back))
            tick(4 + c)
        each(lambda streams: streams[1].pair())
        each(lambda streams: streams[0].open())
        back = dot_lanes(side_by_side(acts, d, ACT_SLOPE, 4), side_by_side(wts, d, W_UP, 4))
        back, gain, shift = ln_back(mid[d], back, gains[d, 1:2])
        lng[pl.ds(d * 4 + 1, 1), :] = gain
        lng[pl.ds(d * 4 + 3, 1), :] = shift
        up[...] += back
        branch = up[...].astype(BF)
        put(W_OUT, dot_rows(panel(acts, d, ACT_ATT), branch))
        back_att[...] = dot_lanes(branch, panel(wts, d, W_OUT)).astype(BF)
        each(lambda streams: streams[1].open())
        for s in range(2):
            for quad in range(2):
                rows, lanes = pl.ds(s * 256, 256), pl.ds(quad * 256, 256)
                qs = stacked(quarter(acts, d, ACT_Q, s, quad), HEAD_DIM**-0.5)
                k = quarter(acts, d, ACT_Q + 1, s, quad)
                v = quarter(acts, d, ACT_Q + 2, s, quad)
                outs = stacked(back_att[rows, lanes], 1.0)
                at = ACT_PROBS + s * 2 + quad
                p = jnp.concatenate([quarter(acts, d, at, h // 2, h % 2) for h in range(4)], axis=0)
                dp = dot_lanes(outs, v)
                pf = p.astype(F32)
                weighted = pf * dp
                total = jnp.sum(weighted, axis=-1, keepdims=True)
                ds = (weighted - pf * total).astype(BF)
                put_quarter(acts, d, ACT_Q, s, quad, unstacked(dot(ds, k)) * HEAD_DIM**-0.5)
                put_quarter(acts, d, ACT_Q + 1, s, quad, dot_rows(ds, qs))
                put_quarter(acts, d, ACT_Q + 2, s, quad, dot_rows(p, outs))
                tick(8 + 2 * s + quad)
        for c in range(3):
            put(c, dot_rows(panel(acts, d, ACT_NORMED), panel(acts, d, ACT_Q + c)))
        each(lambda streams: streams[2].pieces[0].pair_copy().start())
        tick(12)
        back = dot_lanes(side_by_side(acts, d, ACT_Q, 3), side_by_side(wts, d, W_QKV, 3))
        back, gain, shift = ln_back(xin[d], back, gains[d, 0:1])
        lng[pl.ds(d * 4, 1), :] = gain
        lng[pl.ds(d * 4 + 2, 1), :] = shift
        up[...] += back

        @pl.when(d == 1)
        def _():
            for target in (sibling, ahead, behind):
                pl.semaphore_signal(
                    free_sem, inc=1, device_id=(section, target), device_id_type=MESH
                )
            att1.open()
            issue(plan[1, 13])

        return 0

    lax.fori_loop(0, 2, backward, 0)
    eg[...] = up[...].astype(BF)
    turned = jnp.transpose(lng[...]).astype(BF).reshape(8, 2, 32, 128)
    for c in range(2):
        lnown[c, 0] = turned[:, c]
    norms.pair_copy().start()

    def fetch(k):
        i, half = k // 2, k % 2
        base = 16 * half
        copies = []
        for n, (src, lanes) in enumerate(((xl_h, 256), (bl_h, 512), (z1_h, 512), (z2_h, 512))):
            copies.append(
                pltpu.make_async_copy(
                    src.at[i, pl.ds(4 * half, 4)],
                    acts.at[0, pl.ds(base + 4 * n, 4), pl.ds(0, 7), :, pl.ds(0, lanes)],
                    stream_sem.at[half, n],
                )
            )
        return copies

    for copy in fetch(0):
        copy.start()
    att0.open()
    traffic.add(att0)
    hot = jnp.where(iota((512, TABLE), 1) == ids[...], 1.0, 0.0).astype(BF)
    code = dot_rows(eg[...], hot)
    for c in range(2):
        for half in range(2):
            genc[c, 1 + half] = split(code[:, 512 * half : 512 * (half + 1)])[:, c]
        miscown[c, 0] = code[:, CODES:].astype(BF).reshape(8, 2, 32, 128)[:, c]
    dpool[...] = dot_rows(hot[:, POOL_AT : POOL_AT + 96], eg[...])
    issue(traffic.take())
    rows = 4 * BLOCK_ROWS

    def held(ref, d, at, lanes=512):
        return ref[d, pl.ds(at, 4), pl.ds(0, 7), :, pl.ds(0, lanes)].reshape(rows, lanes)

    enc_plan = [(k, half, traffic.take()) for k in range(6) for half in range(2)]
    acc2[...] = jnp.zeros_like(acc2)
    acc1[...] = jnp.zeros_like(acc1)

    def block(k, _):
        base = 16 * (k % 2)

        def tick(half):
            for at, when, hops in enc_plan:
                if hops and when == half:
                    pl.when(k == at)(functools.partial(issue, hops))

        for copy in fetch(k):
            copy.wait()

        @pl.when(k < 5)
        def _():
            for copy in fetch(k + 1):
                copy.start()

        pooled = dpool[pl.ds(pl.multiple_of((k // 2) * 32, 32), FRAMES_BLOCK), :] * (1.0 / 64.0)
        wide = jnp.broadcast_to(pooled[:, None, :], (FRAMES_BLOCK, 8, WIDTH))
        wide = wide.reshape(BLOCK_ROWS, WIDTH)

        def part(bx, _):
            value = acts[0, base + 12 + bx, pl.ds(0, 7)].reshape(BLOCK_ROWS, WIDTH)
            back = (wide * gelu_slope(value)).astype(BF)
            wts[0, bx, pl.ds(0, 7)] = back.reshape(7, 32, WIDTH)
            value = acts[0, base + 8 + bx, pl.ds(0, 7)].reshape(BLOCK_ROWS, WIDTH)
            back = (dot_lanes(back, w2[...]) * gelu_slope(value)).astype(BF)
            wts[0, 4 + bx, pl.ds(0, 7)] = back.reshape(7, 32, WIDTH)
            return 0

        lax.fori_loop(0, 4, part, 0)
        tick(0)
        second = dot_rows(held(wts, 0, 0), held(acts, 0, base + 4))
        back = held(wts, 0, 4)
        patch = held(acts, 0, base, 256)
        first = [
            dot_rows(patch[:, 128 * dy2 : 128 * (dy2 + 1)], back[:, 256 * dy2 : 256 * (dy2 + 1)])
            for dy2 in range(2)
        ]
        first = first[0] + first[1]
        acc2[...] += second
        acc1[...] += first
        tick(1)
        return 0

    lax.fori_loop(0, 6, block, 0)
    shaped = split(acc2[...])
    hot, rest = patch_index(128)
    first = jnp.where(rest[:, :1] < 12, acc1[:, pl.ds(0, 128)], acc1[:, pl.ds(128, 128)])
    first = lax.dot_general(
        first, hot, (((0,), (0,)), ((), ())), preferred_element_type=F32,
        precision=lax.Precision.HIGHEST,
    )
    first = first.reshape(8, 2, 8, 48)
    first = jnp.concatenate([first, jnp.zeros((8, 2, 24, 48), F32)], axis=2).astype(BF)
    for c in range(2):
        genc[c, 0] = shaped[:, c]
        miscown[c, 0, :, :, pl.ds(64, 48)] = first[:, c]
    encoder.pair()
    issue(traffic.take())
    encoder.open()
    traffic.add(encoder)
    issue(traffic.take(99))
    for stream in (down1, up1, att1, down0, up0, att0):
        for crossed in stream.crossings:
            cross_copy(*crossed).wait()
    act_copy.wait()
    act[...] = act_theirs[...]
    late[...] = theirs1[...]
    early[...] = theirs0[...]
    norm[...] = lntheirs[0]
    enc[...] = enc_mine[...]
    misc[...] = miscmine[0]


def train(tok, cot, lens, gains, shifts, wq, wo, wu, wd, xl, bl, g1, g2, w2, ids):
    vm = pl.BlockSpec(memory_space=pltpu.VMEM)
    sm = pl.BlockSpec(memory_space=pltpu.SMEM)
    hb = pl.BlockSpec(memory_space=pl.ANY)

    def panels(w):
        return w.reshape(2, w.shape[1] // 256, 8, 32, w.shape[2])

    def parts(saved):
        return saved.reshape(saved.shape[0], 8, 7, 32, saved.shape[2])

    half = (8, 32, WIDTH)
    pieces = 9
    return pl.pallas_call(
        train_kernel,
        in_specs=[vm, hb, sm, vm, vm] + [hb] * 8 + [vm, vm],
        out_specs=[vm] * 7,
        out_shape=[
            jax.ShapeDtypeStruct((512, WIDTH), BF),
            jax.ShapeDtypeStruct((512, WIDTH), BF),
            jax.ShapeDtypeStruct((12, 32, WIDTH), BF),
            jax.ShapeDtypeStruct((12, 32, WIDTH), BF),
            jax.ShapeDtypeStruct((32, 128), BF),
            jax.ShapeDtypeStruct((3, 32, WIDTH), BF),
            jax.ShapeDtypeStruct((32, 128), BF),
        ],
        scratch_shapes=[
            pltpu.VMEM((2, 2 * W_PANELS) + half, BF),
            pltpu.VMEM((3, 2 * ACT_PANELS) + half, BF),
            pltpu.VMEM((3 * HOPS,) + half, BF),
            pltpu.VMEM((3, 512, WIDTH), F32),
            pltpu.VMEM((2, 512, WIDTH), F32),
            pltpu.VMEM((2, 256, 256), F32),
            pltpu.VMEM((512, WIDTH), BF),
            pltpu.VMEM((128, WIDTH), F32),
            pltpu.VMEM(cot.shape, BF),
            pltpu.VMEM((512, WIDTH), BF),
            pltpu.VMEM((512, WIDTH), BF),
            pltpu.VMEM((12, 32, WIDTH), BF),
            pltpu.VMEM((12, 32, WIDTH), BF),
            pltpu.VMEM((12, 32, WIDTH), BF),
            pltpu.VMEM((12, 32, WIDTH), BF),
            pltpu.VMEM((2, 1, 8, 32, 128), BF),
            pltpu.VMEM((1, 8, 32, 128), BF),
            pltpu.VMEM((2, HOPS, 1, 32, 128), BF),
            pltpu.VMEM((1, 32, 128), BF),
            pltpu.VMEM((1, 32, 128), BF),
            pltpu.VMEM((2, 3) + half, BF),
            pltpu.VMEM((3, 32, WIDTH), BF),
            pltpu.VMEM((2, 1, 8, 32, 128), BF),
            pltpu.VMEM((1, 8, 32, 128), BF),
            pltpu.VMEM((2, HOPS, 1, 32, 128), BF),
            pltpu.VMEM((1, 32, 128), BF),
            pltpu.VMEM((512, WIDTH), F32),
            pltpu.VMEM((128, 256), F32),
            pltpu.VMEM((96, WIDTH), F32),
            pltpu.SemaphoreType.DMA((2, W_PANELS)),
            pltpu.SemaphoreType.DMA((2, 4)),
            pltpu.SemaphoreType.DMA((9, 2)),
            pltpu.SemaphoreType.DMA((pieces, 2)),
            pltpu.SemaphoreType.DMA((pieces, 2, HOPS)),
            pltpu.SemaphoreType.DMA((pieces, 2, HOPS)),
            pltpu.SemaphoreType.REGULAR,
        ],
        compiler_params=pltpu.CompilerParams(
            collective_id=2, has_side_effects=True, vmem_limit_bytes=TRAIN_VMEM
        ),
        name="train",
    )(
        tok, cot, lens, gains, shifts, panels(wq), panels(wo), panels(wu), panels(wd),
        parts(xl), parts(bl), parts(g1), parts(g2), w2, ids,
    )


def outputs_kernel(act_in, eg_in, late, early, norm, enc, misc, *outs):
    act, eg, qkv, out, up, down, gain, bias, bias2, enc1, enc2, book, names = outs
    for source, target in ((act_in, act), (eg_in, eg)):
        slots = [source[pl.ds(s * 256, 256), :].astype(F32)[:252] for s in range(2)]
        target[0] = jnp.stack(slots, axis=1).astype(BF)
    for d, rows in enumerate((early, late)):
        for c in range(3):
            qkv[0, d, :, pl.ds(512 * c, 512)] = rows[W_QKV + c].astype(F32)
        out[0, d] = rows[W_OUT].astype(F32)
        for c in range(4):
            up[0, d, :, pl.ds(512 * c, 512)] = rows[W_UP + c].astype(F32)
            down[0, d, pl.ds(32 * c, 32), :] = rows[W_DOWN + c].astype(F32)
    turned = turn(norm[...].astype(F32))
    for d in range(2):
        gain[0, d] = turned[4 * d : 4 * d + 2]
        bias[0, pl.ds(d, 1)] = turned[4 * d + 2 : 4 * d + 3]
        bias2[0, pl.ds(d, 1)] = turned[4 * d + 3 : 4 * d + 4]
    enc2[0] = enc[0].astype(F32)
    for c in range(2):
        book[0, :, pl.ds(512 * c, 512)] = enc[1 + c].astype(F32)
    enc1[0] = misc[...].astype(F32)[:8, 64:112]
    turned = turn(misc[...].astype(F32))
    for a in range(17):
        names[a] = turned[a : a + 1]


def spread_outputs(*parts):
    vm = pl.BlockSpec(memory_space=pltpu.VMEM)
    shapes = [
        (1, 2, 32, 1536), (1, 2, 32, 512), (1, 2, 32, 2048), (1, 2, 128, 512), (1, 2, 2, 32),
        (1, 2, 32), (1, 2, 32), (1, 8, 48), (1, 32, 512), (1, 32, 1024), (17, 1, 32),
    ]
    acts = [jax.ShapeDtypeStruct((1, 252, 2, WIDTH), BF)] * 2
    outs = pl.pallas_call(
        outputs_kernel,
        in_specs=[vm] * len(parts),
        out_specs=[vm] * (len(shapes) + 2),
        out_shape=acts + [jax.ShapeDtypeStruct(shape, F32) for shape in shapes],
        compiler_params=pltpu.CompilerParams(vmem_limit_bytes=VMEM_LIMIT),
        name="outputs",
    )(*parts)
    outs = [x.transpose(0, 2, 1, 3) for x in outs[:2]] + list(outs[2:])
    outs[6] = outs[6].transpose(0, 1, 3, 2)
    for k in (9, 10, 11):
        outs[k] = outs[k].transpose(0, 2, 1)
    outs[12] = outs[12].transpose(1, 0, 2)
    return tuple(outs)


def swap(array):
    return lax.ppermute(array, "section", [(0, 1), (1, 0)])


def whole_rows(g):
    return g.transpose(1, 0, 2, 3).reshape(512, g.shape[-1])


def scatter_plain(g, gl, e):
    def sums(array, axis):
        return lax.psum_scatter(array.astype(F32)[None], "dp", scatter_dimension=axis, tiled=True)

    layers = [whole_rows(g[d]) for d in range(g.shape[0])]
    qkv = jnp.stack([rows[:, :1536] for rows in layers])
    out = jnp.stack([rows[:, 1536:2048] for rows in layers])
    up = jnp.stack([rows[:, 2048:4096] for rows in layers])
    down = jnp.stack(
        [
            rows[:, 4096:].reshape(16, 32, 4, WIDTH).transpose(0, 2, 1, 3).reshape(2048, WIDTH)
            for rows in layers
        ]
    )
    norm = whole_rows(gl)[:, :8].reshape(512, 2, 4).transpose(1, 0, 2)
    enc = whole_rows(e)
    first = e.transpose(1, 0, 2, 3)[:, :, :8, 1600:1648].reshape(128, 48)
    layer_sums = [sums(x, 2) for x in (qkv, out, up, down, norm)]
    layer_sums = [swap(x) for x in layer_sums]
    norm = layer_sums.pop()
    return tuple(layer_sums) + (
        norm[..., 0:2],
        norm[..., 2],
        norm[..., 3],
        sums(first.T, 2),
        sums(enc[:, :512].T, 2),
        sums(enc[:, 512:1536].T, 2),
        sums(enc[:, 1536:1553].T, 2),
    )


def on_device(
    frames, action_ids, delta_ids, seq_len, enc_w1, enc_w2, codebook, action_table,
    ln_gain, ln_bias, w_qkv, w_out, w_up, w_down, cotangent,
):
    micro, steps = frames.shape[1], frames.shape[2]
    count = micro * steps
    gains, shifts = ln_gain.transpose(0, 2, 1), ln_bias.transpose(0, 2, 1)
    tok, ids, xl, blocks, z1, z2 = enc_forward(
        frames.reshape((count,) + frames.shape[3:]), enc_w1, enc_w2, codebook, action_table,
        action_ids[0], delta_ids[0].transpose(0, 2, 1),
    )
    if lax.axis_size("dp") == 2 * CHIPS:
        parts = train(
            tok, cotangent[0].transpose(1, 0, 2), seq_len, gains, shifts, w_qkv, w_out, w_up, w_down,
            xl, blocks, z1, z2, enc_w2, ids,
        )
        return spread_outputs(*parts)
    lnp = jnp.concatenate([gains, shifts], axis=1)
    act, eg, g, gl = run_layers(tok, cotangent[0], seq_len, lnp, w_qkv, w_out, w_up, w_down)
    embed_grad = eg.reshape(micro, 256, WIDTH)[None, :, : steps * TPS]
    e = enc_backward(eg, xl, blocks, z1, z2, enc_w2, ids)
    return (act[None], embed_grad) + scatter_plain(g, gl, e)


def solution(mesh):
    return jax.shard_map(
        on_device,
        mesh=mesh,
        in_specs=(
            P("section", "dp", None, None, None),
            P("section", "dp", None),
            P("section", "dp", None, None),
            P(None, "dp"),
            P(), P(), P(), P(), P(), P(), P(), P(), P(), P(),
            P("section", "dp", None, None),
        ),
        out_specs=(
            P("section", "dp", None, None),
            P("section", "dp", None, None),
            P("section", None, "dp", None),
            P("section", None, "dp", None),
            P("section", None, "dp", None),
            P("section", None, "dp", None),
            P("section", None, "dp", None),
            P("section", None, "dp"),
            P("section", None, "dp"),
            P("section", None, "dp"),
            P("section", None, "dp"),
            P("section", None, "dp"),
            P("section", None, "dp"),
        ),
        check_vma=False,
    )
```

```python
import functools

import jax
import jax.numpy as jnp
from jax import lax
from jax.experimental import pallas as pl
from jax.experimental.pallas import tpu as pltpu
from jax.sharding import PartitionSpec as P

HEADS = 8
HEAD_DIM = 64
TPS = 6
EPS = 1e-05
BF = jnp.bfloat16
F32 = jnp.float32
I32 = jnp.int32

WIDTH = 512
CODES = 1024
FRAMES_BLOCK = 28
BLOCK_ROWS = FRAMES_BLOCK * 8
TABLE = 1152
POOL_AT = 1056
ACT_AT = 1024
LAYER_COLS = 6144
ENC_COLS = 1664
VMEM_LIMIT = 60 << 20
TRAIN_VMEM = 63 << 20
PLAN = "00000000010110010000001111110101010101012"


def dot(a, b):
    return jnp.dot(a, b, preferred_element_type=F32)


def dot_rows(a, b):
    return lax.dot_general(a, b, (((0,), (0,)), ((), ())), preferred_element_type=F32)


def dot_lanes(a, b):
    return lax.dot_general(a, b, (((1,), (1,)), ((), ())), preferred_element_type=F32)


def iota(shape, axis):
    return lax.broadcasted_iota(I32, shape, axis)


def gelu_pair(v):
    cdf = 0.5 + 0.5 * lax.erf(v * 0.7071067811865476)
    bell = jnp.exp2(v * v * (-0.5 * 1.4426950408889634))
    return v * cdf, cdf + v * (bell * 0.3989422804014327)


def gelu(v):
    return v * (0.5 + 0.5 * lax.erf(v * 0.7071067811865476))


def gelu_slope(v):
    return gelu_pair(v.astype(F32))[1]


def patch_index(rows):
    k = iota((rows, 48), 0)
    dy = (k * 2731) >> 16
    rest = k - dy * 24
    j = jnp.where(rest >= 12, rest - 12, rest)
    return jnp.where((iota((rows, 48), 1) == dy * 12 + j) & (k < 96), 1.0, 0.0), rest


def encoder_weights(w1):
    hot, rest = patch_index(128)
    wide = dot(hot.astype(BF), w1)
    first = jnp.where(rest[:, :1] < 12, wide, 0.0)
    second = jnp.where(rest[:, :1] >= 12, wide, 0.0)
    block = jnp.concatenate([first, second], axis=1)
    zero = jnp.zeros_like(block)
    return jnp.concatenate(
        [jnp.concatenate([block, zero], axis=1), jnp.concatenate([zero, block], axis=1)], axis=0
    ).astype(BF)


def token_ids(s, names, deltas):
    steps = names.shape[1]
    frame = s * steps + iota((1, steps), 1)
    block = (frame * 2341) >> 16
    pool = POOL_AT + block * 32 + frame - FRAMES_BLOCK * block
    kinds = jnp.concatenate([pool, names[s : s + 1] + ACT_AT, deltas[s]], axis=0).astype(F32)
    row = iota((256, 1), 0)
    step = (row * 10923) >> 16
    hot = jnp.where(iota((256, steps), 1) == step, 1.0, 0.0)
    each = lax.dot_general(
        hot, kinds, (((1,), (1,)), ((), ())), preferred_element_type=F32,
        precision=lax.Precision.HIGHEST,
    )
    mine = jnp.where(iota((256, TPS), 1) == row - TPS * step, each, 0.0)
    found = (jnp.sum(mine, axis=1, keepdims=True) + 0.5).astype(I32)
    return jnp.where(row < TPS * steps, found, -1)


def enc_fwd_kernel(
    frames, w1, w2, book, acts, names, deltas,
    tok, ids, xl_h, bl_h, z1_h, z2_h,
    perm, lanes, big, xs, acc, table, xl, blocks, z1, z2, sem, book_sem,
):
    step = pl.program_id(0)
    book_copy = pltpu.make_async_copy(book, table.at[pl.ds(0, CODES)], book_sem)

    def part_rows(bx):
        return pl.ds(pl.multiple_of(bx * BLOCK_ROWS, BLOCK_ROWS), BLOCK_ROWS)

    def save(at, bx):
        rows = part_rows(bx)
        return [
            pltpu.make_async_copy(held.at[at, rows], out.at[at, rows], sem.at[at, bx, n])
            for n, (held, out) in enumerate(((blocks, bl_h), (z1, z1_h), (z2, z2_h)))
        ]

    def save_patches(at):
        return pltpu.make_async_copy(xl.at[at], xl_h.at[at], sem.at[at, 0, 3])

    @pl.when(step == 0)
    def _():
        a, b = iota((256, 256), 0), iota((256, 256), 1)
        perm[...] = jnp.where(b == 8 * (a & 31) + (a >> 5), 1.0, 0.0).astype(BF)
        src = iota((256, 1024), 0)
        px = (src * 5462) >> 16
        at = (px >> 1) * 128 + (px & 1) * 12 + (src - px * 12)
        out = jnp.where(src < 192, iota((256, 1024), 1) - at, -1)
        for dy in range(4):
            lanes[pl.ds(256 * dy, 256), :] = jnp.where(out == dy * 24, 1.0, 0.0).astype(BF)
        xs[...] = jnp.zeros_like(xs)
        big[...] = encoder_weights(w1[...])
        book_copy.start()
        named = acts[...].astype(F32)
        pad = jnp.zeros((TABLE - ACT_AT - named.shape[0], WIDTH), F32)
        table[pl.ds(ACT_AT, TABLE - ACT_AT), :] = jnp.concatenate([named, pad], axis=0).astype(BF)

    for group in range(FRAMES_BLOCK // 4):
        rows = frames[pl.ds(group * 4, 4)].reshape(256, 192)
        moved = dot(perm[...], rows).astype(BF).reshape(2, 4, 32, 192)
        for dy in range(4):
            xs[:, pl.ds(group * 32, 32), pl.ds(256 * dy, 192)] = moved[:, dy]
    for dy2 in range(2):
        spread = dot(xs[dy2], lanes[...]).astype(BF)
        for bx in range(8):
            xl[step, pl.ds(bx * BLOCK_ROWS, BLOCK_ROWS), pl.ds(dy2 * 128, 128)] = spread[
                :, bx * 128 : (bx + 1) * 128
            ]
    save_patches(step).start()
    acc[...] = jnp.zeros_like(acc)

    def part(bx, _):
        rows = part_rows(bx)
        first = dot(xl[step, rows, :], big[...])
        z1[step, rows, :] = first.astype(BF)
        value = gelu(first).astype(BF)
        blocks[step, rows, :] = value
        second = dot(value, w2[...])
        z2[step, rows, :] = second.astype(BF)
        acc[...] += gelu(second)
        for copy in save(step, bx):
            copy.start()
        return 0

    lax.fori_loop(0, 8, part, 0, unroll=True)
    pooled = jnp.sum(acc[...].reshape(FRAMES_BLOCK, 8, WIDTH), axis=1) * (1.0 / 64.0)
    pooled = jnp.concatenate([pooled, jnp.zeros((32 - FRAMES_BLOCK, WIDTH), F32)], axis=0)
    table[pl.ds(pl.multiple_of(POOL_AT + step * 32, 32), 32), :] = pooled.astype(BF)

    @pl.when(step == pl.num_programs(0) - 1)
    def _():
        book_copy.wait()
        for s in range(2):
            rows = pl.ds(s * 256, 256)
            found = token_ids(s, names[...], deltas[...])
            ids[rows, :] = found
            hot = jnp.where(iota((256, TABLE), 1) == found, 1.0, 0.0).astype(BF)
            tok[rows, :] = dot(hot, table[...]).astype(BF)
        for at in range(xl.shape[0]):
            save_patches(at).wait()
            for bx in range(8):
                for copy in save(at, bx):
                    copy.wait()


def enc_forward(frames, w1, w2, book, acts, names, deltas):
    count = frames.shape[0]
    grid = count // FRAMES_BLOCK
    rows = 8 * BLOCK_ROWS

    def whole(shape):
        return pl.BlockSpec(shape, lambda i: (0,) * len(shape))

    hb = pl.BlockSpec(memory_space=pl.ANY)
    return pl.pallas_call(
        enc_fwd_kernel,
        grid=(grid,),
        in_specs=[
            pl.BlockSpec((FRAMES_BLOCK, 64, 192), lambda i: (i, 0, 0)),
            whole(w1.shape),
            whole(w2.shape),
            hb,
            whole(acts.shape),
            whole(names.shape),
            whole(deltas.shape),
        ],
        out_specs=[
            whole((512, WIDTH)), whole((512, 1)), hb, hb, hb, hb,
        ],
        out_shape=[
            jax.ShapeDtypeStruct((512, WIDTH), BF),
            jax.ShapeDtypeStruct((512, 1), I32),
            jax.ShapeDtypeStruct((grid, rows, 256), BF),
            jax.ShapeDtypeStruct((grid, rows, 512), BF),
            jax.ShapeDtypeStruct((grid, rows, 512), BF),
            jax.ShapeDtypeStruct((grid, rows, 512), BF),
        ],
        scratch_shapes=[
            pltpu.VMEM((256, 256), BF),
            pltpu.VMEM((1024, 1024), BF),
            pltpu.VMEM((256, 512), BF),
            pltpu.VMEM((2, BLOCK_ROWS, 1024), BF),
            pltpu.VMEM((BLOCK_ROWS, WIDTH), F32),
            pltpu.VMEM((TABLE, WIDTH), BF),
            pltpu.VMEM((grid, rows, 256), BF),
            pltpu.VMEM((grid, rows, 512), BF),
            pltpu.VMEM((grid, rows, 512), BF),
            pltpu.VMEM((grid, rows, 512), BF),
            pltpu.SemaphoreType.DMA((grid, 8, 4)),
            pltpu.SemaphoreType.DMA,
        ],
        compiler_params=pltpu.CompilerParams(vmem_limit_bytes=VMEM_LIMIT),
        name="enc_fwd",
    )(frames, w1, w2, book, acts, names, deltas)


def ln_parts(x):
    mean = jnp.mean(x, axis=-1, keepdims=True)
    center = x - mean
    var = jnp.mean(center * center, axis=-1, keepdims=True)
    scale = lax.rsqrt(var + EPS)
    return center * scale, scale


def ln_back(x, d, gain):
    hat, scale = ln_parts(x)
    dh = d * gain
    one = jnp.mean(dh, axis=-1, keepdims=True)
    two = jnp.mean(dh * hat, axis=-1, keepdims=True)
    back = scale * (dh - one - hat * two)
    return back, jnp.sum(d * hat, axis=0, keepdims=True), jnp.sum(d, axis=0, keepdims=True)


def head_mask(h):
    lane = iota((1, 256), 1) >> 6
    return lane == h


def stacked(rows, scale):
    out = []
    for h in range(4):
        mask = jnp.where(head_mask(h), scale, 0.0).astype(BF)
        out.append(rows * mask)
    return jnp.concatenate(out, axis=0)


def unstacked(rows):
    out = rows[768:]
    for h in range(3):
        out = jnp.where(head_mask(h), rows[h * 256 : (h + 1) * 256], out)
    return out


def scatter_rows(g, d, cols, value, dests=16):
    shaped = value.astype(BF).reshape(dests // 2, 2, 32, value.shape[1])
    for core in range(2):
        g[d, core, :, :, cols] = shaped[:, core]


def layers_kernel(
    tok, cot_h, lens, lnp, wq_h, wo_h, wu_h, wd_h,
    act, eg, g, gl,
    wq, wo, wu, wd, stream, normed, packed, probs, att, normed2, gated, slope, bias,
    up, back_up, back_att, back_packed, lng, cot, mine, theirs, sems, cross_sem,
):
    layers = wq.shape[0]
    section = lax.axis_index("section")
    barrier = pltpu.get_barrier_semaphore()
    pl.semaphore_signal(
        barrier, inc=1, device_id=(1 - section, lax.axis_index("dp")), device_id_type=MESH
    )
    pl.semaphore_wait(barrier, 1)
    cot_copy = cross_copy(cot_h, cot, cross_sem.at[0])
    cot_copy.start()
    act_copy = cross_copy(mine, theirs, cross_sem.at[1])
    copies = []
    for d in range(layers):
        for k, (src, dst) in enumerate(((wq_h, wq), (wo_h, wo), (wu_h, wu), (wd_h, wd))):
            copy = pltpu.make_async_copy(src.at[d], dst.at[d], sems.at[d, k])
            copy.start()
            copies.append(copy)

    stream[0, 0] = tok[...].astype(F32)
    row = iota((256, 1), 0)
    col = iota((1, 256), 1)
    q_step = ((row * 10923) >> 16).astype(F32)
    k_step = ((col * 10923) >> 16).astype(F32)
    for s in range(2):
        inv = 1.0 / lens[section, s].astype(F32)
        q_seq = jnp.floor((q_step + 0.5) * inv)
        k_seq = jnp.floor((k_step + 0.5) * inv)
        bias[s] = jnp.where((k_step <= q_step) & (q_seq == k_seq), 0.0, -1e30)
    for copy in copies:
        copy.wait()

    def forward(d, _):
        x = stream[d, 0]
        hat, _ = ln_parts(x)
        normed[d] = (hat * lnp[d, 0:1] + lnp[d, 2:3]).astype(BF)
        for c in range(3):
            cols = pl.ds(c * 512, 512)
            packed[d, :, cols] = dot(normed[d], wq[d, :, cols]).astype(BF)
        for s in range(2):
            rows = pl.ds(s * 256, 256)
            for quad in range(2):
                q = stacked(packed[d, rows, pl.ds(quad * 256, 256)], HEAD_DIM**-0.5)
                k = packed[d, rows, pl.ds(512 + quad * 256, 256)]
                v = packed[d, rows, pl.ds(1024 + quad * 256, 256)]
                scores = dot_lanes(q, k).reshape(4, 256, 256) + bias[s][None]
                top = jnp.max(scores, axis=-1, keepdims=True)
                e = jnp.exp(scores - top)
                total = jnp.sum(e, axis=-1, keepdims=True)
                p = (e * (1.0 / total)).astype(BF).reshape(1024, 256)
                probs[d, s * 2 + quad] = p
                att[d, rows, pl.ds(quad * 256, 256)] = unstacked(dot(p, v)).astype(BF)
        middle = stream[d, 0] + dot(att[d], wo[d])
        stream[d, 1] = middle
        hat, _ = ln_parts(middle)
        normed2[d] = (hat * lnp[d, 1:2] + lnp[d, 3:4]).astype(BF)

        def chunk(c, _):
            cols = pl.ds(pl.multiple_of(c * 512, 512), 512)
            value, grad = gelu_pair(dot(normed2[d], wu[d, :, cols]))
            gated[d, :, cols] = value.astype(BF)
            slope[d, :, cols] = grad.astype(BF)
            return 0

        lax.fori_loop(0, 4, chunk, 0)
        stream[d + 1, 0] = stream[d, 1] + dot(gated[d], wd[d])
        return 0

    lax.fori_loop(0, layers, forward, 0)
    cot_copy.wait()
    mine[...] = stream[layers, 0].astype(BF)
    act_copy.start()
    for s in range(2):
        up[pl.ds(s * 256, 252), :] = cot[s].astype(F32)
        up[pl.ds(s * 256 + 252, 4), :] = jnp.zeros((4, WIDTH), F32)
    lng[...] = jnp.zeros_like(lng)

    def backward(i, _):
        d = layers - 1 - i
        down = up[...].astype(BF)

        def chunk(c, _):
            cols = pl.ds(pl.multiple_of(c * 256, 256), 256)
            part = dot_rows(gated[d, :, cols], down).astype(BF).reshape(2, 4, 32, WIDTH)
            for core in range(2):
                for j in range(4):
                    g[d, core, c, :, pl.ds(4096 + 512 * j, 512)] = part[core, j]
            back = dot_lanes(down, wd[d, cols, :])
            back = (back * slope[d, :, cols].astype(F32)).astype(BF)
            back_up[:, cols] = back
            part = dot_rows(normed2[d], back).astype(BF).reshape(8, 2, 32, 256)
            out = pl.ds(pl.multiple_of(2048 + c * 256, 256), 256)
            for core in range(2):
                g[d, core, :, :, out] = part[:, core]
            return 0

        lax.fori_loop(0, 8, chunk, 0)
        back, gain, shift = ln_back(stream[d, 1], dot_lanes(back_up[...], wu[d]), lnp[d, 1:2])
        lng[pl.ds(d * 4 + 1, 1), :] = gain
        lng[pl.ds(d * 4 + 3, 1), :] = shift
        up[...] += back
        branch = up[...].astype(BF)
        scatter_rows(g, d, pl.ds(1536, 512), dot_rows(att[d], branch))
        back_att[...] = dot_lanes(branch, wo[d]).astype(BF)
        for s in range(2):
            rows = pl.ds(s * 256, 256)
            for quad in range(2):
                lanes = pl.ds(quad * 256, 256)
                qs = stacked(packed[d, rows, lanes], HEAD_DIM**-0.5)
                k = packed[d, rows, pl.ds(512 + quad * 256, 256)]
                v = packed[d, rows, pl.ds(1024 + quad * 256, 256)]
                outs = stacked(back_att[rows, lanes], 1.0)
                p = probs[d, s * 2 + quad]
                dp = dot_lanes(outs, v)
                pf = p.astype(F32)
                weighted = pf * dp
                total = jnp.sum(weighted, axis=-1, keepdims=True)
                ds = (weighted - pf * total).astype(BF)
                back_packed[rows, lanes] = (unstacked(dot(ds, k)) * HEAD_DIM**-0.5).astype(BF)
                back_packed[rows, pl.ds(512 + quad * 256, 256)] = dot_rows(ds, qs).astype(BF)
                back_packed[rows, pl.ds(1024 + quad * 256, 256)] = dot_rows(p, outs).astype(BF)
        for c in range(3):
            cols = pl.ds(c * 512, 512)
            scatter_rows(g, d, cols, dot_rows(normed[d], back_packed[:, cols]))
        back, gain, shift = ln_back(stream[d, 0], dot_lanes(back_packed[...], wq[d]), lnp[d, 0:1])
        lng[pl.ds(d * 4, 1), :] = gain
        lng[pl.ds(d * 4 + 2, 1), :] = shift
        up[...] += back
        return 0

    lax.fori_loop(0, layers, backward, 0)
    eg[...] = up[...].astype(BF)
    act_copy.wait()
    for s in range(2):
        act[s] = theirs[pl.ds(s * 256, 256), :].astype(F32)[:252].astype(BF)
    turned = jnp.transpose(lng[...]).astype(BF).reshape(8, 2, 32, 128)
    for core in range(2):
        gl[core] = turned[:, core]


def run_layers(tok, cot, lens, lnp, wq, wo, wu, wd):
    layers = wq.shape[0]
    vm = pl.BlockSpec(memory_space=pltpu.VMEM)
    sm = pl.BlockSpec(memory_space=pltpu.SMEM)
    hb = pl.BlockSpec(memory_space=pl.ANY)
    rows = 512
    return pl.pallas_call(
        layers_kernel,
        in_specs=[vm, hb, sm, vm, hb, hb, hb, hb],
        out_specs=[vm, vm, vm, vm],
        out_shape=[
            jax.ShapeDtypeStruct((2, 252, WIDTH), BF),
            jax.ShapeDtypeStruct((rows, WIDTH), BF),
            jax.ShapeDtypeStruct((layers, 2, 8, 32, LAYER_COLS), BF),
            jax.ShapeDtypeStruct((2, 8, 32, 128), BF),
        ],
        scratch_shapes=[
            pltpu.VMEM(wq.shape, BF),
            pltpu.VMEM(wo.shape, BF),
            pltpu.VMEM(wu.shape, BF),
            pltpu.VMEM(wd.shape, BF),
            pltpu.VMEM((layers + 1, 2, rows, WIDTH), F32),
            pltpu.VMEM((layers, rows, WIDTH), BF),
            pltpu.VMEM((layers, rows, 3 * WIDTH), BF),
            pltpu.VMEM((layers, 4, 1024, 256), BF),
            pltpu.VMEM((layers, rows, WIDTH), BF),
            pltpu.VMEM((layers, rows, WIDTH), BF),
            pltpu.VMEM((layers, rows, 4 * WIDTH), BF),
            pltpu.VMEM((layers, rows, 4 * WIDTH), BF),
            pltpu.VMEM((2, 256, 256), F32),
            pltpu.VMEM((rows, WIDTH), F32),
            pltpu.VMEM((rows, 4 * WIDTH), BF),
            pltpu.VMEM((rows, WIDTH), BF),
            pltpu.VMEM((rows, 3 * WIDTH), BF),
            pltpu.VMEM((128, WIDTH), F32),
            pltpu.VMEM(cot.shape, BF),
            pltpu.VMEM((rows, WIDTH), BF),
            pltpu.VMEM((rows, WIDTH), BF),
            pltpu.SemaphoreType.DMA((layers, 4)),
            pltpu.SemaphoreType.DMA((2, 2)),
        ],
        compiler_params=pltpu.CompilerParams(
            collective_id=1, has_side_effects=True, vmem_limit_bytes=VMEM_LIMIT
        ),
        name="layers",
    )(tok, cot, lens, lnp, wq, wo, wu, wd)


def enc_bwd_kernel(eg, xl, blocks, g1, g2, w2, ids, e, dpool, bs, bf, acc2, acc1):
    step = pl.program_id(0)

    @pl.when(step == 0)
    def _():
        hot = jnp.where(iota((512, TABLE), 1) == ids[...], 1.0, 0.0).astype(BF)
        code = dot_rows(eg[...], hot[:, :POOL_AT + 96]).astype(BF)
        dpool[...] = dot_rows(hot[:, POOL_AT : POOL_AT + 96], eg[...])
        parts = code[:, :CODES].reshape(8, 2, 32, CODES)
        tail = code[:, CODES : CODES + 128].reshape(8, 2, 32, 128)
        for core in range(2):
            e[core, :, :, pl.ds(512, CODES)] = parts[:, core]
            e[core, :, :, pl.ds(1536, 128)] = tail[:, core]
        acc2[...] = jnp.zeros_like(acc2)
        acc1[...] = jnp.zeros_like(acc1)

    pooled = dpool[pl.ds(pl.multiple_of(step * 32, 32), 32), :][:FRAMES_BLOCK] * (1.0 / 64.0)
    wide = jnp.broadcast_to(pooled[:, None, :], (FRAMES_BLOCK, 8, WIDTH)).reshape(BLOCK_ROWS, WIDTH)

    def part(bx, _):
        rows = pl.ds(pl.multiple_of(bx * BLOCK_ROWS, BLOCK_ROWS), BLOCK_ROWS)
        back = (wide * gelu_slope(g2[0, rows, :])).astype(BF)
        bs[rows, :] = back
        bf[rows, :] = (dot_lanes(back, w2[...]) * gelu_slope(g1[0, rows, :])).astype(BF)
        return 0

    lax.fori_loop(0, 8, part, 0)
    acc2[...] += dot_rows(bs[...], blocks[0])
    for dy2 in range(2):
        acc1[:, pl.ds(dy2 * 256, 256)] += dot_rows(
            xl[0, :, pl.ds(dy2 * 128, 128)], bf[:, pl.ds(dy2 * 256, 256)]
        )

    @pl.when(step == pl.num_programs(0) - 1)
    def _():
        parts = acc2[...].astype(BF).reshape(8, 2, 32, WIDTH)
        both = acc1[:, pl.ds(0, 256)] + acc1[:, pl.ds(256, 256)]
        hot, rest = patch_index(128)
        first = jnp.where(rest[:, :1] < 12, both[:, :128], both[:, 128:])
        first = lax.dot_general(
            first, hot, (((0,), (0,)), ((), ())), preferred_element_type=F32,
            precision=lax.Precision.HIGHEST,
        )
        first = first.reshape(8, 2, 8, 48)
        first = jnp.concatenate([first, jnp.zeros((8, 2, 24, 48), F32)], axis=2).astype(BF)
        for core in range(2):
            e[core, :, :, pl.ds(0, WIDTH)] = parts[:, core]
            e[core, :, :, pl.ds(1536 + 64, 48)] = first[:, core]


def enc_backward(eg, xl, blocks, g1, g2, w2, ids):
    grid, rows, _ = xl.shape

    def whole(shape):
        return pl.BlockSpec(shape, lambda i: (0,) * len(shape))

    def saved(lanes):
        return pl.BlockSpec((1, rows, lanes), lambda i: (i, 0, 0))

    return pl.pallas_call(
        enc_bwd_kernel,
        grid=(grid,),
        in_specs=[
            whole(eg.shape), saved(256), saved(512), saved(512), saved(512),
            whole(w2.shape), whole(ids.shape),
        ],
        out_specs=whole((2, 8, 32, ENC_COLS)),
        out_shape=jax.ShapeDtypeStruct((2, 8, 32, ENC_COLS), BF),
        scratch_shapes=[
            pltpu.VMEM((96, WIDTH), F32),
            pltpu.VMEM((rows, WIDTH), BF),
            pltpu.VMEM((rows, WIDTH), BF),
            pltpu.VMEM((WIDTH, WIDTH), F32),
            pltpu.VMEM((128, WIDTH), F32),
        ],
        compiler_params=pltpu.CompilerParams(vmem_limit_bytes=VMEM_LIMIT),
        name="enc_bwd",
    )(eg, xl, blocks, g1, g2, w2, ids)


CHIPS = 8
HOPS = CHIPS // 2
MESH = pl.DeviceIdType.MESH


def ring_place(chip):
    z, x = chip // 2, chip % 2
    return z * (1 - x) + (7 - z) * x


def ring_chip(place):
    half = place // 4
    return (1 - half) * (2 * place) + half * (15 - 2 * place)


def where_am_i():
    section, me = lax.axis_index("section"), lax.axis_index("dp")
    core, chip = me % 2, me // 2
    place = ring_place(chip)
    ahead = ring_chip((place + 1) % CHIPS) * 2 + core
    behind = ring_chip((place + CHIPS - 1) % CHIPS) * 2 + core
    sibling = chip * 2 + (1 - core)
    return section, me, core, place, ahead, behind, sibling


def greet():
    section, me, _, _, ahead, behind, sibling = where_am_i()
    barrier = pltpu.get_barrier_semaphore()
    for target in ((section, sibling), (section, ahead), (section, behind), (1 - section, me)):
        pl.semaphore_signal(barrier, inc=1, device_id=target, device_id_type=MESH)
    pl.semaphore_wait(barrier, 4)


def cross_copy(src, dst, sem):
    section, me = lax.axis_index("section"), lax.axis_index("dp")
    return pltpu.make_async_remote_copy(
        src_ref=src, dst_ref=dst, send_sem=sem.at[0], recv_sem=sem.at[1],
        device_id=(1 - section, me), device_id_type=MESH,
    )


def turn(rows):
    tall = jnp.concatenate([rows, jnp.zeros((96, rows.shape[1]), F32)], axis=0)
    return jnp.transpose(tall)[:, :32]


ACT_NORMED, ACT_Q, ACT_PROBS, ACT_ATT, ACT_NORMED2, ACT_GATED, ACT_SLOPE = 0, 1, 4, 8, 9, 10, 14
ACT_PANELS = 18
W_QKV, W_OUT, W_UP, W_DOWN = 0, 3, 4, 8
W_PANELS = 12


def panel(ref, d, p):
    return ref[d, pl.ds(2 * p, 2)].reshape(512, WIDTH)


def put_panel(ref, d, p, value):
    ref[d, pl.ds(2 * p, 2)] = value.astype(BF).reshape(2, 8, 32, WIDTH)


def quarter(ref, d, p, s, quad):
    return ref[d, 2 * p + s, :, :, pl.ds(256 * quad, 256)].reshape(256, 256)


def put_quarter(ref, d, p, s, quad, value):
    ref[d, 2 * p + s, :, :, pl.ds(256 * quad, 256)] = value.astype(BF).reshape(8, 32, 256)


def side_by_side(ref, d, p, count):
    return jnp.concatenate([panel(ref, d, p + c) for c in range(count)], axis=1)


class Piece:
    def __init__(self, own, pair, hop, mine, sems):
        self.own, self.pair, self.hop, self.mine = own, pair, hop, mine
        self.pair_sem, self.send_sem, self.recv_sem = sems

    def pair_copy(self):
        section, _, core, _, _, _, sibling = where_am_i()
        return pltpu.make_async_remote_copy(
            src_ref=self.own(1 - core), dst_ref=self.pair,
            send_sem=self.pair_sem.at[0], recv_sem=self.pair_sem.at[1],
            device_id=(section, sibling), device_id_type=MESH,
        )

    def target(self, way, step):
        place, far = where_am_i()[3], HOPS - step
        return ring_chip((place + (far if way == 0 else CHIPS - far)) % CHIPS)

    def rows(self, way, step):
        return pl.ds(0, 32) if step else pl.ds(16 * way, 16)

    def hop_copy(self, way, step):
        section, _, _, _, ahead, behind, _ = where_am_i()
        return pltpu.make_async_remote_copy(
            src_ref=self.pair.at[:, self.target(way, step), self.rows(way, step), :],
            dst_ref=self.hop(way, step),
            send_sem=self.send_sem.at[way, step], recv_sem=self.recv_sem.at[way, step],
            device_id=(section, ahead if way == 0 else behind), device_id_type=MESH,
        )

    def both(self, n, at, rows):
        core = where_am_i()[2]
        return self.own(core)[n, at, rows, :].astype(F32) + self.pair[n, at, rows, :].astype(F32)

    def each(self, body):
        def run(n, _):
            body(n)
            return 0

        lax.fori_loop(0, self.pair.shape[0], run, 0)

    def send(self, step):
        for way in range(2):
            if step:
                self.hop_copy(way, step - 1).wait()
            at = self.target(way, step)

            def add(n):
                for half in range(2):
                    if step == 0 and half != way:
                        continue
                    rows = pl.ds(16 * half, 16)
                    value = self.both(n, at, rows)
                    if step == 1 and half == way:
                        value += self.hop(way, 0)[n].astype(F32)
                    elif step > 1:
                        value += self.hop(way, step - 1)[n, rows, :].astype(F32)
                    self.pair[n, at, rows, :] = value.astype(BF)

            self.each(add)
            self.hop_copy(way, step).start()

    def close(self):
        at = ring_chip(where_am_i()[3])
        for way in range(2):
            self.hop_copy(way, HOPS - 1).wait()

        def add(n):
            value = self.both(n, at, pl.ds(0, 32))
            for way in range(2):
                value += self.hop(way, HOPS - 1)[n].astype(F32)
            self.mine[n] = value.astype(self.mine.dtype)

        self.each(add)


class Stream:
    def __init__(self, pieces, crossings):
        self.pieces, self.crossings = pieces, crossings

    def pair(self):
        for piece in self.pieces:
            piece.pair_copy().start()

    def open(self):
        for piece in self.pieces:
            piece.pair_copy().wait()
            piece.send(0)

    def send(self, step):
        for piece in self.pieces:
            piece.send(step)

    def close(self):
        for piece in self.pieces:
            piece.close()
        for crossing in self.crossings:
            cross_copy(*crossing).start()


class Traffic:
    def __init__(self, plan):
        self.queue, self.plan = [], plan

    def add(self, stream):
        self.queue.append((stream, 1))

    def take(self, count=None):
        if count is None:
            count, self.plan = int(self.plan[0]), self.plan[1:]
        hops = []
        while count and self.queue:
            stream, step = self.queue.pop(0)
            hops.append((stream, step))
            if step < HOPS:
                self.queue.append((stream, step + 1))
            count -= 1
        return hops


def issue(hops):
    for stream, step in hops:
        if step < HOPS:
            stream.send(step)
        else:
            stream.close()


def train_kernel(
    tok, cot_h, lens, gains, shifts, wq_h, wo_h, wu_h, wd_h, xl_h, bl_h, z1_h, z2_h, w2, ids,
    act, eg, late, early, norm, enc, misc,
    wts, acts, hop1, xin, mid, bias, back_att, lng, cot, act_mine, act_theirs,
    mine1, theirs1, mine0, theirs0, lnown, lnpair, lnhop, lnmine, lntheirs,
    genc, enc_mine, miscown, miscpair, mischop, miscmine, acc2, acc1, dpool,
    load_sem, stream_sem, cross_sem, pair_sem, send_sem, recv_sem, free_sem,
):
    section, me, core, _, ahead, behind, sibling = where_am_i()
    greet()
    cot_copy = cross_copy(cot_h, cot, cross_sem.at[0])
    cot_copy.start()
    act_copy = cross_copy(act_mine, act_theirs, cross_sem.at[1])
    for d in range(2):
        for c in range(W_PANELS):
            if c < 3:
                src = wq_h.at[d, :, :, :, pl.ds(512 * c, 512)]
            elif c == 3:
                src = wo_h.at[d]
            elif c < 8:
                src = wu_h.at[d, :, :, :, pl.ds(512 * (c - 4), 512)]
            else:
                src = wd_h.at[d, pl.ds(2 * (c - 8), 2)]
            pltpu.make_async_copy(src, wts.at[d, pl.ds(2 * c, 2)], load_sem.at[d, c]).start()

    xin[0] = tok[...].astype(F32)
    row, col = iota((256, 1), 0), iota((1, 256), 1)
    q_step = ((row * 10923) >> 16).astype(F32)
    k_step = ((col * 10923) >> 16).astype(F32)
    for s in range(2):
        inv = 1.0 / lens[section, s].astype(F32)
        q_seq = jnp.floor((q_step + 0.5) * inv)
        k_seq = jnp.floor((k_step + 0.5) * inv)
        bias[s] = jnp.where((k_step <= q_step) & (q_seq == k_seq), 0.0, -1e30)
    def loaded(d, first, count):
        for c in range(first, first + count):
            at = wts.at[d, pl.ds(2 * c, 2)]
            pltpu.make_async_copy(at, at, load_sem.at[d, c]).wait()

    def forward(d, _):
        loaded(d, W_QKV, 3)
        hat, _ = ln_parts(xin[d])
        normed = (hat * gains[d, 0:1] + shifts[d, 0:1]).astype(BF)
        put_panel(acts, d, ACT_NORMED, normed)
        for c in range(3):
            put_panel(acts, d, ACT_Q + c, dot(normed, panel(wts, d, W_QKV + c)))
        for s in range(2):
            for quad in range(2):
                q = stacked(quarter(acts, d, ACT_Q, s, quad), HEAD_DIM**-0.5)
                k = quarter(acts, d, ACT_Q + 1, s, quad)
                v = quarter(acts, d, ACT_Q + 2, s, quad)
                scores = dot_lanes(q, k).reshape(4, 256, 256) + bias[s][None]
                top = jnp.max(scores, axis=-1, keepdims=True)
                e = jnp.exp(scores - top)
                total = jnp.sum(e, axis=-1, keepdims=True)
                p = (e * (1.0 / total)).astype(BF)
                for h in range(4):
                    put_quarter(acts, d, ACT_PROBS + s * 2 + quad, h // 2, h % 2, p[h])
                out = unstacked(dot(p.reshape(1024, 256), v))
                put_quarter(acts, d, ACT_ATT, s, quad, out)
        loaded(d, W_OUT, 1)
        middle = xin[d] + dot(panel(acts, d, ACT_ATT), panel(wts, d, W_OUT))
        mid[d] = middle
        loaded(d, W_UP, 4)
        hat, _ = ln_parts(middle)
        put_panel(acts, d, ACT_NORMED2, hat * gains[d, 1:2] + shifts[d, 1:2])

        def chunk(c, _):
            value, grad = gelu_pair(dot(panel(acts, d, ACT_NORMED2), panel(wts, d, W_UP + c)))
            put_panel(acts, d, ACT_GATED + c, value)
            put_panel(acts, d, ACT_SLOPE + c, grad)
            return 0

        lax.fori_loop(0, 4, chunk, 0, unroll=True)
        loaded(d, W_DOWN, 4)
        down = wts[d, pl.ds(2 * W_DOWN, 8)].reshape(4 * WIDTH, WIDTH)
        xin[d + 1] = mid[d] + dot(side_by_side(acts, d, ACT_GATED, 4), down)
        return 0

    lax.fori_loop(0, 2, forward, 0)
    act_mine[...] = xin[2].astype(BF)
    cot_copy.wait()
    act_copy.start()
    up = xin.at[2]
    wide = cot[...].astype(F32)
    for s in range(2):
        up[pl.ds(s * 256, 252), :] = wide[:, s]
        up[pl.ds(s * 256 + 252, 4), :] = jnp.zeros((4, WIDTH), F32)
    lng[...] = jnp.zeros_like(lng)

    def sems(k):
        return pair_sem.at[k], send_sem.at[k], recv_sem.at[k]

    def hop_rows(step):
        return pl.ds(0, 32 if step else 16)

    def piece1(k, first, hop_at):
        return Piece(
            lambda c: acts.at[2, pl.ds(c * 12 + first, 4)],
            acts.at[2, pl.ds(24 + first, 4)],
            lambda way, step: hop1.at[hop_at + step, pl.ds(4 * way, 4), hop_rows(step), :],
            mine1.at[pl.ds(first, 4)], sems(k),
        )

    def piece0(k, first, hop_at):
        return Piece(
            lambda c: acts.at[1, pl.ds(c * 12 + first, 4)],
            acts.at[1, pl.ds(24 + first, 4)],
            lambda way, step: wts.at[1, hop_at + step, pl.ds(4 * way, 4), hop_rows(step), :],
            mine0.at[pl.ds(first, 4)], sems(k),
        )

    def crossing(mine, theirs, first, k):
        return mine.at[pl.ds(first, 4)], theirs.at[pl.ds(first, 4)], cross_sem.at[k]

    down1 = Stream([piece1(0, W_DOWN, 0)], [crossing(mine1, theirs1, W_DOWN, 2)])
    up1 = Stream([piece1(1, W_UP, HOPS)], [crossing(mine1, theirs1, W_UP, 3)])
    att1 = Stream([piece1(2, 0, 2 * HOPS)], [crossing(mine1, theirs1, 0, 4)])
    down0 = Stream([piece0(3, W_DOWN, 0)], [crossing(mine0, theirs0, W_DOWN, 5)])
    up0 = Stream([piece0(4, W_UP, HOPS)], [crossing(mine0, theirs0, W_UP, 6)])
    norms = Piece(
        lambda c: lnown.at[c], lnpair, lambda way, step: lnhop.at[way, step, :, hop_rows(step), :], lnmine, sems(5)
    )
    att0 = Stream(
        [piece0(6, 0, 2 * HOPS), norms],
        [crossing(mine0, theirs0, 0, 7), (lnmine, lntheirs, cross_sem.at[8])],
    )
    encoder = Stream(
        [
            Piece(
                lambda c: genc.at[c], wts.at[1, pl.ds(21, 3)],
                lambda way, step: wts.at[1, 3 * HOPS + step, pl.ds(4 * way, 3), hop_rows(step), :],
                enc_mine, sems(7),
            ),
            Piece(
                lambda c: miscown.at[c], miscpair, lambda way, step: mischop.at[way, step, :, hop_rows(step), :],
                miscmine, sems(8),
            ),
        ],
        [],
    )
    traffic = Traffic(PLAN)

    def split(value):
        return value.astype(BF).reshape(8, 2, 32, WIDTH)

    layer_streams = {1: (down1, up1, att1), 0: (down0, up0, att0)}
    plan = {}
    for d in (1, 0):
        for n in range(8):
            plan[d, n] = traffic.take()
        traffic.add(layer_streams[d][0])
        traffic.add(layer_streams[d][1])
        for n in range(8, 13):
            plan[d, n] = traffic.take()
        if d == 1:
            traffic.add(att1)
            plan[d, 13] = traffic.take()

    def backward(i, _):
        d = 1 - i

        def each(act):
            for which in (1, 0):
                pl.when(d == which)(functools.partial(act, layer_streams[which]))

        def tick(n):
            for which in (1, 0):
                if plan[which, n]:
                    pl.when(d == which)(functools.partial(issue, plan[which, n]))

        def put(p, value):
            shaped = split(value)
            for c in range(2):
                acts[d + 1, c * 12 + p] = shaped[:, c]

        down = up[...].astype(BF)
        for c in range(4):
            part = dot_rows(panel(acts, d, ACT_GATED + c), down).astype(BF).reshape(4, 4, 32, WIDTH)
            for e in range(4):
                for j in range(4):
                    acts[d + 1, (e % 2) * 12 + W_DOWN + j, 2 * c + e // 2] = part[e, j]
            tick(c)

        @pl.when(d == 0)
        def _():
            pl.semaphore_wait(free_sem, 3)

        each(lambda streams: streams[0].pair())
        for c in range(4):
            back = dot_lanes(down, panel(wts, d, W_DOWN + c))
            back = (back * panel(acts, d, ACT_SLOPE + c).astype(F32)).astype(BF)
            put_panel(acts, d, ACT_SLOPE + c, back)
            put(W_UP + c, dot_rows(panel(acts, d, ACT_NORMED2), back))
            tick(4 + c)
        each(lambda streams: streams[1].pair())
        each(lambda streams: streams[0].open())
        back = dot_lanes(side_by_side(acts, d, ACT_SLOPE, 4), side_by_side(wts, d, W_UP, 4))
        back, gain, shift = ln_back(mid[d], back, gains[d, 1:2])
        lng[pl.ds(d * 4 + 1, 1), :] = gain
        lng[pl.ds(d * 4 + 3, 1), :] = shift
        up[...] += back
        branch = up[...].astype(BF)
        put(W_OUT, dot_rows(panel(acts, d, ACT_ATT), branch))
        back_att[...] = dot_lanes(branch, panel(wts, d, W_OUT)).astype(BF)
        each(lambda streams: streams[1].open())
        for s in range(2):
            for quad in range(2):
                rows, lanes = pl.ds(s * 256, 256), pl.ds(quad * 256, 256)
                qs = stacked(quarter(acts, d, ACT_Q, s, quad), HEAD_DIM**-0.5)
                k = quarter(acts, d, ACT_Q + 1, s, quad)
                v = quarter(acts, d, ACT_Q + 2, s, quad)
                outs = stacked(back_att[rows, lanes], 1.0)
                at = ACT_PROBS + s * 2 + quad
                p = jnp.concatenate([quarter(acts, d, at, h // 2, h % 2) for h in range(4)], axis=0)
                dp = dot_lanes(outs, v)
                pf = p.astype(F32)
                weighted = pf * dp
                total = jnp.sum(weighted, axis=-1, keepdims=True)
                ds = (weighted - pf * total).astype(BF)
                put_quarter(acts, d, ACT_Q, s, quad, unstacked(dot(ds, k)) * HEAD_DIM**-0.5)
                put_quarter(acts, d, ACT_Q + 1, s, quad, dot_rows(ds, qs))
                put_quarter(acts, d, ACT_Q + 2, s, quad, dot_rows(p, outs))
                tick(8 + 2 * s + quad)
        for c in range(3):
            put(c, dot_rows(panel(acts, d, ACT_NORMED), panel(acts, d, ACT_Q + c)))
        each(lambda streams: streams[2].pieces[0].pair_copy().start())
        tick(12)
        back = dot_lanes(side_by_side(acts, d, ACT_Q, 3), side_by_side(wts, d, W_QKV, 3))
        back, gain, shift = ln_back(xin[d], back, gains[d, 0:1])
        lng[pl.ds(d * 4, 1), :] = gain
        lng[pl.ds(d * 4 + 2, 1), :] = shift
        up[...] += back

        @pl.when(d == 1)
        def _():
            for target in (sibling, ahead, behind):
                pl.semaphore_signal(
                    free_sem, inc=1, device_id=(section, target), device_id_type=MESH
                )
            att1.open()
            issue(plan[1, 13])

        return 0

    lax.fori_loop(0, 2, backward, 0)
    eg[...] = up[...].astype(BF)
    turned = jnp.transpose(lng[...]).astype(BF).reshape(8, 2, 32, 128)
    for c in range(2):
        lnown[c, 0] = turned[:, c]
    norms.pair_copy().start()

    def fetch(k):
        i, half = k // 2, k % 2
        base = 16 * half
        copies = []
        for n, (src, lanes) in enumerate(((xl_h, 256), (bl_h, 512), (z1_h, 512), (z2_h, 512))):
            copies.append(
                pltpu.make_async_copy(
                    src.at[i, pl.ds(4 * half, 4)],
                    acts.at[0, pl.ds(base + 4 * n, 4), pl.ds(0, 7), :, pl.ds(0, lanes)],
                    stream_sem.at[half, n],
                )
            )
        return copies

    for copy in fetch(0):
        copy.start()
    att0.open()
    traffic.add(att0)
    hot = jnp.where(iota((512, TABLE), 1) == ids[...], 1.0, 0.0).astype(BF)
    code = dot_rows(eg[...], hot)
    for c in range(2):
        for half in range(2):
            genc[c, 1 + half] = split(code[:, 512 * half : 512 * (half + 1)])[:, c]
        miscown[c, 0] = code[:, CODES:].astype(BF).reshape(8, 2, 32, 128)[:, c]
    dpool[...] = dot_rows(hot[:, POOL_AT : POOL_AT + 96], eg[...])
    issue(traffic.take())
    rows = 4 * BLOCK_ROWS

    def held(ref, d, at, lanes=512):
        return ref[d, pl.ds(at, 4), pl.ds(0, 7), :, pl.ds(0, lanes)].reshape(rows, lanes)

    enc_plan = [(k, half, traffic.take()) for k in range(6) for half in range(2)]
    acc2[...] = jnp.zeros_like(acc2)
    acc1[...] = jnp.zeros_like(acc1)

    def block(k, _):
        base = 16 * (k % 2)

        def tick(half):
            for at, when, hops in enc_plan:
                if hops and when == half:
                    pl.when(k == at)(functools.partial(issue, hops))

        for copy in fetch(k):
            copy.wait()

        @pl.when(k < 5)
        def _():
            for copy in fetch(k + 1):
                copy.start()

        pooled = dpool[pl.ds(pl.multiple_of((k // 2) * 32, 32), FRAMES_BLOCK), :] * (1.0 / 64.0)
        wide = jnp.broadcast_to(pooled[:, None, :], (FRAMES_BLOCK, 8, WIDTH))
        wide = wide.reshape(BLOCK_ROWS, WIDTH)

        def part(bx, _):
            value = acts[0, base + 12 + bx, pl.ds(0, 7)].reshape(BLOCK_ROWS, WIDTH)
            back = (wide * gelu_slope(value)).astype(BF)
            wts[0, bx, pl.ds(0, 7)] = back.reshape(7, 32, WIDTH)
            value = acts[0, base + 8 + bx, pl.ds(0, 7)].reshape(BLOCK_ROWS, WIDTH)
            back = (dot_lanes(back, w2[...]) * gelu_slope(value)).astype(BF)
            wts[0, 4 + bx, pl.ds(0, 7)] = back.reshape(7, 32, WIDTH)
            return 0

        lax.fori_loop(0, 4, part, 0)
        tick(0)
        second = dot_rows(held(wts, 0, 0), held(acts, 0, base + 4))
        back = held(wts, 0, 4)
        patch = held(acts, 0, base, 256)
        first = [
            dot_rows(patch[:, 128 * dy2 : 128 * (dy2 + 1)], back[:, 256 * dy2 : 256 * (dy2 + 1)])
            for dy2 in range(2)
        ]
        first = first[0] + first[1]
        acc2[...] += second
        acc1[...] += first
        tick(1)
        return 0

    lax.fori_loop(0, 6, block, 0)
    shaped = split(acc2[...])
    hot, rest = patch_index(128)
    first = jnp.where(rest[:, :1] < 12, acc1[:, pl.ds(0, 128)], acc1[:, pl.ds(128, 128)])
    first = lax.dot_general(
        first, hot, (((0,), (0,)), ((), ())), preferred_element_type=F32,
        precision=lax.Precision.HIGHEST,
    )
    first = first.reshape(8, 2, 8, 48)
    first = jnp.concatenate([first, jnp.zeros((8, 2, 24, 48), F32)], axis=2).astype(BF)
    for c in range(2):
        genc[c, 0] = shaped[:, c]
        miscown[c, 0, :, :, pl.ds(64, 48)] = first[:, c]
    encoder.pair()
    issue(traffic.take())
    encoder.open()
    traffic.add(encoder)
    issue(traffic.take(99))
    for stream in (down1, up1, att1, down0, up0, att0):
        for crossed in stream.crossings:
            cross_copy(*crossed).wait()
    act_copy.wait()
    act[...] = act_theirs[...]
    late[...] = theirs1[...]
    early[...] = theirs0[...]
    norm[...] = lntheirs[0]
    enc[...] = enc_mine[...]
    misc[...] = miscmine[0]


def train(tok, cot, lens, gains, shifts, wq, wo, wu, wd, xl, bl, g1, g2, w2, ids):
    vm = pl.BlockSpec(memory_space=pltpu.VMEM)
    sm = pl.BlockSpec(memory_space=pltpu.SMEM)
    hb = pl.BlockSpec(memory_space=pl.ANY)

    def panels(w):
        return w.reshape(2, w.shape[1] // 256, 8, 32, w.shape[2])

    def parts(saved):
        return saved.reshape(saved.shape[0], 8, 7, 32, saved.shape[2])

    half = (8, 32, WIDTH)
    pieces = 9
    return pl.pallas_call(
        train_kernel,
        in_specs=[vm, hb, sm, vm, vm] + [hb] * 8 + [vm, vm],
        out_specs=[vm] * 7,
        out_shape=[
            jax.ShapeDtypeStruct((512, WIDTH), BF),
            jax.ShapeDtypeStruct((512, WIDTH), BF),
            jax.ShapeDtypeStruct((12, 32, WIDTH), BF),
            jax.ShapeDtypeStruct((12, 32, WIDTH), BF),
            jax.ShapeDtypeStruct((32, 128), BF),
            jax.ShapeDtypeStruct((3, 32, WIDTH), BF),
            jax.ShapeDtypeStruct((32, 128), BF),
        ],
        scratch_shapes=[
            pltpu.VMEM((2, 2 * W_PANELS) + half, BF),
            pltpu.VMEM((3, 2 * ACT_PANELS) + half, BF),
            pltpu.VMEM((3 * HOPS,) + half, BF),
            pltpu.VMEM((3, 512, WIDTH), F32),
            pltpu.VMEM((2, 512, WIDTH), F32),
            pltpu.VMEM((2, 256, 256), F32),
            pltpu.VMEM((512, WIDTH), BF),
            pltpu.VMEM((128, WIDTH), F32),
            pltpu.VMEM(cot.shape, BF),
            pltpu.VMEM((512, WIDTH), BF),
            pltpu.VMEM((512, WIDTH), BF),
            pltpu.VMEM((12, 32, WIDTH), BF),
            pltpu.VMEM((12, 32, WIDTH), BF),
            pltpu.VMEM((12, 32, WIDTH), BF),
            pltpu.VMEM((12, 32, WIDTH), BF),
            pltpu.VMEM((2, 1, 8, 32, 128), BF),
            pltpu.VMEM((1, 8, 32, 128), BF),
            pltpu.VMEM((2, HOPS, 1, 32, 128), BF),
            pltpu.VMEM((1, 32, 128), BF),
            pltpu.VMEM((1, 32, 128), BF),
            pltpu.VMEM((2, 3) + half, BF),
            pltpu.VMEM((3, 32, WIDTH), BF),
            pltpu.VMEM((2, 1, 8, 32, 128), BF),
            pltpu.VMEM((1, 8, 32, 128), BF),
            pltpu.VMEM((2, HOPS, 1, 32, 128), BF),
            pltpu.VMEM((1, 32, 128), BF),
            pltpu.VMEM((512, WIDTH), F32),
            pltpu.VMEM((128, 256), F32),
            pltpu.VMEM((96, WIDTH), F32),
            pltpu.SemaphoreType.DMA((2, W_PANELS)),
            pltpu.SemaphoreType.DMA((2, 4)),
            pltpu.SemaphoreType.DMA((9, 2)),
            pltpu.SemaphoreType.DMA((pieces, 2)),
            pltpu.SemaphoreType.DMA((pieces, 2, HOPS)),
            pltpu.SemaphoreType.DMA((pieces, 2, HOPS)),
            pltpu.SemaphoreType.REGULAR,
        ],
        compiler_params=pltpu.CompilerParams(
            collective_id=2, has_side_effects=True, vmem_limit_bytes=TRAIN_VMEM
        ),
        name="train",
    )(
        tok, cot, lens, gains, shifts, panels(wq), panels(wo), panels(wu), panels(wd),
        parts(xl), parts(bl), parts(g1), parts(g2), w2, ids,
    )


def outputs_kernel(act_in, eg_in, late, early, norm, enc, misc, *outs):
    act, eg, qkv, out, up, down, gain, bias, bias2, enc1, enc2, book, names = outs
    for source, target in ((act_in, act), (eg_in, eg)):
        slots = [source[pl.ds(s * 256, 256), :].astype(F32)[:252] for s in range(2)]
        target[0] = jnp.stack(slots, axis=1).astype(BF)
    for d, rows in enumerate((early, late)):
        for c in range(3):
            qkv[0, d, :, pl.ds(512 * c, 512)] = rows[W_QKV + c].astype(F32)
        out[0, d] = rows[W_OUT].astype(F32)
        for c in range(4):
            up[0, d, :, pl.ds(512 * c, 512)] = rows[W_UP + c].astype(F32)
            down[0, d, pl.ds(32 * c, 32), :] = rows[W_DOWN + c].astype(F32)
    turned = turn(norm[...].astype(F32))
    for d in range(2):
        gain[0, d] = turned[4 * d : 4 * d + 2]
        bias[0, pl.ds(d, 1)] = turned[4 * d + 2 : 4 * d + 3]
        bias2[0, pl.ds(d, 1)] = turned[4 * d + 3 : 4 * d + 4]
    enc2[0] = enc[0].astype(F32)
    for c in range(2):
        book[0, :, pl.ds(512 * c, 512)] = enc[1 + c].astype(F32)
    enc1[0] = misc[...].astype(F32)[:8, 64:112]
    turned = turn(misc[...].astype(F32))
    for a in range(17):
        names[a] = turned[a : a + 1]


def spread_outputs(*parts):
    vm = pl.BlockSpec(memory_space=pltpu.VMEM)
    shapes = [
        (1, 2, 32, 1536), (1, 2, 32, 512), (1, 2, 32, 2048), (1, 2, 128, 512), (1, 2, 2, 32),
        (1, 2, 32), (1, 2, 32), (1, 8, 48), (1, 32, 512), (1, 32, 1024), (17, 1, 32),
    ]
    acts = [jax.ShapeDtypeStruct((1, 252, 2, WIDTH), BF)] * 2
    outs = pl.pallas_call(
        outputs_kernel,
        in_specs=[vm] * len(parts),
        out_specs=[vm] * (len(shapes) + 2),
        out_shape=acts + [jax.ShapeDtypeStruct(shape, F32) for shape in shapes],
        compiler_params=pltpu.CompilerParams(vmem_limit_bytes=VMEM_LIMIT),
        name="outputs",
    )(*parts)
    outs = [x.transpose(0, 2, 1, 3) for x in outs[:2]] + list(outs[2:])
    outs[6] = outs[6].transpose(0, 1, 3, 2)
    for k in (9, 10, 11):
        outs[k] = outs[k].transpose(0, 2, 1)
    outs[12] = outs[12].transpose(1, 0, 2)
    return tuple(outs)


def swap(array):
    return lax.ppermute(array, "section", [(0, 1), (1, 0)])


def whole_rows(g):
    return g.transpose(1, 0, 2, 3).reshape(512, g.shape[-1])


def scatter_plain(g, gl, e):
    def sums(array, axis):
        return lax.psum_scatter(array.astype(F32)[None], "dp", scatter_dimension=axis, tiled=True)

    layers = [whole_rows(g[d]) for d in range(g.shape[0])]
    qkv = jnp.stack([rows[:, :1536] for rows in layers])
    out = jnp.stack([rows[:, 1536:2048] for rows in layers])
    up = jnp.stack([rows[:, 2048:4096] for rows in layers])
    down = jnp.stack(
        [
            rows[:, 4096:].reshape(16, 32, 4, WIDTH).transpose(0, 2, 1, 3).reshape(2048, WIDTH)
            for rows in layers
        ]
    )
    norm = whole_rows(gl)[:, :8].reshape(512, 2, 4).transpose(1, 0, 2)
    enc = whole_rows(e)
    first = e.transpose(1, 0, 2, 3)[:, :, :8, 1600:1648].reshape(128, 48)
    layer_sums = [sums(x, 2) for x in (qkv, out, up, down, norm)]
    layer_sums = [swap(x) for x in layer_sums]
    norm = layer_sums.pop()
    return tuple(layer_sums) + (
        norm[..., 0:2],
        norm[..., 2],
        norm[..., 3],
        sums(first.T, 2),
        sums(enc[:, :512].T, 2),
        sums(enc[:, 512:1536].T, 2),
        sums(enc[:, 1536:1553].T, 2),
    )


def on_device(
    frames, action_ids, delta_ids, seq_len, enc_w1, enc_w2, codebook, action_table,
    ln_gain, ln_bias, w_qkv, w_out, w_up, w_down, cotangent,
):
    micro, steps = frames.shape[1], frames.shape[2]
    count = micro * steps
    gains, shifts = ln_gain.transpose(0, 2, 1), ln_bias.transpose(0, 2, 1)
    tok, ids, xl, blocks, z1, z2 = enc_forward(
        frames.reshape((count,) + frames.shape[3:]), enc_w1, enc_w2, codebook, action_table,
        action_ids[0], delta_ids[0].transpose(0, 2, 1),
    )
    if lax.axis_size("dp") == 2 * CHIPS:
        parts = train(
            tok, cotangent[0].transpose(1, 0, 2), seq_len, gains, shifts, w_qkv, w_out, w_up, w_down,
            xl, blocks, z1, z2, enc_w2, ids,
        )
        return spread_outputs(*parts)
    lnp = jnp.concatenate([gains, shifts], axis=1)
    act, eg, g, gl = run_layers(tok, cotangent[0], seq_len, lnp, w_qkv, w_out, w_up, w_down)
    embed_grad = eg.reshape(micro, 256, WIDTH)[None, :, : steps * TPS]
    e = enc_backward(eg, xl, blocks, z1, z2, enc_w2, ids)
    return (act[None], embed_grad) + scatter_plain(g, gl, e)


def solution(mesh):
    return jax.shard_map(
        on_device,
        mesh=mesh,
        in_specs=(
            P("section", "dp", None, None, None),
            P("section", "dp", None),
            P("section", "dp", None, None),
            P(None, "dp"),
            P(), P(), P(), P(), P(), P(), P(), P(), P(), P(),
            P("section", "dp", None, None),
        ),
        out_specs=(
            P("section", "dp", None, None),
            P("section", "dp", None, None),
            P("section", None, "dp", None),
            P("section", None, "dp", None),
            P("section", None, "dp", None),
            P("section", None, "dp", None),
            P("section", None, "dp", None),
            P("section", None, "dp"),
            P("section", None, "dp"),
            P("section", None, "dp"),
            P("section", None, "dp"),
            P("section", None, "dp"),
            P("section", None, "dp"),
        ),
        check_vma=False,
    )
```
